32 devices in a mesh: replica: 8 (over z, x), group: 4 (over y, core).
Axes of the slice: x: 2, y: 2, z: 4, core: 2. Of those that a mesh axis runs over, the one named last changes fastest.
Arguments:
- hidden_in: bfloat16 [16, 1024, 1024], P('replica', 'group'), may hold values from -6 to 6
- segments: int32 [16, 1024], P('replica', 'group'), may hold values from 0 to 63, as said below
- positions: int32 [16, 1024], P('replica', 'group'), may hold values from 0 to 2047, as said below
- out_grad: bfloat16 [16, 1024, 1024], P('replica', 'group'), may hold values from -6 to 6
- attn_gain: bfloat16 [1024], P('group'), may hold values from 0.099609375 to 1.8984375
- w_query: bfloat16 [1024, 1024], P('group'), may hold values from -0.1875 to 0.1875
- w_key: bfloat16 [1024, 512], P('group'), may hold values from -0.1875 to 0.1875
- w_value: bfloat16 [1024, 512], P('group'), may hold values from -0.1875 to 0.1875
- query_gain: bfloat16 [64], replicated, may hold values from 0.099609375 to 1.8984375
- key_gain: bfloat16 [64], replicated, may hold values from 0.099609375 to 1.8984375
- w_out: bfloat16 [1024, 1024], P('group'), may hold values from -0.75 to 0.75
- ffn_gain: bfloat16 [1024], P('group'), may hold values from 0.099609375 to 1.8984375
- w_gate: bfloat16 [1024, 4608], P('group'), may hold values from -0.1875 to 0.1875
- w_up: bfloat16 [1024, 4608], P('group'), may hold values from -0.1875 to 0.1875
- w_down: bfloat16 [4608, 1024], P('group'), may hold values from -0.09375 to 0.09375
Outputs:
- block_out: bfloat16 [16, 1024, 1024], P('replica', 'group')
- input_grad: float32 [16, 1024, 1024], P('replica', 'group')
- attn_gain_grad: float32 [1024], P('group')
- w_query_grad: float32 [1024, 1024], P('group')
- w_key_grad: float32 [1024, 512], P('group')
- w_value_grad: float32 [1024, 512], P('group')
- query_gain_grad: float32 [64], replicated
- key_gain_grad: float32 [64], replicated
- w_out_grad: float32 [1024, 1024], P('group')
- ffn_gain_grad: float32 [1024], P('group')
- w_gate_grad: float32 [1024, 4608], P('group')
- w_up_grad: float32 [1024, 4608], P('group')
- w_down_grad: float32 [4608, 1024], P('group')
The draws below stay inside these ranges and needn't reach their ends.
Inputs may be any that keep to these rules, and one draw needn't show every extreme that they name: `segments`: within a sequence the document numbers start at 0, never fall and grow by at most one from token to token, so that each document is a run of consecutive tokens; some sequence reaches the most. Within a document the positions rise by one from token to token; later documents of a sequence start at 0, the first one may continue a document of an earlier pack.
All inputs are finite; a program needn't handle non-finite values.
Results may differ from the reference program's by a relative error of at most 0.015.
Values may be sent and summed in bfloat16 or wider, within the bound.
No kernel may reach another device: no remote copies, remote signals or barrier semaphores. Data moves between devices by JAX's collectives and lax.ppermute only.
A program may use at most 256 MiB of HBM per device.

```python
import jax
import jax.numpy as jnp
from jax import lax

D = 1024
HQ = 16
KV = 8
HD = 64
FF = 4608
SEQ_GROUP = 2
LENGTH = 1024
SEQUENCES = 16


def packing(key):
    rate_key, start_key, pick_key = jax.random.split(key, 3)
    exponent = jax.random.randint(rate_key, (SEQUENCES, 1), 3, 11)
    spacing = 2 ** exponent
    raw_draws = jax.random.randint(start_key, (SEQUENCES, LENGTH), 0, 1 << 20)
    starts = raw_draws % spacing == 0
    group_count = SEQUENCES // SEQ_GROUP
    chosen = jax.random.randint(pick_key, (group_count,), 0, SEQ_GROUP)
    seq_index = jnp.arange(SEQUENCES)
    token_index = jnp.arange(LENGTH)
    forced_seq = (chosen[0] + 1) % SEQ_GROUP
    regular = token_index % 16 == 0
    starts = starts | (seq_index == forced_seq)[:, None] & regular[None, :]
    single = seq_index % SEQ_GROUP == jnp.repeat(chosen, SEQ_GROUP)
    first_col = token_index == 0
    starts = jnp.where(single[:, None], first_col[None, :], starts | first_col[None, :])
    segment_ids = jnp.minimum(jnp.cumsum(starts.astype(jnp.int32), 1) - 1, LENGTH // 16 - 1)
    previous = jnp.concatenate([jnp.full((SEQUENCES, 1), -1, jnp.int32), segment_ids[:, :-1]], 1)
    starts = segment_ids != previous
    return (starts, segment_ids.astype(jnp.int32))


def draw_segments(key, part):
    starts, segment_ids = packing(key)
    return segment_ids


def draw_positions(key, part):
    starts, segment_ids = packing(key)
    key = jax.random.fold_in(key, 2)
    offset_key, pick_key = jax.random.split(key)
    token_index = jnp.arange(LENGTH, dtype=jnp.int32)
    doc_start = lax.cummax(jnp.where(starts, token_index[None, :], 0), axis=1)
    within = token_index[None, :] - doc_start
    first_len = jnp.sum((segment_ids == 0).astype(jnp.int32), 1)
    top_place = 2 * LENGTH - first_len
    offsets = jax.random.randint(offset_key, (SEQUENCES,), 0, 1 << 20) % (top_place + 1)
    top_seq = jax.random.randint(pick_key, (), 0, SEQUENCES)
    seq_index = jnp.arange(SEQUENCES)
    offsets = jnp.where(seq_index == top_seq, top_place, offsets)
    offsets = jnp.where(seq_index == (top_seq + 1) % SEQUENCES, 0, offsets)
    return (within + jnp.where(segment_ids == 0, offsets[:, None], 0)).astype(jnp.int32)


def steps_of(own_key, shape, cuts, least, largest):
    def one(axis_at, blocks):
        heights = jax.random.uniform(jax.random.fold_in(jax.random.fold_in(own_key, 6), axis_at), (blocks,), jnp.float32, least / len(cuts), largest / len(cuts))
        return jnp.repeat(jnp.exp(heights), shape[axis_at] // blocks).reshape((-1,) + (1,) * (len(shape) - axis_at - 1))

    level = one(*cuts[0])
    for cut in cuts[1:]:
        level = level * one(*cut)
    return level


def bell_draw(stream_key, dims, scale, limit, shards=(), kind=jnp.bfloat16):
    entries = scale * jax.random.normal(stream_key, dims, jnp.float32)
    if shards:
        entries = entries * steps_of(stream_key, dims, shards, -0.22, 0.18)
    return jnp.clip(entries, -limit, limit).astype(kind)


def setup_inputs(seed: int = 0) -> dict:
    key_of = jax.random.split(jax.random.key(seed), 16)
    return {
        "hidden_in": bell_draw(key_of[0], (SEQUENCES, LENGTH, D), 1.0, 6.0, ((0, 8), (1, 4))),
        "segments": draw_segments(jax.random.fold_in(key_of[15], 71), 0),
        "positions": draw_positions(jax.random.fold_in(key_of[15], 71), 0),
        "out_grad": bell_draw(key_of[3], (SEQUENCES, LENGTH, D), 1.0, 6.0, ((0, 8), (1, 4))),
        "attn_gain": jnp.clip(1.0 + 0.18 * jax.random.normal(key_of[4], (D,), jnp.float32), 0.099609375, 1.8984375).astype(jnp.bfloat16),
        "w_query": bell_draw(key_of[5], (D, HQ * HD), D ** -0.5, 0.1875, ((0, 4),)),
        "w_key": bell_draw(key_of[6], (D, KV * HD), D ** -0.5, 0.1875, ((0, 4),)),
        "w_value": bell_draw(key_of[7], (D, KV * HD), D ** -0.5, 0.1875, ((0, 4),)),
        "query_gain": jnp.clip(1.0 + 0.18 * jax.random.normal(key_of[8], (HD,), jnp.float32), 0.099609375, 1.8984375).astype(jnp.bfloat16),
        "key_gain": jnp.clip(1.0 + 0.18 * jax.random.normal(key_of[9], (HD,), jnp.float32), 0.099609375, 1.8984375).astype(jnp.bfloat16),
        "w_out": bell_draw(key_of[10], (HQ * HD, D), (HQ * HD // 16) ** -0.5, 0.75, ((0, 4),)),
        "ffn_gain": jnp.clip(1.0 + 0.18 * jax.random.normal(key_of[11], (D,), jnp.float32), 0.099609375, 1.8984375).astype(jnp.bfloat16),
        "w_gate": bell_draw(key_of[12], (D, FF), D ** -0.5, 0.1875, ((0, 4),)),
        "w_up": bell_draw(key_of[13], (D, FF), D ** -0.5, 0.1875, ((0, 4),)),
        "w_down": bell_draw(key_of[14], (FF, D), FF ** -0.5, 0.09375, ((0, 4),)),
    }


EPS = 1e-05
THETA = 1000000.0
NEG = -1e+30
HIGH = lax.Precision.HIGHEST

@jax.custom_vjp
def low(v):
    return lax.optimization_barrier(v.astype(jnp.bfloat16)).astype(jnp.float32)

@jax.custom_vjp
def low_back(v):
    return v

def low_keep(v):
    return (low(v), None)

def low_pass(kept, grad):
    return (grad,)

def back_keep(v):
    return (v, None)

def back_low(kept, grad):
    return (low(grad),)
low.defvjp(low_keep, low_pass)
low_back.defvjp(back_keep, back_low)

def matmul(left, right):
    return jnp.dot(left, right, precision=HIGH)

def normalize(inputs):
    return inputs * lax.rsqrt(lax.optimization_barrier(jnp.mean(inputs * inputs, -1, keepdims=True)) + EPS)

def rope_tables(places, head_size):
    half_size = head_size // 2
    freq_table = THETA ** (-(jnp.arange(half_size, dtype=jnp.float32) * 2.0 / head_size))
    angle = places.astype(jnp.float32)[..., None] * freq_table
    return (jnp.cos(angle), jnp.sin(angle))

def rotate(heads, cosine, sine_table):
    half_size = heads.shape[-1] // 2
    first_half = heads[..., :half_size]
    second_half = heads[..., half_size:]
    cos_col = cosine[..., None, :]
    sin_col = sine_table[..., None, :]
    return jnp.concatenate([first_half * cos_col - second_half * sin_col, second_half * cos_col + first_half * sin_col], -1)

def layer(params, inputs, seg_ids, places):
    attn_gain, w_query, w_key, w_value, query_gain, key_gain, w_out, ffn_gain, w_gate, w_up, w_down = params
    length = inputs.shape[0]
    hidden_one = low(normalize(inputs) * attn_gain)
    query_raw = low_back(matmul(hidden_one, w_query))
    key_raw = low_back(matmul(hidden_one, w_key))
    value_low = low(low_back(matmul(hidden_one, w_value)))
    cosine, sine_table = rope_tables(places, HD)
    query_rot = low(rotate(normalize(query_raw.reshape(length, HQ, HD)) * query_gain, cosine, sine_table))
    key_rot = low(rotate(normalize(key_raw.reshape(length, KV, HD)) * key_gain, cosine, sine_table))
    grouped = query_rot.reshape(length, KV, HQ // KV, HD)
    value_heads = value_low.reshape(length, KV, HD)
    scores = low_back(jnp.einsum('tkgd,jkd->kgtj', grouped, key_rot, precision=HIGH) * HD ** (-0.5))
    token_index = jnp.arange(length)
    visible = (seg_ids[:, None] == seg_ids[None, :]) & (token_index[None, :] <= token_index[:, None])
    masked = jnp.where(visible, scores, NEG)
    row_max = lax.optimization_barrier(jnp.max(masked, -1, keepdims=True))
    weights = jnp.exp(masked - row_max)
    prob_low = low(weights / lax.optimization_barrier(jnp.sum(weights, -1, keepdims=True)))
    mixed_heads = jnp.einsum('kgtj,jkd->tkgd', prob_low, value_heads, precision=HIGH).reshape(length, HQ * HD)
    mixed_low = low(low_back(mixed_heads))
    middle = inputs + low_back(matmul(mixed_low, w_out))
    hidden_two = low(normalize(middle) * ffn_gain)
    gate_raw = low_back(matmul(hidden_two, w_gate))
    upward = low_back(matmul(hidden_two, w_up))
    activated = low(jax.nn.silu(gate_raw) * upward)
    return middle + low_back(matmul(activated, w_down))

def add_up(total, extra):
    return total + extra

def reference(hidden_in, segments, positions, out_grad, attn_gain, w_query, w_key, w_value, query_gain, key_gain, w_out, ffn_gain, w_gate, w_up, w_down):
    params = tuple((item.astype(jnp.float32) for item in (attn_gain, w_query, w_key, w_value, query_gain, key_gain, w_out, ffn_gain, w_gate, w_up, w_down)))
    start_sums = jax.tree.map(jnp.zeros_like, params)

    def add_sequence(running, sequence):
        inputs, seg_ids, places, cotangent = sequence

        def forward(weights, acts):
            return layer(weights, acts, seg_ids, places)
        result, pullback = jax.vjp(forward, params, inputs)
        grad_params, grad_inputs = pullback(cotangent)
        running = jax.tree.map(add_up, running, grad_params)
        return (running, (result.astype(jnp.bfloat16), grad_inputs))
    totals, outputs = lax.scan(add_sequence, start_sums, (hidden_in.astype(jnp.float32), segments, positions, out_grad.astype(jnp.float32)))
    block_out, input_grad = outputs
    return (block_out, input_grad, totals[0], totals[1], totals[2], totals[3], totals[4], totals[5], totals[6], totals[7], totals[8], totals[9], totals[10])
```

```python
import functools

import jax
import jax.numpy as jnp
from jax import lax
from jax.experimental import pallas as pl
from jax.experimental.pallas import tpu as pltpu
from jax.sharding import PartitionSpec as P

HEADS = 8
PAIRS = 4
HD = 64
HALF = 32
SPAN = 256

EPS = 1e-05
THETA = 1000000.0
NEG = -1e30

BF = jnp.bfloat16
F32 = jnp.float32

Y_SWAP = [(0, 2), (2, 0), (1, 3), (3, 1)]
CORE_SWAP = [(0, 1), (1, 0), (2, 3), (3, 2)]


def contract(left, right, left_dim, right_dim):
    return lax.dot_general(
        left, right, (((left_dim,), (right_dim,)), ((), ())), preferred_element_type=F32
    )


def visible_block(seg_col, seg_row, block):
    end = (block + 1) * SPAN
    key_at = lax.broadcasted_iota(jnp.int32, (end, SPAN), 0)
    query_at = lax.broadcasted_iota(jnp.int32, (end, SPAN), 1) + block * SPAN
    return (seg_col[0:end, :] == seg_row[:, block * SPAN : end]) & (key_at <= query_at)


def forward_kernel(
    hidden_ref,
    weight_ref,
    cos_ref,
    sin_ref,
    seg_row_ref,
    seg_col_ref,
    gain_ref,
    mixed_ref,
    rot_ref,
    key_ref,
    value_ref,
    value_t_ref,
    normed_ref,
    inv_ref,
    log_ref,
):
    blocks = hidden_ref.shape[0] // SPAN
    heads = HEADS + PAIRS
    for block in range(blocks):
        span = slice(block * SPAN, (block + 1) * SPAN)
        raw = jnp.dot(hidden_ref[span, :], weight_ref[...], preferred_element_type=F32)
        value_ref[span, :] = raw[:, heads * HD :].astype(BF)
        raw_t = raw.T
        value_t_ref[:, span] = raw_t[heads * HD :, :].astype(BF)
        cosine = cos_ref[:, span]
        sine = sin_ref[:, span]
        for head in range(heads):
            rows = slice(head * HD, (head + 1) * HD)
            part = raw_t[rows, :]
            inv = lax.rsqrt(jnp.mean(part * part, 0, keepdims=True) + EPS)
            normed = part * inv
            normed_ref[rows, span] = normed
            inv_ref[head : head + 1, span] = inv
            kind = 0 if head < HEADS else 1
            scaled = normed * gain_ref[:, kind : kind + 1]
            first = scaled[:HALF, :]
            second = scaled[HALF:, :]
            turned = jnp.concatenate(
                [first * cosine - second * sine, second * cosine + first * sine], 0
            )
            if head < HEADS:
                rot_ref[rows, span] = turned.astype(BF) * BF(HD**-0.5)
            else:
                rot_ref[rows, span] = turned.astype(BF)
    for pair in range(PAIRS):
        rows = slice((HEADS + pair) * HD, (HEADS + pair + 1) * HD)
        key_ref[pair] = rot_ref[rows, :].astype(F32).T.astype(BF)
    for block in range(blocks):
        end = (block + 1) * SPAN
        span = slice(block * SPAN, end)
        visible = visible_block(seg_col_ref[...], seg_row_ref[...], block)

        def one_pair(pair, carry, end=end, span=span, visible=visible):
            keys = key_ref[pair, 0:end, :]
            values_t = value_t_ref[pl.ds(pl.multiple_of(pair * HD, HD), HD), 0:end]
            outs = []
            for side in range(2):
                head = pair * 2 + side
                rows = pl.ds(pl.multiple_of(head * HD, HD), HD)
                score = jnp.dot(keys, rot_ref[rows, span], preferred_element_type=F32)
                score = jnp.where(visible, score, NEG)
                top = jnp.max(score, 0, keepdims=True)
                weight = jnp.exp(score - top)
                total = jnp.sum(weight, 0, keepdims=True)
                log_ref[pl.ds(head, 1), span] = top + jnp.log(total)
                prob = (weight * (1.0 / total)).astype(BF)
                outs.append(jnp.dot(values_t, prob, preferred_element_type=F32))
            both = jnp.concatenate(outs, 0).T
            cols = pl.ds(pl.multiple_of(pair * 2 * HD, 2 * HD), 2 * HD)
            mixed_ref[span, cols] = both.astype(BF)
            return carry

        lax.fori_loop(0, PAIRS, one_pair, 0)


def backward_kernel(
    grad_ref,
    rot_ref,
    key_ref,
    value_ref,
    normed_ref,
    inv_ref,
    log_ref,
    cos_ref,
    sin_ref,
    seg_row_ref,
    seg_col_ref,
    gain_ref,
    out_ref,
    gain_grad_ref,
    grad_t,
    query_grad,
    value_one,
    key_sum,
    value_sum,
    out_t,
):
    length = grad_ref.shape[0]
    blocks = length // SPAN
    heads = HEADS + PAIRS
    for part in range(HEADS // 2):
        cols = slice(part * 2 * HD, (part + 1) * 2 * HD)
        grad_t[cols, :] = grad_ref[:, cols].astype(F32).T.astype(BF)
    values_t = value_ref[...].astype(F32).T
    for pair in range(PAIRS):
        value_one[pair] = values_t[pair * HD : (pair + 1) * HD, :].T.astype(BF)
    left_lane = lax.broadcasted_iota(jnp.int32, (SPAN, 2 * HD), 1) < HD
    zero = jnp.zeros((SPAN, 2 * HD), BF)

    def one_pair(pair, carry):
        key_sum[...] = jnp.zeros_like(key_sum)
        value_sum[...] = jnp.zeros_like(value_sum)
        keys_t = rot_ref[pl.ds(pl.multiple_of((HEADS + pair) * HD, HD), HD), :]
        both = pl.ds(pl.multiple_of(pair * 2 * HD, 2 * HD), 2 * HD)
        for block in range(blocks):
            end = (block + 1) * SPAN
            span = slice(block * SPAN, end)
            visible = visible_block(seg_col_ref[...], seg_row_ref[...], block)
            queries = rot_ref[both, span].astype(F32).T.astype(BF)
            grads = grad_ref[span, both]
            for side in range(2):
                head = pair * 2 + side
                rows = pl.ds(pl.multiple_of(head * HD, HD), HD)
                score = jnp.dot(
                    key_ref[pair, 0:end, :], rot_ref[rows, span], preferred_element_type=F32
                )
                prob = jnp.where(visible, jnp.exp(score - log_ref[pl.ds(head, 1), span]), 0.0)
                grad_prob = jnp.dot(
                    value_one[pair, 0:end, :], grad_t[rows, span], preferred_element_type=F32
                )
                inner = jnp.sum(prob * grad_prob, 0, keepdims=True)
                grad_score = (prob * (grad_prob - inner)).astype(BF)
                mine = left_lane if side == 0 else jnp.logical_not(left_lane)
                value_sum[0:end, :] += jnp.dot(
                    prob.astype(BF), jnp.where(mine, grads, zero), preferred_element_type=F32
                )
                key_sum[0:end, :] += jnp.dot(
                    grad_score, jnp.where(mine, queries, zero), preferred_element_type=F32
                )
                query_grad[rows, span] = jnp.dot(
                    keys_t[:, 0:end], grad_score, preferred_element_type=F32
                ) * (HD**-0.5)
        key_t = key_sum[...].T
        value_t = value_sum[...].T
        key_rows = pl.ds(pl.multiple_of((HEADS + pair) * HD, HD), HD)
        query_grad[key_rows, :] = key_t[:HD, :] + key_t[HD:, :]
        value_rows = pl.ds(pl.multiple_of((heads + pair) * HD, HD), HD)
        out_t[value_rows, :] = value_t[:HD, :] + value_t[HD:, :]
        return carry

    lax.fori_loop(0, PAIRS, one_pair, 0)

    cosine = cos_ref[...]
    sine = sin_ref[...]
    gain_sums = [jnp.zeros((HD, length), F32), jnp.zeros((HD, length), F32)]
    for head in range(heads):
        rows = slice(head * HD, (head + 1) * HD)
        kind = 0 if head < HEADS else 1
        part = query_grad[rows, :]
        first = part[:HALF, :]
        second = part[HALF:, :]
        turned = jnp.concatenate(
            [first * cosine + second * sine, second * cosine - first * sine], 0
        )
        normed = normed_ref[rows, :]
        gain_sums[kind] = gain_sums[kind] + turned * normed
        scaled = turned * gain_ref[:, kind : kind + 1]
        mean = jnp.mean(scaled * normed, 0, keepdims=True)
        out_t[rows, :] = inv_ref[head : head + 1, :] * (scaled - normed * mean)
    for kind in range(2):
        gain_grad_ref[:, kind : kind + 1] = jnp.sum(gain_sums[kind], 1, keepdims=True)
    width = out_t.shape[0]
    for part in range(width // (2 * HD)):
        cols = slice(part * 2 * HD, (part + 1) * 2 * HD)
        out_ref[:, cols] = out_t[cols, :].T.astype(BF)


def whole_refs(count):
    return [pl.BlockSpec(memory_space=pltpu.VMEM)] * count


def attention_forward(hidden, weight, cosine, sine, seg_row, seg_col, gains):
    length = hidden.shape[0]
    rows = (HEADS + PAIRS) * HD
    outs = [
        ((length, HEADS * HD), BF),
        ((rows, length), BF),
        ((PAIRS, length, HD), BF),
        ((length, PAIRS * HD), BF),
        ((PAIRS * HD, length), BF),
        ((rows, length), F32),
        ((16, length), F32),
        ((HEADS, length), F32),
    ]
    return pl.pallas_call(
        forward_kernel,
        out_shape=[jax.ShapeDtypeStruct(shape, kind) for shape, kind in outs],
        in_specs=whole_refs(7),
        out_specs=whole_refs(len(outs)),
        compiler_params=pltpu.CompilerParams(vmem_limit_bytes=48 * 1024 * 1024),
        cost_estimate=pl.CostEstimate(
            flops=12 * 10**9, bytes_accessed=16 * 2**20, transcendentals=6 * 10**6
        ),
        name="attention_forward",
    )(hidden, weight, cosine, sine, seg_row, seg_col, gains)


def attention_backward(grad, rot, key, value, normed, inv, log, cosine, sine, seg_row, seg_col, gains):
    length = grad.shape[0]
    rows = (HEADS + PAIRS) * HD
    width = rows + PAIRS * HD
    return pl.pallas_call(
        backward_kernel,
        out_shape=[
            jax.ShapeDtypeStruct((length, width), BF),
            jax.ShapeDtypeStruct((HD, 2), F32),
        ],
        in_specs=whole_refs(12),
        out_specs=whole_refs(2),
        scratch_shapes=[
            pltpu.VMEM((HEADS * HD, length), BF),
            pltpu.VMEM((rows, length), F32),
            pltpu.VMEM((PAIRS, length, HD), BF),
            pltpu.VMEM((length, 2 * HD), F32),
            pltpu.VMEM((length, 2 * HD), F32),
            pltpu.VMEM((width, length), F32),
        ],
        compiler_params=pltpu.CompilerParams(vmem_limit_bytes=56 * 1024 * 1024),
        cost_estimate=pl.CostEstimate(
            flops=25 * 10**9, bytes_accessed=16 * 2**20, transcendentals=6 * 10**6
        ),
        name="attention_backward",
    )(grad, rot, key, value, normed, inv, log, cosine, sine, seg_row, seg_col, gains)


def norm_rows(inputs):
    inv = lax.rsqrt(jnp.mean(inputs * inputs, -1, keepdims=True) + EPS)
    return (inputs * inv, inv)


def norm_back(grad, normed, inv):
    return inv * (grad - normed * jnp.mean(grad * normed, -1, keepdims=True))


def swap_y(value):
    return lax.ppermute(value, "group", Y_SWAP)


def swap_core(value):
    return lax.ppermute(value, "group", CORE_SWAP)


def cycle_of(count):
    return list(range(0, count, 2)) + list(range(count - 1, 0, -2))


class Ring:
    def __init__(self, way):
        count = lax.axis_size("replica")
        cycle = cycle_of(count)
        if way < 0:
            cycle = cycle[::-1]
        places = [cycle.index(member) for member in range(count)]
        self.count = count
        self.cycle = jnp.array(cycle, jnp.int32)
        self.place = jnp.array(places, jnp.int32)[lax.axis_index("replica")]
        self.hops = [(cycle[at], cycle[(at + 1) % count]) for at in range(count)]

    def chunk_at(self, back):
        return self.cycle[lax.rem(self.place - back + 2 * self.count, self.count)]

    def send(self, value):
        return lax.ppermute(value, "replica", self.hops)

    def reduce(self, pick):
        moving = pick(self.chunk_at(1)).astype(BF)
        for step in range(self.count - 1):
            arrived = self.send(moving)
            moving = (pick(self.chunk_at(step + 2)) + arrived.astype(F32)).astype(BF)
        return moving

    def gather(self, chunk, place):
        moving = chunk
        place(self.chunk_at(0), moving)
        for step in range(self.count - 1):
            moving = self.send(moving)
            place(self.chunk_at(step + 1), moving)


def pick_rows(whole, dim):
    def pick(index):
        return lax.dynamic_index_in_dim(whole, index, dim, keepdims=False).astype(F32)

    return pick


def gather_rows(ring, chunk, count):
    rows, columns = chunk.shape
    store = [jnp.zeros((count * rows, columns), F32)]

    def place(index, value):
        store[0] = lax.dynamic_update_slice(store[0], value.astype(F32), (index * rows, 0))

    ring.gather(chunk, place)
    return store[0]


def per_device(
    hidden_in,
    segments,
    positions,
    out_grad,
    attn_gain,
    w_query,
    w_key,
    w_value,
    query_gain,
    key_gain,
    w_out,
    ffn_gain,
    w_gate,
    w_up,
    w_down,
):
    copies = lax.axis_size("replica")
    member = lax.axis_index("group")
    y_at = member // 2
    core = lax.rem(member, 2)
    on_low_y = y_at == 0
    on_low_core = core == 0
    span, width = hidden_in.shape[1:]
    hidden_units = w_down.shape[0]

    def by_y(mine, other):
        return jnp.where(on_low_y, mine, other), jnp.where(on_low_y, other, mine)

    def by_core(mine, other):
        return jnp.where(on_low_core, mine, other), jnp.where(on_low_core, other, mine)

    def at_y(pair_low, pair_high):
        return jnp.where(on_low_y, pair_low, pair_high), jnp.where(on_low_y, pair_high, pair_low)

    def at_core(low, high):
        return jnp.where(on_low_core, low, high), jnp.where(on_low_core, high, low)

    small = jnp.concatenate(
        [
            attn_gain.astype(F32)[None],
            ffn_gain.astype(F32)[None],
            segments.astype(F32),
            positions.astype(F32),
        ],
        0,
    )
    small_low, small_high = by_y(small, swap_y(small))
    small_two = jnp.stack([small_low, small_high])
    small_even, small_odd = by_core(small_two, swap_core(small_two))
    small_all = jnp.stack([small_even, small_odd], 1).reshape(4, 6, span)
    small_rows = small_all.transpose(1, 0, 2).reshape(6, 4 * span)
    gain_one = small_rows[0]
    gain_two = small_rows[1]
    seg = jnp.where(on_low_y, small_rows[2], small_rows[3])
    place = jnp.where(on_low_y, small_rows[4], small_rows[5])

    seq_mine, seq_other = at_y(hidden_in[0], hidden_in[1])
    own_low, own_high = by_y(seq_mine, swap_y(seq_other))
    own_in = jnp.stack([own_low, own_high])
    all_even, all_odd = by_core(own_in, swap_core(own_in))
    all_in = jnp.stack([all_even, all_odd], 1).reshape(4 * span, width)

    def head_columns(weight):
        rows = weight.shape[0]
        parts = weight.reshape(rows, 2, 2, -1)
        mine, other = at_core(parts[:, :, 0], parts[:, :, 1])
        return mine.reshape(rows, -1), other.reshape(rows, -1)

    columns = [head_columns(weight) for weight in (w_query, w_key, w_value)]
    mine_cols = jnp.concatenate([mine for mine, other in columns], 1)
    other_cols = jnp.concatenate([other for mine, other in columns], 1)
    two_rows = jnp.concatenate(by_core(mine_cols, swap_core(other_cols)), 0)
    w_attn = jnp.concatenate(by_y(two_rows, swap_y(two_rows)), 0)
    w_mix = jnp.concatenate(by_y(w_out, swap_y(w_out)), 0)

    def unit_columns(weight):
        rows = weight.shape[0]
        parts = weight.reshape(rows, 2, 2, -1)
        return at_core(parts[:, :, 0], parts[:, :, 1])

    gate_mine, gate_other = unit_columns(w_gate)
    up_mine, up_other = unit_columns(w_up)
    ffn_mine = jnp.concatenate([gate_mine, up_mine], -1)
    ffn_other = jnp.concatenate([gate_other, up_other], -1)
    ffn_rows = jnp.concatenate(by_core(ffn_mine, swap_core(ffn_other)), 0)
    ffn_here, ffn_there = at_y(ffn_rows[:, 0], ffn_rows[:, 1])
    w_ffn = jnp.concatenate(by_y(ffn_here, swap_y(ffn_there)), 0)

    dy_mine, dy_other = at_y(out_grad[0], out_grad[1])
    dy_y = swap_y(out_grad)
    dy_y_mine, dy_y_other = at_y(dy_y[0], dy_y[1])
    dy_own = jnp.concatenate(by_y(dy_mine, dy_y_mine), 0)
    dy_next = jnp.concatenate(by_y(dy_other, dy_y_other), 0)
    dy_sib = swap_core(dy_own)
    dy_diag = swap_core(dy_next)
    dy_near = jnp.concatenate([dy_own, dy_sib], 0)
    dy_far = jnp.concatenate([dy_next, dy_diag], 0)

    normed_all, _ = norm_rows(all_in.astype(F32))
    hidden_one = (normed_all * gain_one).astype(BF)
    freq = THETA ** (-(jnp.arange(HALF, dtype=F32) * 2.0 / HD))
    angle = freq[:, None] * place[None, :]
    cosine, sine = jnp.cos(angle), jnp.sin(angle)
    gains = jnp.stack([query_gain, key_gain], 1).astype(F32)
    seg_row = seg[None, :]
    seg_col = seg[:, None]
    mixed, rot, key_rot, value_low, _, head_normed, head_inv, log_total = attention_forward(
        hidden_one, w_attn, cosine, sine, seg_row, seg_col, gains
    )

    def own_and_other(rows):
        parts = rows.reshape(2, 2, span, rows.shape[-1])
        mine, other = at_core(parts[:, 0], parts[:, 1])
        return mine.reshape(2 * span, -1), other.reshape(2 * span, -1)

    mix_part = jnp.dot(mixed, w_mix, preferred_element_type=F32)
    mix_mine, mix_other = own_and_other(mix_part)
    inputs = own_in.reshape(2 * span, width).astype(F32)
    middle = inputs + mix_mine + swap_core(mix_other.astype(BF)).astype(F32)
    normed_two, inv_two = norm_rows(middle)
    hidden_two = (normed_two * gain_two).astype(BF)

    h2_next = swap_y(hidden_two)
    h2_sib = swap_core(hidden_two)
    h2_diag = swap_core(h2_next)
    h2_near = jnp.concatenate([hidden_two, h2_sib], 0)
    h2_far = jnp.concatenate([h2_next, h2_diag], 0)
    units = hidden_units

    def ffn(h2, dy):
        both = contract(h2, w_ffn, 1, 0)
        gate, up = both[:, :units], both[:, units:]
        sig = jax.nn.sigmoid(gate)
        act = (gate * sig * up).astype(BF)
        grad_act = contract(dy, w_down, 1, 1)
        grad_gate = (grad_act * up * sig * (1.0 + gate * (1.0 - sig))).astype(BF)
        grad_up = (grad_act * gate * sig).astype(BF)
        return act, jnp.concatenate([grad_gate, grad_up], 1)

    act_near, grad_near = ffn(h2_near, dy_near)
    act_far, grad_far = ffn(h2_far, dy_far)
    down_grad = (contract(act_near, dy_near, 0, 0) + contract(act_far, dy_far, 0, 0)).astype(BF)
    back_far = contract(grad_far, w_ffn, 1, 1)
    back_near = contract(grad_near, w_ffn, 1, 1)
    rows_own = 2 * span
    dh2_far = back_far[:rows_own] + swap_core(back_far[rows_own:].astype(BF)).astype(F32)
    dh2_near = back_near[:rows_own] + swap_core(back_near[rows_own:].astype(BF)).astype(F32)
    grad_hidden_two = dh2_near + swap_y(dh2_far.astype(BF)).astype(F32)
    ffn_grad = (contract(h2_near, grad_near, 0, 0) + contract(h2_far, grad_far, 0, 0)).astype(BF)

    out_near = contract(act_near, w_down, 1, 0)
    out_far = contract(act_far, w_down, 1, 0)
    out_own = middle + out_near[:rows_own] + swap_core(out_near[rows_own:].astype(BF)).astype(F32)
    out_next = out_far[:rows_own] + swap_core(out_far[rows_own:].astype(BF)).astype(F32)

    def chunk_pair(rows):
        parts = rows.reshape(2, span, width)
        return at_y(parts[0], parts[1])

    own_here, own_there = chunk_pair(out_own)
    next_here, next_there = chunk_pair(out_next)
    out_back = swap_y(jnp.stack([own_there, next_there]).astype(BF)).astype(F32)
    block_out = jnp.stack(by_y(own_here + out_back[1], next_here + out_back[0])).astype(BF)

    ffn_gain_part = jnp.sum(grad_hidden_two * normed_two, 0)
    grad_middle = dy_own.astype(F32) + norm_back(grad_hidden_two * gain_two, normed_two, inv_two)
    grad_branch = grad_middle.astype(BF).reshape(2, span, width)
    branch_even, branch_odd = by_core(grad_branch, swap_core(grad_branch))
    branch_all = jnp.stack([branch_even, branch_odd], 1).reshape(4 * span, width)
    grad_mixed = contract(branch_all, w_mix, 1, 1).astype(BF)
    mix_grad = contract(mixed, branch_all, 0, 0)
    grad_heads, head_gain_part = attention_backward(
        grad_mixed,
        rot,
        key_rot,
        value_low,
        head_normed,
        head_inv,
        log_total,
        cosine,
        sine,
        seg_row,
        seg_col,
        gains,
    )
    back_one = contract(grad_heads, w_attn, 1, 1)
    one_mine, one_other = own_and_other(back_one)
    grad_hidden_one = one_mine + swap_core(one_other.astype(BF)).astype(F32)
    normed_one, inv_one = norm_rows(inputs)
    attn_gain_part = jnp.sum(grad_hidden_one * normed_one, 0)
    grad_input = grad_middle + norm_back(grad_hidden_one * gain_one, normed_one, inv_one)
    input_here, input_there = chunk_pair(grad_input)
    input_back = swap_y(input_there.astype(BF)).astype(F32)
    input_grad = jnp.stack(by_y(input_here, input_back))

    attn_grad = contract(hidden_one, grad_heads, 0, 0).reshape(2, 2 * span, -1)
    rows_here, rows_there = at_y(attn_grad[0], attn_grad[1])
    attn_grad_y = rows_here + swap_y(rows_there.astype(BF)).astype(F32)
    mix_here, mix_there = at_y(mix_grad[:span], mix_grad[span:])
    mix_grad_y = mix_here + swap_y(mix_there.astype(BF)).astype(F32)

    sums = jnp.concatenate([attn_gain_part, ffn_gain_part, head_gain_part.T.reshape(-1)])
    sums = sums.reshape(-1, 128)
    sums = sums + swap_core(sums)
    sums = sums + swap_y(sums)
    step = 1
    while step < copies:
        sums = sums + lax.ppermute(sums, "replica", [(at, at ^ step) for at in range(copies)])
        step *= 2
    sums = sums.reshape(-1)
    attn_gain_grad = lax.dynamic_slice(sums, (member * span,), (span,))
    ffn_gain_grad = lax.dynamic_slice(sums, (width + member * span,), (span,))
    query_gain_grad = sums[2 * width : 2 * width + HD]
    key_gain_grad = sums[2 * width + HD : 2 * width + 2 * HD]

    right, left = Ring(1), Ring(-1)
    half = width // 2
    down_rows = hidden_units // copies
    down_view = down_grad.reshape(copies, down_rows, width)
    down_right = right.reduce(pick_rows(down_view[:, :, :half], 0))
    down_left = left.reduce(pick_rows(down_view[:, :, half:], 0))
    w_down_grad = jnp.concatenate(
        [gather_rows(right, down_right, copies), gather_rows(left, down_left, copies)], 1
    )

    rows = span // copies
    ffn_view = ffn_grad.reshape(4, copies, rows, 2 * units)
    gate_part = right.reduce(pick_rows(ffn_view[..., :units], 1))
    up_part = left.reduce(pick_rows(ffn_view[..., units:], 1))

    def own_rows(part):
        parts = part.reshape(2, 2, rows, units)
        mine, other = at_core(parts[:, 0], parts[:, 1])
        both_cores = jnp.stack(by_core(mine, swap_core(other)), 1)
        here, there = at_y(both_cores[0], both_cores[1])
        all_units = jnp.stack(by_y(here, swap_y(there)))
        return all_units.transpose(2, 0, 1, 3).reshape(rows, 4 * units)

    w_gate_grad = gather_rows(right, own_rows(gate_part), copies)
    w_up_grad = gather_rows(left, own_rows(up_part), copies)

    query_width = 2 * span
    attn_view = attn_grad_y.reshape(2, copies, rows, -1)
    query_part = right.reduce(pick_rows(attn_view[..., :query_width], 1))
    rest_part = left.reduce(pick_rows(attn_view[..., query_width:], 1))
    mix_view = mix_grad_y.reshape(copies, rows, width)
    mix_right = right.reduce(pick_rows(mix_view[..., :half], 0))
    mix_left = left.reduce(pick_rows(mix_view[..., half:], 0))

    def all_heads(part, kinds):
        mine, other = at_core(part[0], part[1])
        even, odd = by_core(mine, swap_core(other))
        shape = (rows, kinds, 2, 1, part.shape[-1] // (2 * kinds))
        return jnp.concatenate([even.reshape(shape), odd.reshape(shape)], 3).reshape(rows, -1)

    query_all = gather_rows(right, all_heads(query_part, 1), copies)
    rest_all = gather_rows(left, all_heads(rest_part, 2), copies)
    w_out_grad = jnp.concatenate(
        [gather_rows(right, mix_right, copies), gather_rows(left, mix_left, copies)], 1
    )
    w_query_grad = query_all
    w_key_grad = rest_all[:, : 2 * span]
    w_value_grad = rest_all[:, 2 * span :]

    return (
        block_out,
        input_grad,
        attn_gain_grad,
        w_query_grad,
        w_key_grad,
        w_value_grad,
        query_gain_grad,
        key_gain_grad,
        w_out_grad,
        ffn_gain_grad,
        w_gate_grad,
        w_up_grad,
        w_down_grad,
    )


def solution(mesh):
    rows = P("group", None)
    tokens = P("replica", "group", None)
    placed = (
        tokens,
        P("replica", "group"),
        P("replica", "group"),
        tokens,
        P("group"),
        rows,
        rows,
        rows,
        P(),
        P(),
        rows,
        P("group"),
        rows,
        rows,
        rows,
    )
    return jax.shard_map(
        per_device,
        mesh=mesh,
        in_specs=placed,
        out_specs=(
            tokens,
            tokens,
            P("group"),
            rows,
            rows,
            rows,
            P(),
            P(),
            rows,
            P("group"),
            rows,
            rows,
            rows,
        ),
        check_vma=False,
    )
```

```python
import functools

import jax
import jax.numpy as jnp
from jax import lax
from jax.experimental import pallas as pl
from jax.experimental.pallas import tpu as pltpu
from jax.sharding import PartitionSpec as P

HEADS = 8
PAIRS = 4
HD = 64
HALF = 32
SPAN = 256

EPS = 1e-05
THETA = 1000000.0
NEG = -1e30

BF = jnp.bfloat16
F32 = jnp.float32

Y_SWAP = [(0, 2), (2, 0), (1, 3), (3, 1)]
CORE_SWAP = [(0, 1), (1, 0), (2, 3), (3, 2)]
CROSS_SWAP = [(0, 3), (3, 0), (1, 2), (2, 1)]


def contract(left, right, left_dim, right_dim):
    return lax.dot_general(
        left, right, (((left_dim,), (right_dim,)), ((), ())), preferred_element_type=F32
    )


def visible_block(seg_col, seg_row, block):
    end = (block + 1) * SPAN
    key_at = lax.broadcasted_iota(jnp.int32, (end, SPAN), 0)
    query_at = lax.broadcasted_iota(jnp.int32, (end, SPAN), 1) + block * SPAN
    return (seg_col[0:end, :] == seg_row[:, block * SPAN : end]) & (key_at <= query_at)


def forward_kernel(
    hidden_ref,
    weight_ref,
    cos_ref,
    sin_ref,
    seg_row_ref,
    seg_col_ref,
    gain_ref,
    mixed_ref,
    rot_ref,
    key_ref,
    value_ref,
    value_t_ref,
    normed_ref,
    inv_ref,
    log_ref,
):
    blocks = hidden_ref.shape[0] // SPAN
    heads = HEADS + PAIRS
    for block in range(blocks):
        span = slice(block * SPAN, (block + 1) * SPAN)
        raw = jnp.dot(hidden_ref[span, :], weight_ref[...], preferred_element_type=F32)
        value_ref[span, :] = raw[:, heads * HD :].astype(BF)
        raw_t = raw.T
        value_t_ref[:, span] = raw_t[heads * HD :, :].astype(BF)
        cosine = cos_ref[:, span]
        sine = sin_ref[:, span]
        for head in range(heads):
            rows = slice(head * HD, (head + 1) * HD)
            part = raw_t[rows, :]
            inv = lax.rsqrt(jnp.mean(part * part, 0, keepdims=True) + EPS)
            normed = part * inv
            normed_ref[rows, span] = normed
            inv_ref[head : head + 1, span] = inv
            kind = 0 if head < HEADS else 1
            scaled = normed * gain_ref[:, kind : kind + 1]
            first = scaled[:HALF, :]
            second = scaled[HALF:, :]
            turned = jnp.concatenate(
                [first * cosine - second * sine, second * cosine + first * sine], 0
            )
            if head < HEADS:
                rot_ref[rows, span] = turned.astype(BF) * BF(HD**-0.5)
            else:
                rot_ref[rows, span] = turned.astype(BF)
    for pair in range(PAIRS):
        rows = slice((HEADS + pair) * HD, (HEADS + pair + 1) * HD)
        key_ref[pair] = rot_ref[rows, :].astype(F32).T.astype(BF)
    for block in range(blocks):
        end = (block + 1) * SPAN
        span = slice(block * SPAN, end)
        visible = visible_block(seg_col_ref[...], seg_row_ref[...], block)

        def one_pair(pair, carry, end=end, span=span, visible=visible):
            keys = key_ref[pair, 0:end, :]
            values_t = value_t_ref[pl.ds(pl.multiple_of(pair * HD, HD), HD), 0:end]
            outs = []
            for side in range(2):
                head = pair * 2 + side
                rows = pl.ds(pl.multiple_of(head * HD, HD), HD)
                score = jnp.dot(keys, rot_ref[rows, span], preferred_element_type=F32)
                score = jnp.where(visible, score, NEG)
                top = jnp.max(score, 0, keepdims=True)
                weight = jnp.exp(score - top)
                total = jnp.sum(weight, 0, keepdims=True)
                log_ref[pl.ds(head, 1), span] = top + jnp.log(total)
                prob = (weight * (1.0 / total)).astype(BF)
                outs.append(jnp.dot(values_t, prob, preferred_element_type=F32))
            both = jnp.concatenate(outs, 0).T
            cols = pl.ds(pl.multiple_of(pair * 2 * HD, 2 * HD), 2 * HD)
            mixed_ref[span, cols] = both.astype(BF)
            return carry

        lax.fori_loop(0, PAIRS, one_pair, 0)


def backward_kernel(
    grad_ref,
    rot_ref,
    key_ref,
    value_ref,
    normed_ref,
    inv_ref,
    log_ref,
    cos_ref,
    sin_ref,
    seg_row_ref,
    seg_col_ref,
    gain_ref,
    out_ref,
    gain_grad_ref,
    grad_t,
    query_grad,
    value_one,
    key_sum,
    value_sum,
    out_t,
):
    length = grad_ref.shape[0]
    blocks = length // SPAN
    heads = HEADS + PAIRS
    for part in range(HEADS // 2):
        cols = slice(part * 2 * HD, (part + 1) * 2 * HD)
        grad_t[cols, :] = grad_ref[:, cols].astype(F32).T.astype(BF)
    values_t = value_ref[...].astype(F32).T
    for pair in range(PAIRS):
        value_one[pair] = values_t[pair * HD : (pair + 1) * HD, :].T.astype(BF)
    left_lane = lax.broadcasted_iota(jnp.int32, (SPAN, 2 * HD), 1) < HD
    zero = jnp.zeros((SPAN, 2 * HD), BF)

    def one_pair(pair, carry):
        key_sum[...] = jnp.zeros_like(key_sum)
        value_sum[...] = jnp.zeros_like(value_sum)
        keys_t = rot_ref[pl.ds(pl.multiple_of((HEADS + pair) * HD, HD), HD), :]
        both = pl.ds(pl.multiple_of(pair * 2 * HD, 2 * HD), 2 * HD)
        for block in range(blocks):
            end = (block + 1) * SPAN
            span = slice(block * SPAN, end)
            visible = visible_block(seg_col_ref[...], seg_row_ref[...], block)
            queries = rot_ref[both, span].astype(F32).T.astype(BF)
            grads = grad_ref[span, both]
            for side in range(2):
                head = pair * 2 + side
                rows = pl.ds(pl.multiple_of(head * HD, HD), HD)
                score = jnp.dot(
                    key_ref[pair, 0:end, :], rot_ref[rows, span], preferred_element_type=F32
                )
                prob = jnp.where(visible, jnp.exp(score - log_ref[pl.ds(head, 1), span]), 0.0)
                grad_prob = jnp.dot(
                    value_one[pair, 0:end, :], grad_t[rows, span], preferred_element_type=F32
                )
                inner = jnp.sum(prob * grad_prob, 0, keepdims=True)
                grad_score = (prob * (grad_prob - inner)).astype(BF)
                mine = left_lane if side == 0 else jnp.logical_not(left_lane)
                value_sum[0:end, :] += jnp.dot(
                    prob.astype(BF), jnp.where(mine, grads, zero), preferred_element_type=F32
                )
                key_sum[0:end, :] += jnp.dot(
                    grad_score, jnp.where(mine, queries, zero), preferred_element_type=F32
                )
                query_grad[rows, span] = jnp.dot(
                    keys_t[:, 0:end], grad_score, preferred_element_type=F32
                ) * (HD**-0.5)
        key_t = key_sum[...].T
        value_t = value_sum[...].T
        key_rows = pl.ds(pl.multiple_of((HEADS + pair) * HD, HD), HD)
        query_grad[key_rows, :] = key_t[:HD, :] + key_t[HD:, :]
        value_rows = pl.ds(pl.multiple_of((heads + pair) * HD, HD), HD)
        out_t[value_rows, :] = value_t[:HD, :] + value_t[HD:, :]
        return carry

    lax.fori_loop(0, PAIRS, one_pair, 0)

    cosine = cos_ref[...]
    sine = sin_ref[...]
    gain_sums = [jnp.zeros((HD, length), F32), jnp.zeros((HD, length), F32)]
    for head in range(heads):
        rows = slice(head * HD, (head + 1) * HD)
        kind = 0 if head < HEADS else 1
        part = query_grad[rows, :]
        first = part[:HALF, :]
        second = part[HALF:, :]
        turned = jnp.concatenate(
            [first * cosine + second * sine, second * cosine - first * sine], 0
        )
        normed = normed_ref[rows, :]
        gain_sums[kind] = gain_sums[kind] + turned * normed
        scaled = turned * gain_ref[:, kind : kind + 1]
        mean = jnp.mean(scaled * normed, 0, keepdims=True)
        out_t[rows, :] = inv_ref[head : head + 1, :] * (scaled - normed * mean)
    for kind in range(2):
        gain_grad_ref[:, kind : kind + 1] = jnp.sum(gain_sums[kind], 1, keepdims=True)
    width = out_t.shape[0]
    for part in range(width // (2 * HD)):
        cols = slice(part * 2 * HD, (part + 1) * 2 * HD)
        out_ref[:, cols] = out_t[cols, :].T.astype(BF)


def whole_refs(count):
    return [pl.BlockSpec(memory_space=pltpu.VMEM)] * count


def attention_forward(hidden, weight, cosine, sine, seg_row, seg_col, gains):
    length = hidden.shape[0]
    rows = (HEADS + PAIRS) * HD
    outs = [
        ((length, HEADS * HD), BF),
        ((rows, length), BF),
        ((PAIRS, length, HD), BF),
        ((length, PAIRS * HD), BF),
        ((PAIRS * HD, length), BF),
        ((rows, length), F32),
        ((16, length), F32),
        ((HEADS, length), F32),
    ]
    return pl.pallas_call(
        forward_kernel,
        out_shape=[jax.ShapeDtypeStruct(shape, kind) for shape, kind in outs],
        in_specs=whole_refs(7),
        out_specs=whole_refs(len(outs)),
        compiler_params=pltpu.CompilerParams(vmem_limit_bytes=48 * 1024 * 1024),
        cost_estimate=pl.CostEstimate(
            flops=12 * 10**9, bytes_accessed=16 * 2**20, transcendentals=6 * 10**6
        ),
        name="attention_forward",
    )(hidden, weight, cosine, sine, seg_row, seg_col, gains)


def attention_backward(grad, rot, key, value, normed, inv, log, cosine, sine, seg_row, seg_col, gains):
    length = grad.shape[0]
    rows = (HEADS + PAIRS) * HD
    width = rows + PAIRS * HD
    return pl.pallas_call(
        backward_kernel,
        out_shape=[
            jax.ShapeDtypeStruct((length, width), BF),
            jax.ShapeDtypeStruct((HD, 2), F32),
        ],
        in_specs=whole_refs(12),
        out_specs=whole_refs(2),
        scratch_shapes=[
            pltpu.VMEM((HEADS * HD, length), BF),
            pltpu.VMEM((rows, length), F32),
            pltpu.VMEM((PAIRS, length, HD), BF),
            pltpu.VMEM((length, 2 * HD), F32),
            pltpu.VMEM((length, 2 * HD), F32),
            pltpu.VMEM((width, length), F32),
        ],
        compiler_params=pltpu.CompilerParams(vmem_limit_bytes=56 * 1024 * 1024),
        cost_estimate=pl.CostEstimate(
            flops=25 * 10**9, bytes_accessed=16 * 2**20, transcendentals=6 * 10**6
        ),
        name="attention_backward",
    )(grad, rot, key, value, normed, inv, log, cosine, sine, seg_row, seg_col, gains)


def norm_rows(inputs):
    inv = lax.rsqrt(jnp.mean(inputs * inputs, -1, keepdims=True) + EPS)
    return (inputs * inv, inv)


def norm_back(grad, normed, inv):
    return inv * (grad - normed * jnp.mean(grad * normed, -1, keepdims=True))


def swap_y(value):
    return lax.ppermute(value, "group", Y_SWAP)


def swap_cross(value):
    return lax.ppermute(value, "group", CROSS_SWAP)


def swap_core(value):
    return lax.ppermute(value, "group", CORE_SWAP)


def after(value, *earlier):
    return lax.optimization_barrier((value, earlier))[0]


def cycle_of(count):
    return list(range(0, count, 2)) + list(range(count - 1, 0, -2))


class Ring:
    def __init__(self, way):
        count = lax.axis_size("replica")
        cycle = cycle_of(count)[::way]
        self.count = count
        self.way = way
        self.hops = [(cycle[at], cycle[(at + 1) % count]) for at in range(count)]
        mine = lax.axis_index("replica")
        self.place = jnp.where(lax.rem(mine, 2) == 0, mine // 2, count - 1 - mine // 2)

    def chunk_at(self, back):
        at = lax.rem(self.place - self.way * back + self.count, self.count)
        return jnp.where(at < self.count // 2, 2 * at, 2 * (self.count - 1 - at) + 1)

    def send(self, value):
        return lax.ppermute(value, "replica", self.hops)


def sum_over_ring(ring, pick):
    moving = pick(ring.chunk_at(1)).astype(BF)
    for step in range(ring.count - 1):
        arrived = ring.send(moving)
        moving = (pick(ring.chunk_at(step + 2)) + arrived.astype(F32)).astype(BF)
    return moving


def place_kernel(step, targets, rows, index_ref, *refs):
    chunks = refs[:2]
    count = 1 + max(target[0] for target in targets)
    outs = refs[-3 - count : -3]
    wide = refs[-3:-1]
    sems = refs[-1]
    for side in range(2):
        wide[side][...] = chunks[side][...].astype(F32)
    copies = []
    for at, (store, side, start, end, column) in enumerate(targets):
        row = pl.multiple_of(index_ref[step, side] * rows, 8)
        copies.append(
            pltpu.make_async_copy(
                wide[side].at[:, start:end],
                outs[store].at[pl.ds(row, rows), column : column + end - start],
                sems.at[at],
            )
        )
    for copy in copies:
        copy.start()
    for copy in copies:
        copy.wait()


def place_chunks(step, indices, chunks, stores, shapes, targets):
    rows = chunks[0].shape[0]
    if rows % 8:
        stores = stores or [jnp.zeros(shape, F32) for shape in shapes]
        for store, side, start, end, column in targets:
            stores[store] = lax.dynamic_update_slice(
                stores[store],
                chunks[side][:, start:end].astype(F32),
                (indices[step, side] * rows, column),
            )
        return stores
    given = stores or []
    return list(
        pl.pallas_call(
            functools.partial(place_kernel, step, targets, rows),
            out_shape=[jax.ShapeDtypeStruct(shape, F32) for shape in shapes],
            in_specs=[pl.BlockSpec(memory_space=pltpu.SMEM)]
            + [pl.BlockSpec(memory_space=pltpu.VMEM)] * 2
            + [pl.BlockSpec(memory_space=pl.ANY)] * len(given),
            out_specs=[pl.BlockSpec(memory_space=pl.ANY)] * len(shapes),
            scratch_shapes=[pltpu.VMEM(chunk.shape, F32) for chunk in chunks]
            + [pltpu.SemaphoreType.DMA((len(targets),))],
            input_output_aliases={3 + at: at for at in range(len(given))},
            compiler_params=pltpu.CompilerParams(vmem_limit_bytes=16 * 1024 * 1024),
            name="place_chunks",
        )(indices, *chunks, *given)
    )


def gather_over_rings(rings, indices, chunks, shapes, targets):
    stores = place_chunks(0, indices, chunks, None, shapes, targets)
    for step in range(1, rings[0].count):
        chunks = [ring.send(chunk) for ring, chunk in zip(rings, chunks)]
        stores = place_chunks(step, indices, chunks, stores, shapes, targets)
    return stores


def per_device(
    hidden_in,
    segments,
    positions,
    out_grad,
    attn_gain,
    w_query,
    w_key,
    w_value,
    query_gain,
    key_gain,
    w_out,
    ffn_gain,
    w_gate,
    w_up,
    w_down,
):
    copies = lax.axis_size("replica")
    member = lax.axis_index("group")
    y_at = member // 2
    core = lax.rem(member, 2)
    on_low_y = y_at == 0
    on_low_core = core == 0
    span, width = hidden_in.shape[1:]
    hidden_units = w_down.shape[0]

    def by_y(mine, other):
        return jnp.where(on_low_y, mine, other), jnp.where(on_low_y, other, mine)

    def by_core(mine, other):
        return jnp.where(on_low_core, mine, other), jnp.where(on_low_core, other, mine)

    def at_y(pair_low, pair_high):
        return jnp.where(on_low_y, pair_low, pair_high), jnp.where(on_low_y, pair_high, pair_low)

    def at_core(low, high):
        return jnp.where(on_low_core, low, high), jnp.where(on_low_core, high, low)

    seq_mine, seq_other = at_y(hidden_in[0], hidden_in[1])
    seq_got = swap_y(seq_other)
    w_query, w_key, w_value = after((w_query, w_key, w_value), seq_other)
    w_gate, w_up, w_out = after((w_gate, w_up, w_out), seq_got)

    small = jnp.concatenate(
        [
            attn_gain.astype(F32)[None],
            ffn_gain.astype(F32)[None],
            segments.astype(F32),
            positions.astype(F32),
        ],
        0,
    )
    small_low, small_high = by_y(small, swap_y(small))
    small_two = jnp.stack([small_low, small_high])
    small_even, small_odd = by_core(small_two, swap_core(small_two))
    small_all = jnp.stack([small_even, small_odd], 1).reshape(4, 6, span)
    small_rows = small_all.transpose(1, 0, 2).reshape(6, 4 * span)
    gain_one = small_rows[0]
    gain_two = small_rows[1]
    seg = jnp.where(on_low_y, small_rows[2], small_rows[3])
    place = jnp.where(on_low_y, small_rows[4], small_rows[5])

    own_low, own_high = by_y(seq_mine, seq_got)
    own_in = jnp.stack([own_low, own_high])
    all_even, all_odd = by_core(own_in, swap_core(own_in))
    all_in = jnp.stack([all_even, all_odd], 1).reshape(4 * span, width)

    def quarters(weight):
        size = weight.shape[1] // 4
        return [weight[:, at * size : (at + 1) * size] for at in range(4)]

    low_cols = []
    high_cols = []
    for weight in (w_query, w_key, w_value):
        parts = quarters(weight)
        low_cols += [parts[0], parts[2]]
        high_cols += [parts[1], parts[3]]
    mine_cols, other_cols = at_core(jnp.concatenate(low_cols, 1), jnp.concatenate(high_cols, 1))
    rows_core = swap_core(other_cols)
    rows_y = swap_y(mine_cols)
    rows_cross = swap_cross(other_cols)

    def in_order(mine, at_y, sibling, across):
        here = jnp.concatenate(by_core(mine, sibling), 0)
        there = jnp.concatenate(by_core(at_y, across), 0)
        return jnp.concatenate(by_y(here, there), 0)

    w_attn = in_order(mine_cols, rows_y, rows_core, rows_cross)
    w_mix = jnp.concatenate(by_y(w_out, swap_y(w_out)), 0)
    gate_parts = quarters(w_gate)
    up_parts = quarters(w_up)
    even = lax.rem(lax.axis_index("replica"), 2) == 0

    def halves_by_y(parts):
        pairs = [at_y(parts[at], parts[at + 2]) for at in range(2)]
        return [pair[0] for pair in pairs], [pair[1] for pair in pairs]

    gate_here, gate_there = halves_by_y(gate_parts)
    up_here, up_there = halves_by_y(up_parts)
    gate_mine, gate_sib = at_core(*gate_here)
    up_mine, up_sib = at_core(*up_here)
    one_there = [jnp.where(even, *pair) for pair in zip(gate_there, up_there)]
    one_y, one_cross = at_core(*one_there)
    kind_core = swap_core(jnp.concatenate([gate_sib, up_sib], 1))
    kind_y = swap_y(one_y)
    kind_cross = swap_cross(one_cross)
    by_replica = [(at, at ^ 1) for at in range(copies)]
    normed_all, inv_all = norm_rows(all_in.astype(F32))
    hidden_one = (normed_all * gain_one).astype(BF)
    freq = THETA ** (-(jnp.arange(HALF, dtype=F32) * 2.0 / HD))
    angle = freq[:, None] * place[None, :]
    cosine, sine = jnp.cos(angle), jnp.sin(angle)
    gains = jnp.stack([query_gain, key_gain], 1).astype(F32)
    seg_row = seg[None, :]
    seg_col = seg[:, None]
    mixed, rot, key_rot, value_low, _, head_normed, head_inv, log_total = attention_forward(
        hidden_one, w_attn, cosine, sine, seg_row, seg_col, gains
    )

    kind_y, kind_cross = after((kind_y, kind_cross), mixed)
    other_y = lax.ppermute(kind_y, "replica", by_replica)
    other_cross = lax.ppermute(kind_cross, "replica", by_replica)

    def both_kinds(first, second):
        return jnp.concatenate(
            [jnp.where(even, first, second), jnp.where(even, second, first)], 1
        )

    w_ffn = in_order(
        jnp.concatenate([gate_mine, up_mine], 1),
        both_kinds(kind_y, other_y),
        kind_core,
        both_kinds(kind_cross, other_cross),
    )

    dy_mine, dy_other = at_y(out_grad[0], out_grad[1])
    dy_own = jnp.concatenate(by_y(dy_mine, swap_y(after(dy_other, mixed))), 0)
    dy_sib = swap_core(dy_own)
    dy_near = jnp.concatenate([dy_own, dy_sib], 0)

    def own_and_other(rows):
        parts = rows.reshape(2, 2, span, rows.shape[-1])
        mine, other = at_core(parts[:, 0], parts[:, 1])
        return mine.reshape(2 * span, -1), other.reshape(2 * span, -1)

    mix_part = jnp.dot(mixed, w_mix, preferred_element_type=F32)
    mix_mine, mix_other = own_and_other(mix_part)
    inputs = own_in.reshape(2 * span, width).astype(F32)
    middle = inputs + mix_mine + swap_core(mix_other.astype(BF)).astype(F32)
    normed_two, inv_two = norm_rows(middle)
    hidden_two = (normed_two * gain_two).astype(BF)

    h2_next = swap_y(hidden_two)
    h2_sib = swap_core(hidden_two)
    h2_diag = swap_core(h2_next)
    dy_next = jnp.concatenate(by_y(dy_other, swap_y(after(dy_mine, hidden_two))), 0)
    dy_diag = swap_core(dy_next)
    dy_far = jnp.concatenate([dy_next, dy_diag], 0)
    h2_near = jnp.concatenate([hidden_two, h2_sib], 0)
    h2_far = jnp.concatenate([h2_next, h2_diag], 0)
    units = hidden_units

    def ffn(h2, dy):
        both = contract(h2, w_ffn, 1, 0)
        gate, up = both[:, :units], both[:, units:]
        sig = jax.nn.sigmoid(gate)
        act = (gate * sig * up).astype(BF)
        grad_act = contract(dy, w_down, 1, 1)
        grad_gate = (grad_act * up * sig * (1.0 + gate * (1.0 - sig))).astype(BF)
        grad_up = (grad_act * gate * sig).astype(BF)
        return act, jnp.concatenate([grad_gate, grad_up], 1)

    act_near, grad_near = ffn(h2_near, dy_near)
    act_far, grad_far = ffn(h2_far, dy_far)
    down_grad = (contract(act_near, dy_near, 0, 0) + contract(act_far, dy_far, 0, 0)).astype(BF)
    grad_far = after(grad_far, down_grad)
    back_far = contract(grad_far, w_ffn, 1, 1)
    back_near = contract(grad_near, w_ffn, 1, 1)
    rows_own = 2 * span
    dh2_far = back_far[:rows_own] + swap_core(back_far[rows_own:].astype(BF)).astype(F32)
    dh2_near = back_near[:rows_own] + swap_core(back_near[rows_own:].astype(BF)).astype(F32)
    dh2_got = swap_y(dh2_far.astype(BF))
    ffn_grad = (contract(h2_near, grad_near, 0, 0) + contract(h2_far, grad_far, 0, 0)).astype(BF)
    dh2_got, dh2_near = after((dh2_got, dh2_near), down_grad, ffn_grad)
    grad_hidden_two = dh2_near + dh2_got.astype(F32)

    def chunk_pair(rows):
        parts = rows.reshape(2, span, width)
        return at_y(parts[0], parts[1])

    ffn_gain_part = jnp.sum(grad_hidden_two * normed_two, 0)
    grad_middle = dy_own.astype(F32) + norm_back(grad_hidden_two * gain_two, normed_two, inv_two)
    grad_branch = grad_middle.astype(BF).reshape(2, span, width)
    branch_even, branch_odd = by_core(grad_branch, swap_core(grad_branch))
    branch_all = jnp.stack([branch_even, branch_odd], 1).reshape(4 * span, width)
    grad_mixed = contract(branch_all, w_mix, 1, 1).astype(BF)
    mix_grad = contract(mixed, branch_all, 0, 0)
    grad_heads, head_gain_part = attention_backward(
        grad_mixed,
        rot,
        key_rot,
        value_low,
        head_normed,
        head_inv,
        log_total,
        cosine,
        sine,
        seg_row,
        seg_col,
        gains,
    )
    back_one = contract(grad_heads, w_attn, 1, 1)
    one_mine, one_other = own_and_other(back_one)
    grad_hidden_one = one_mine + swap_core(one_other.astype(BF)).astype(F32)
    inv_one, _ = own_and_other(inv_all)
    normed_one = inputs * inv_one
    attn_gain_part = jnp.sum(grad_hidden_one * normed_one, 0)
    grad_input = grad_middle + norm_back(grad_hidden_one * gain_one, normed_one, inv_one)
    input_here, input_there = chunk_pair(grad_input)
    input_back = swap_y(input_there.astype(BF))

    act_near, act_far = after((act_near, act_far), back_one)
    out_near = contract(act_near, w_down, 1, 0)
    out_far = contract(act_far, w_down, 1, 0)
    out_own = middle + out_near[:rows_own] + swap_core(out_near[rows_own:].astype(BF)).astype(F32)
    out_next = out_far[:rows_own] + swap_core(out_far[rows_own:].astype(BF)).astype(F32)

    own_here, own_there = chunk_pair(out_own)
    next_here, next_there = chunk_pair(out_next)
    out_back = swap_y(jnp.stack([own_there, next_there]).astype(BF))
    attn_grad = contract(hidden_one, grad_heads, 0, 0).reshape(2, 2 * span, -1)
    rows_here, rows_there = at_y(attn_grad[0], attn_grad[1])
    attn_grad_y = rows_here + swap_y(rows_there.astype(BF)).astype(F32)
    mix_here, mix_there = at_y(mix_grad[:span], mix_grad[span:])
    mix_grad_y = mix_here + swap_y(mix_there.astype(BF)).astype(F32)

    right, left = Ring(1), Ring(-1)
    half = width // 2
    rows = span // copies

    def replica_sum(value, dim):
        return lax.psum_scatter(value, "replica", scatter_dimension=dim, tiled=True)

    down_part = replica_sum(down_grad, 0)
    ffn_part = replica_sum(ffn_grad.reshape(4, span, 2 * units), 1)

    def own_rows(part):
        parts = part.reshape(2, 2, rows, units)
        mine, other = at_core(parts[:, 0], parts[:, 1])
        both_cores = jnp.stack(by_core(mine, swap_core(other)), 1)
        here, there = at_y(both_cores[0], both_cores[1])
        all_units = jnp.stack(by_y(here, swap_y(there)))
        return all_units.transpose(2, 0, 1, 3).reshape(rows, 4 * units)

    gate_all = own_rows(ffn_part[..., :units])
    up_all = own_rows(ffn_part[..., units:])
    indices = jnp.stack(
        [jnp.stack([ring.chunk_at(step) for ring in (right, left)]) for step in range(copies)]
    )
    down_part = after(down_part, rows_there)
    (w_down_grad,) = gather_over_rings(
        (right, left),
        indices,
        [down_part[:, :half], down_part[:, half:]],
        [(hidden_units, width)],
        [(0, 0, 0, half, 0), (0, 1, 0, half, half)],
    )

    query_width = 2 * span
    head_sum = jnp.concatenate([attn_grad_y.reshape(2, span, -1), mix_grad_y[None]])
    head_sum = head_sum.reshape(3, copies, rows, width)

    def pick_half(start):
        def pick(index):
            return lax.dynamic_index_in_dim(
                head_sum[..., start : start + half], index, 1, keepdims=False
            )

        return pick

    head_right = sum_over_ring(right, pick_half(0))
    head_left = sum_over_ring(left, pick_half(half))

    def all_heads(part, kinds):
        mine, other = at_core(part[0], part[1])
        even, odd = by_core(mine, swap_core(other))
        shape = (rows, kinds, 2, 1, part.shape[-1] // (2 * kinds))
        return jnp.concatenate([even.reshape(shape), odd.reshape(shape)], 3).reshape(rows, -1)

    query_all = all_heads(head_right[:2], 1)
    rest_all = all_heads(head_left[:2], 2)
    chunk_right = jnp.concatenate([gate_all, query_all, head_right[2]], 1)
    chunk_left = jnp.concatenate([up_all, rest_all, head_left[2]], 1)
    full = 4 * span
    gate_end = 4 * units
    heads_end = gate_end + full
    w_gate_grad, w_up_grad, w_query_grad, w_key_grad, w_value_grad, w_out_grad = gather_over_rings(
        (right, left),
        indices,
        [chunk_right, chunk_left],
        [(span, value.shape[1]) for value in (w_gate, w_up, w_query, w_key, w_value, w_out)],
        [
            (0, 0, 0, gate_end, 0),
            (1, 1, 0, gate_end, 0),
            (2, 0, gate_end, heads_end, 0),
            (3, 1, gate_end, gate_end + full // 2, 0),
            (4, 1, gate_end + full // 2, heads_end, 0),
            (5, 0, heads_end, heads_end + half, 0),
            (5, 1, heads_end, heads_end + half, half),
        ],
    )

    sums = jnp.concatenate([attn_gain_part, ffn_gain_part, head_gain_part.T.reshape(-1)])
    sums = after(sums.reshape(-1, 128), head_right)
    sums = sums + swap_core(sums)
    sums = sums + swap_y(sums)
    step = 1
    while step < copies:
        sums = sums + lax.ppermute(sums, "replica", [(at, at ^ step) for at in range(copies)])
        step *= 2
    sums = sums.reshape(-1)
    attn_gain_grad = lax.dynamic_slice(sums, (member * span,), (span,))
    ffn_gain_grad = lax.dynamic_slice(sums, (width + member * span,), (span,))
    query_gain_grad = sums[2 * width : 2 * width + HD]
    key_gain_grad = sums[2 * width + HD : 2 * width + 2 * HD]

    out_back, input_back = after((out_back, input_back), head_right)
    out_back, input_back = out_back.astype(F32), input_back.astype(F32)
    input_grad = jnp.stack(by_y(input_here, input_back))
    block_out = jnp.stack(by_y(own_here + out_back[1], next_here + out_back[0])).astype(BF)

    return (
        block_out,
        input_grad,
        attn_gain_grad,
        w_query_grad,
        w_key_grad,
        w_value_grad,
        query_gain_grad,
        key_gain_grad,
        w_out_grad,
        ffn_gain_grad,
        w_gate_grad,
        w_up_grad,
        w_down_grad,
    )


def solution(mesh):
    rows = P("group", None)
    tokens = P("replica", "group", None)
    placed = (
        tokens,
        P("replica", "group"),
        P("replica", "group"),
        tokens,
        P("group"),
        rows,
        rows,
        rows,
        P(),
        P(),
        rows,
        P("group"),
        rows,
        rows,
        rows,
    )
    return jax.shard_map(
        per_device,
        mesh=mesh,
        in_specs=placed,
        out_specs=(
            tokens,
            tokens,
            P("group"),
            rows,
            rows,
            rows,
            P(),
            P(),
            rows,
            P("group"),
            rows,
            rows,
            rows,
        ),
        check_vma=False,
    )
```

```python
import functools

import jax
import jax.numpy as jnp
from jax import lax
from jax.experimental import pallas as pl
from jax.experimental.pallas import tpu as pltpu
from jax.sharding import PartitionSpec as P

HEADS = 8
PAIRS = 4
HD = 64
HALF = 32
SPAN = 256
LANES = 128

EPS = 1e-05
THETA = 1000000.0
NEG = -1e30

BF = jnp.bfloat16
F32 = jnp.float32
NO_COST = pl.CostEstimate(flops=0, bytes_accessed=0, transcendentals=0)

Y_SWAP = [(0, 2), (2, 0), (1, 3), (3, 1)]
CORE_SWAP = [(0, 1), (1, 0), (2, 3), (3, 2)]
CROSS_SWAP = [(0, 3), (3, 0), (1, 2), (2, 1)]


def contract(left, right, left_dim, right_dim):
    return lax.dot_general(
        left, right, (((left_dim,), (right_dim,)), ((), ())), preferred_element_type=F32
    )


def visible_block(seg_col, seg_row, block):
    end = (block + 1) * SPAN
    key_at = lax.broadcasted_iota(jnp.int32, (end, SPAN), 0)
    query_at = lax.broadcasted_iota(jnp.int32, (end, SPAN), 1) + block * SPAN
    return (seg_col[0:end, :] == seg_row[:, block * SPAN : end]) & (key_at <= query_at)


def project_kernel(
    hidden_ref,
    weight_ref,
    cos_ref,
    sin_ref,
    gain_ref,
    rot_ref,
    key_ref,
    value_ref,
    value_t_ref,
    normed_ref,
    inv_ref,
):
    blocks = hidden_ref.shape[0] // SPAN
    heads = HEADS + PAIRS
    for block in range(blocks):
        span = slice(block * SPAN, (block + 1) * SPAN)
        raw = jnp.dot(hidden_ref[span, :], weight_ref[...], preferred_element_type=F32)
        raw_t = raw.T
        for half in range(2):
            cols = slice(half * 2 * SPAN + 3 * LANES, (half + 1) * 2 * SPAN)
            place = slice(half * LANES, (half + 1) * LANES)
            value_ref[span, place] = raw[:, cols].astype(BF)
            value_t_ref[place, span] = raw_t[cols, :].astype(BF)
        cosine = cos_ref[:, span]
        sine = sin_ref[:, span]
        for head in range(heads):
            rows = slice(head * HD, (head + 1) * HD)
            if head < HEADS:
                at = head // 4 * 2 * SPAN + head % 4 * HD
            else:
                at = (head - HEADS) // 2 * 2 * SPAN + SPAN + head % 2 * HD
            part = raw_t[at : at + HD, :]
            inv = lax.rsqrt(jnp.mean(part * part, 0, keepdims=True) + EPS)
            normed = part * inv
            normed_ref[rows, span] = normed
            inv_ref[head : head + 1, span] = inv
            kind = 0 if head < HEADS else 1
            scaled = normed * gain_ref[:, kind : kind + 1]
            first = scaled[:HALF, :]
            second = scaled[HALF:, :]
            turned = jnp.concatenate(
                [first * cosine - second * sine, second * cosine + first * sine], 0
            )
            if head < HEADS:
                rot_ref[rows, span] = turned.astype(BF) * BF(HD**-0.5)
            else:
                rot_ref[rows, span] = turned.astype(BF)
    for pair in range(PAIRS):
        rows = slice((HEADS + pair) * HD, (HEADS + pair + 1) * HD)
        key_ref[pair] = rot_ref[rows, :].astype(F32).T.astype(BF)


def forward_kernel(
    rot_ref,
    key_ref,
    value_t_ref,
    seg_row_ref,
    seg_col_ref,
    at_ref,
    w_own_ref,
    w_got_ref,
    mixed_ref,
    log_ref,
    w_mix_ref,
    mine_ref,
    other_ref,
):
    w_mix_ref[pl.ds(pl.multiple_of(at_ref[0] * SPAN, SPAN), SPAN), :] = w_own_ref[...]
    w_mix_ref[pl.ds(pl.multiple_of((1 - at_ref[0]) * SPAN, SPAN), SPAN), :] = w_got_ref[...]
    for block in range(mixed_ref.shape[0] // SPAN):
        end = (block + 1) * SPAN
        span = slice(block * SPAN, end)
        visible = visible_block(seg_col_ref[...], seg_row_ref[...], block)

        def one_pair(pair, carry, end=end, span=span, visible=visible):
            keys = key_ref[pair, 0:end, :]
            values_t = value_t_ref[pl.ds(pl.multiple_of(pair * HD, HD), HD), 0:end]
            outs = []
            for side in range(2):
                head = pair * 2 + side
                rows = pl.ds(pl.multiple_of(head * HD, HD), HD)
                score = jnp.dot(keys, rot_ref[rows, span], preferred_element_type=F32)
                score = jnp.where(visible, score, NEG)
                top = jnp.max(score, 0, keepdims=True)
                weight = jnp.exp(score - top)
                total = jnp.sum(weight, 0, keepdims=True)
                log_ref[pl.ds(head, 1), span] = top + jnp.log(total)
                prob = (weight * (1.0 / total)).astype(BF)
                outs.append(jnp.dot(values_t, prob, preferred_element_type=F32))
            both = jnp.concatenate(outs, 0).T
            cols = pl.ds(pl.multiple_of(pair * 2 * HD, 2 * HD), 2 * HD)
            mixed_ref[span, cols] = both.astype(BF)
            return carry

        lax.fori_loop(0, PAIRS, one_pair, 0)
    core = at_ref[1]
    for part in range(2):
        span = slice(part * SPAN, (part + 1) * SPAN)
        for where, out in ((core, mine_ref), (1 - core, other_ref)):
            rows = pl.ds(pl.multiple_of((2 * part + where) * SPAN, SPAN), SPAN)
            out[span, :] = jnp.dot(
                mixed_ref[rows, :], w_mix_ref[...], preferred_element_type=F32
            ).astype(out.dtype)


def backward_kernel(
    half,
    grad_ref,
    query_ref,
    key_t_ref,
    key_ref,
    value_ref,
    query_normed_ref,
    key_normed_ref,
    inv_ref,
    log_ref,
    cos_ref,
    sin_ref,
    seg_row_ref,
    seg_col_ref,
    gain_ref,
    out_ref,
    gain_grad_ref,
    grad_t,
    head_grad,
    value_one,
    key_sum,
    value_sum,
    out_t,
):
    length = grad_ref.shape[0]
    heads = HEADS // 2
    pairs = PAIRS // 2
    for part in range(pairs):
        cols = slice(part * 2 * HD, (part + 1) * 2 * HD)
        grad_t[cols, :] = grad_ref[:, cols].astype(F32).T.astype(BF)
    values_t = value_ref[...].astype(F32).T
    for pair in range(pairs):
        value_one[pair] = values_t[pair * HD : (pair + 1) * HD, :].T.astype(BF)
    left_lane = lax.broadcasted_iota(jnp.int32, (SPAN, 2 * HD), 1) < HD
    zero = jnp.zeros((SPAN, 2 * HD), BF)

    def one_pair(pair, carry):
        key_sum[...] = jnp.zeros_like(key_sum)
        value_sum[...] = jnp.zeros_like(value_sum)
        keys_t = key_t_ref[pl.ds(pl.multiple_of(pair * HD, HD), HD), :]
        both = pl.ds(pl.multiple_of(pair * 2 * HD, 2 * HD), 2 * HD)
        for block in range(length // SPAN):
            end = (block + 1) * SPAN
            span = slice(block * SPAN, end)
            visible = visible_block(seg_col_ref[...], seg_row_ref[...], block)
            queries = query_ref[both, span].astype(F32).T.astype(BF)
            grads = grad_ref[span, both]
            for side in range(2):
                head = pair * 2 + side
                rows = pl.ds(pl.multiple_of(head * HD, HD), HD)
                score = jnp.dot(
                    key_ref[pair, 0:end, :], query_ref[rows, span], preferred_element_type=F32
                )
                logs = log_ref[pl.ds(half * heads + head, 1), span]
                prob = jnp.where(visible, jnp.exp(score - logs), 0.0)
                grad_prob = jnp.dot(
                    value_one[pair, 0:end, :], grad_t[rows, span], preferred_element_type=F32
                )
                inner = jnp.sum(prob * grad_prob, 0, keepdims=True)
                grad_score = (prob * (grad_prob - inner)).astype(BF)
                mine = left_lane if side == 0 else jnp.logical_not(left_lane)
                value_sum[0:end, :] += jnp.dot(
                    prob.astype(BF), jnp.where(mine, grads, zero), preferred_element_type=F32
                )
                key_sum[0:end, :] += jnp.dot(
                    grad_score, jnp.where(mine, queries, zero), preferred_element_type=F32
                )
                head_grad[rows, span] = jnp.dot(
                    keys_t[:, 0:end], grad_score, preferred_element_type=F32
                ) * (HD**-0.5)
        key_t = key_sum[...].T
        value_t = value_sum[...].T
        key_rows = pl.ds(pl.multiple_of((heads + pair) * HD, HD), HD)
        head_grad[key_rows, :] = key_t[:HD, :] + key_t[HD:, :]
        value_rows = pl.ds(pl.multiple_of((heads + pairs + pair) * HD, HD), HD)
        out_t[value_rows, :] = value_t[:HD, :] + value_t[HD:, :]
        return carry

    lax.fori_loop(0, pairs, one_pair, 0)

    cosine = cos_ref[...]
    sine = sin_ref[...]
    gain_sums = [jnp.zeros((HD, length), F32), jnp.zeros((HD, length), F32)]
    for head in range(heads + pairs):
        rows = slice(head * HD, (head + 1) * HD)
        kind = 0 if head < heads else 1
        part = head_grad[rows, :]
        first = part[:HALF, :]
        second = part[HALF:, :]
        turned = jnp.concatenate(
            [first * cosine + second * sine, second * cosine - first * sine], 0
        )
        if kind == 0:
            normed = query_normed_ref[rows, :]
            line = half * heads + head
        else:
            normed = key_normed_ref[(head - heads) * HD : (head - heads + 1) * HD, :]
            line = HEADS + half * pairs + head - heads
        gain_sums[kind] = gain_sums[kind] + turned * normed
        scaled = turned * gain_ref[:, kind : kind + 1]
        mean = jnp.mean(scaled * normed, 0, keepdims=True)
        out_t[rows, :] = inv_ref[line : line + 1, :] * (scaled - normed * mean)
    for kind in range(2):
        gain_grad_ref[:, kind : kind + 1] = jnp.sum(gain_sums[kind], 1, keepdims=True)
    for part in range(out_t.shape[0] // (2 * HD)):
        cols = slice(part * 2 * HD, (part + 1) * 2 * HD)
        out_ref[:, cols] = out_t[cols, :].T.astype(BF)


def in_hbm(shape, kind):
    return pltpu.HBM(shape, kind)


def from_hbm(*operands):
    return [
        pltpu.with_memory_space_constraint(value, pltpu.HBM) if value.size >= 2**16 else value
        for value in operands
    ]


def whole_refs(count):
    return [pl.BlockSpec(memory_space=pltpu.VMEM)] * count


def project(hidden, weight, cosine, sine, gains):
    length = hidden.shape[0]
    rows = (HEADS + PAIRS) * HD
    outs = [
        ((rows, length), BF),
        ((PAIRS, length, HD), BF),
        ((length, PAIRS * HD), BF),
        ((PAIRS * HD, length), BF),
        ((rows, length), F32),
        ((16, length), F32),
    ]
    return pl.pallas_call(
        project_kernel,
        out_shape=[in_hbm(shape, kind) for shape, kind in outs],
        in_specs=whole_refs(5),
        out_specs=whole_refs(len(outs)),
        compiler_params=pltpu.CompilerParams(vmem_limit_bytes=24 * 1024 * 1024),
        cost_estimate=NO_COST,
        name="project",
    )(*from_hbm(hidden, weight), cosine, sine, gains)


def attention_forward(rot, key, value_t, seg_row, seg_col, at, w_own, w_got):
    length = rot.shape[1]
    width = w_own.shape[1]
    outs = [
        ((length, HEADS * HD), BF),
        ((HEADS, length), F32),
        ((HEADS * HD, width), BF),
        ((length // 2, width), F32),
        ((length // 2, width), BF),
    ]
    return pl.pallas_call(
        forward_kernel,
        out_shape=[in_hbm(shape, kind) for shape, kind in outs],
        in_specs=whole_refs(5) + [pl.BlockSpec(memory_space=pltpu.SMEM)] + whole_refs(2),
        out_specs=whole_refs(len(outs)),
        compiler_params=pltpu.CompilerParams(vmem_limit_bytes=24 * 1024 * 1024),
        cost_estimate=NO_COST,
        name="attention_forward",
    )(*from_hbm(rot, key, value_t), seg_row, seg_col, at, *from_hbm(w_own, w_got))


def middle_kernel(inputs_ref, mine_ref, got_ref, gain_ref, middle_ref, hidden_ref):
    middle = inputs_ref[...].astype(F32) + mine_ref[...] + got_ref[...].astype(F32)
    middle_ref[...] = middle
    normed, _ = norm_rows(middle)
    hidden_ref[...] = (normed * gain_ref[...]).astype(BF)


def by_rows(kernel, name, rows_in, whole_in, rows_out, sums_out=0):
    rows, width = rows_in[0].shape
    tile = 2 * LANES
    block = pl.BlockSpec((tile, width), lambda at: (at, 0))
    line = pl.BlockSpec((1, width), lambda at: (0, 0))
    return pl.pallas_call(
        kernel,
        grid=(rows // tile,),
        out_shape=[in_hbm((rows, width), kind) for kind in rows_out]
        + [jax.ShapeDtypeStruct((1, width), F32)] * sums_out,
        in_specs=[block] * len(rows_in) + [line] * len(whole_in),
        out_specs=[block] * len(rows_out) + [line] * sums_out,
        compiler_params=pltpu.CompilerParams(vmem_limit_bytes=16 * 1024 * 1024),
        cost_estimate=NO_COST,
        name=name,
    )(*[from_hbm(value)[0] if value.dtype == F32 else value for value in rows_in], *whole_in)


def middle_grad_kernel(
    own_ref, sib_ref, got_ref, middle_ref, dy_ref, gain_ref, grad_ref, branch_ref, gain_grad_ref
):
    dh2 = own_ref[...] + sib_ref[...].astype(F32) + got_ref[...].astype(F32)
    normed, inv = norm_rows(middle_ref[...])

    @pl.when(pl.program_id(0) == 0)
    def _():
        gain_grad_ref[...] = jnp.zeros_like(gain_grad_ref)

    gain_grad_ref[...] += jnp.sum(dh2 * normed, 0, keepdims=True)
    grad = dy_ref[...].astype(F32) + norm_back(dh2 * gain_ref[...], normed, inv)
    grad_ref[...] = grad
    branch_ref[...] = grad.astype(BF)


def attention_backward(half, grad, rot, key, value, normed, inv, log, cosine, sine, seg_row, seg_col, gains):
    length = grad.shape[0]
    queries = HEADS * HD // 2
    keys = PAIRS * HD // 2
    width = queries + 2 * keys

    def rows_of(count, at):
        return pl.BlockSpec((count, length), lambda step: (at, 0))

    def columns_of(count):
        return pl.BlockSpec((length, count), lambda step: (0, half))

    key_at = 2 * queries // keys + half
    return pl.pallas_call(
        functools.partial(backward_kernel, half),
        grid=(1,),
        out_shape=[
            in_hbm((length, width), BF),
            jax.ShapeDtypeStruct((HD, 2), F32),
        ],
        in_specs=[
            columns_of(queries),
            rows_of(queries, half),
            rows_of(keys, key_at),
            pl.BlockSpec((PAIRS // 2, length, HD), lambda step: (half, 0, 0)),
            columns_of(keys),
            rows_of(queries, half),
            rows_of(keys, key_at),
        ]
        + whole_refs(7),
        out_specs=whole_refs(2),
        scratch_shapes=[
            pltpu.VMEM((queries, length), BF),
            pltpu.VMEM((queries + keys, length), F32),
            pltpu.VMEM((PAIRS // 2, length, HD), BF),
            pltpu.VMEM((length, 2 * HD), F32),
            pltpu.VMEM((length, 2 * HD), F32),
            pltpu.VMEM((width, length), F32),
        ],
        compiler_params=pltpu.CompilerParams(vmem_limit_bytes=28 * 1024 * 1024),
        cost_estimate=NO_COST,
        name="attention_backward",
    )(
        *from_hbm(grad, rot, rot, key, value, normed, normed),
        inv,
        log,
        cosine,
        sine,
        seg_row,
        seg_col,
        gains,
    )


def feed_forward_kernel(
    at_ref,
    h2_a,
    h2_b,
    dy_a,
    dy_a_got,
    dy_b,
    dy_b_got,
    w_gate,
    w_up,
    w_sib,
    piece_0,
    piece_1,
    piece_2,
    piece_3,
    w_down,
    act_a,
    act_b,
    grad_a,
    grad_b,
    back_a,
    back_b,
    dy_out_a,
    dy_out_b,
    h2_v,
    dy_v,
    in_v,
    down_v,
    act_v,
    grad_v,
    back_own,
    back_sib,
    grad_act,
    load_sems,
    store_sems,
):
    units = down_v.shape[0]

    def rows_at(index):
        return pl.ds(pl.multiple_of(at_ref[index], SPAN), SPAN)

    def units_at(index):
        return pl.ds(pl.multiple_of(at_ref[index], LANES), units)

    loads = []

    def load(source, target):
        loads.append(pltpu.make_async_copy(source, target, load_sems.at[len(loads)]))
        loads[-1].start()

    def load_dy(part, own, got):
        load(own.at[at_ref[0]], dy_v.at[part, rows_at(1)])
        load(got.at[at_ref[0]], dy_v.at[part, rows_at(2)])

    load_dy(0, dy_a, dy_a_got)
    load(w_down, down_v)
    load(h2_a, h2_v.at[0])
    load(w_gate.at[:, units_at(3)], in_v.at[rows_at(4), 0:units])
    load(w_up.at[:, units_at(3)], in_v.at[rows_at(4), units : 2 * units])
    load(w_sib, in_v.at[rows_at(5)])
    for at, piece in enumerate((piece_0, piece_1, piece_2, piece_3)):
        load(piece, in_v.at[rows_at(6 + at), units_at(10 + at)])
    weights_end = len(loads)
    load_dy(1, dy_b, dy_b_got)
    load(h2_b, h2_v.at[1])
    stores = []
    for part in range(2):
        for at in range(3) if part == 0 else range(weights_end, weights_end + 2):
            loads[at].wait()
        for start in range(0, units, 256):
            end = min(start + 256, units)
            grad_act[:, start:end] = contract(dy_v[part], down_v[start:end, :], 1, 1)
        for at in range(3, weights_end) if part == 0 else [weights_end + 2]:
            loads[at].wait()
        for start in range(0, units, LANES):
            gate_cols = slice(start, start + LANES)
            up_cols = slice(units + start, units + start + LANES)
            weight = jnp.concatenate([in_v[:, gate_cols], in_v[:, up_cols]], 1)
            both = jnp.dot(h2_v[part], weight, preferred_element_type=F32)
            gate, up = both[:, :LANES], both[:, LANES:]
            sig = jax.nn.sigmoid(gate)
            silu = gate * sig
            grad = grad_act[:, gate_cols]
            act_v[part, :, gate_cols] = (silu * up).astype(BF)
            grad_gate = grad * up * sig * (1.0 + gate * (1.0 - sig))
            grad_v[part, :, gate_cols] = grad_gate.astype(BF)
            grad_v[part, :, up_cols] = (grad * silu).astype(BF)
        back = contract(grad_v[part], in_v[...], 1, 1)
        if part == 0:
            back_own[...] = back
        else:
            back_sib[...] = back.astype(BF)
        for at, (source, target) in enumerate(
            [
                (act_v.at[part], (act_a, act_b)[part]),
                (grad_v.at[part], (grad_a, grad_b)[part]),
                ((back_own, back_sib)[part], (back_a, back_b)[part]),
                (dy_v.at[part], (dy_out_a, dy_out_b)[part]),
            ]
        ):
            stores.append(pltpu.make_async_copy(source, target, store_sems.at[part * 4 + at]))
            stores[-1].start()
    for store in stores:
        store.wait()


def feed_forward(at, h2, dy, weights, w_down):
    rows, width = h2[0].shape
    units = w_down.shape[0]
    outs = (
        [((rows, units), BF)] * 2
        + [((rows, 2 * units), BF)] * 2
        + [((rows, width), F32), ((rows, width), BF)]
        + [((rows, width), BF)] * 2
    )
    operands = from_hbm(*h2, *dy, *weights, w_down)
    return pl.pallas_call(
        feed_forward_kernel,
        out_shape=[in_hbm(shape, kind) for shape, kind in outs],
        in_specs=[pl.BlockSpec(memory_space=pltpu.SMEM)]
        + [pl.BlockSpec(memory_space=pl.ANY)] * len(operands),
        out_specs=[pl.BlockSpec(memory_space=pl.ANY)] * len(outs),
        scratch_shapes=[
            pltpu.VMEM((2, rows, width), BF),
            pltpu.VMEM((2, rows, width), BF),
            pltpu.VMEM((width, 2 * units), BF),
            pltpu.VMEM(w_down.shape, BF),
            pltpu.VMEM((2, rows, units), BF),
            pltpu.VMEM((2, rows, 2 * units), BF),
            pltpu.VMEM((rows, width), F32),
            pltpu.VMEM((rows, width), BF),
            pltpu.VMEM((rows, units), F32),
            pltpu.SemaphoreType.DMA((14,)),
            pltpu.SemaphoreType.DMA((8,)),
        ],
        compiler_params=pltpu.CompilerParams(vmem_limit_bytes=36 * 1024 * 1024),
        cost_estimate=NO_COST,
        name="feed_forward",
    )(at, *operands)


def weight_grad_kernel(count, *refs):
    left, right = refs[:count], refs[count : 2 * count]
    out, left_t = refs[-2:]

    @pl.when(pl.program_id(0) == 0)
    def _():
        for at in range(count):
            left_t[at] = left[at][...].T

    total = jnp.dot(left_t[0], right[0][...], preferred_element_type=F32)
    for at in range(1, count):
        total += jnp.dot(left_t[at], right[at][...], preferred_element_type=F32)
    out[...] = total.astype(BF)


def weight_grad(left, right):
    rows, height = left[0].shape
    width = right[0].shape[1]
    count = len(left)
    step = SPAN
    return pl.pallas_call(
        functools.partial(weight_grad_kernel, count),
        grid=(width // step,),
        out_shape=in_hbm((height, width), BF),
        in_specs=[pl.BlockSpec((rows, height), lambda at: (0, 0))] * count
        + [pl.BlockSpec((rows, step), lambda at: (0, at))] * count,
        out_specs=pl.BlockSpec((height, step), lambda at: (0, at)),
        scratch_shapes=[pltpu.VMEM((count, height, rows), BF)],
        compiler_params=pltpu.CompilerParams(vmem_limit_bytes=24 * 1024 * 1024),
        cost_estimate=NO_COST,
        name="weight_grad",
    )(*from_hbm(*left, *right))


def norm_rows(inputs):
    inv = lax.rsqrt(jnp.mean(inputs * inputs, -1, keepdims=True) + EPS)
    return (inputs * inv, inv)


def norm_back(grad, normed, inv):
    return inv * (grad - normed * jnp.mean(grad * normed, -1, keepdims=True))


def swap_y(value):
    return lax.ppermute(value, "group", Y_SWAP)


def swap_cross(value):
    return lax.ppermute(value, "group", CROSS_SWAP)


def swap_core(value):
    return lax.ppermute(value, "group", CORE_SWAP)


def after(value, *earlier):
    return lax.optimization_barrier((value, earlier))[0]


def cycle_of(count):
    return list(range(0, count, 2)) + list(range(count - 1, 0, -2))


class Ring:
    def __init__(self, way):
        count = lax.axis_size("replica")
        cycle = cycle_of(count)[::way]
        self.count = count
        self.way = way
        self.hops = [(cycle[at], cycle[(at + 1) % count]) for at in range(count)]
        mine = lax.axis_index("replica")
        self.place = jnp.where(lax.rem(mine, 2) == 0, mine // 2, count - 1 - mine // 2)

    def chunk_at(self, back):
        at = lax.rem(self.place - self.way * back + self.count, self.count)
        return jnp.where(at < self.count // 2, 2 * at, 2 * (self.count - 1 - at) + 1)

    def send(self, value):
        return lax.ppermute(value, "replica", self.hops)


def pick_kernel(step, count, index_ref, *refs):
    sources = refs[:count]
    arrived = refs[count:-5]
    outs = refs[-5:-3]
    low, high, sems = refs[-3:]
    rows_low = low.shape[1]
    half = low.shape[2]
    down_rows, rows = rows_low, high.shape[2]
    copies = []
    for side in range(2):
        index = index_ref[step, side]
        cols = slice(side * half, (side + 1) * half)
        copies.append(
            pltpu.make_async_copy(
                sources[0].at[pl.ds(pl.multiple_of(index * down_rows, 16), down_rows), cols],
                low.at[side],
                sems.at[side, 0],
            )
        )
        copies.append(
            pltpu.make_async_copy(
                sources[1].at[:, pl.ds(pl.multiple_of(index * rows, 16), rows), cols],
                high.at[side],
                sems.at[side, 1],
            )
        )
    for copy in copies:
        copy.start()
    for copy in copies:
        copy.wait()
    for side in range(2):
        parts = [(0, rows_low, low[side].astype(F32))]
        for at in range(high.shape[1]):
            start = rows_low + at * rows
            parts.append((start, start + rows, high[side, at].astype(F32)))
        for start, end, part in parts:
            if arrived:
                part = part + arrived[side][start:end, :].astype(F32)
            outs[side][start:end, :] = part.astype(BF)


def pick_chunks(step, indices, sources, arrived):
    copies = indices.shape[0]
    down_rows = sources[0].shape[0] // copies
    kinds, span, width = sources[1].shape
    rows = span // copies
    half = width // 2
    if rows % 16 or down_rows % 16:
        moving = []
        for side in range(2):
            index = indices[step, side]
            start = side * half
            low = lax.dynamic_slice(sources[0], (index * down_rows, start), (down_rows, half))
            high = lax.dynamic_slice(sources[1], (0, index * rows, start), (kinds, rows, half))
            part = jnp.concatenate([low.astype(F32), high.astype(F32).reshape(-1, half)])
            if arrived:
                part = part + arrived[side].astype(F32)
            moving.append(part.astype(BF))
        return moving
    total = down_rows + kinds * rows
    return pl.pallas_call(
        functools.partial(pick_kernel, step, 2),
        out_shape=[jax.ShapeDtypeStruct((total, half), BF)] * 2,
        in_specs=[pl.BlockSpec(memory_space=pltpu.SMEM)]
        + [pl.BlockSpec(memory_space=pl.ANY)] * 2
        + whole_refs(len(arrived)),
        out_specs=whole_refs(2),
        scratch_shapes=[
            pltpu.VMEM((2, down_rows, half), sources[0].dtype),
            pltpu.VMEM((2, kinds, rows, half), sources[1].dtype),
            pltpu.SemaphoreType.DMA((2, 2)),
        ],
        compiler_params=pltpu.CompilerParams(vmem_limit_bytes=8 * 1024 * 1024),
        cost_estimate=NO_COST,
        name="pick_chunks",
    )(indices, *from_hbm(*sources), *arrived)


def sum_over_rings(rings, indices, sources):
    moving = pick_chunks(1, indices, sources, [])
    for step in range(2, rings[0].count + 1):
        arrived = [ring.send(chunk) for ring, chunk in zip(rings, moving)]
        moving = pick_chunks(step % rings[0].count, indices, sources, arrived)
    return moving


def place_kernel(step, targets, stores, index_ref, *refs):
    chunks = refs[:2]
    outs = refs[-3 - stores : -3]
    wide = refs[-3:-1]
    sems = refs[-1]
    for side in range(2):
        wide[side][...] = chunks[side][...].astype(F32)
    copies = []
    for at, (store, side, (top, bottom), (start, end), column) in enumerate(targets):
        rows = bottom - top
        row = pl.multiple_of(index_ref[step, side] * rows, 8)
        copies.append(
            pltpu.make_async_copy(
                wide[side].at[top:bottom, start:end],
                outs[store].at[pl.ds(row, rows), column : column + end - start],
                sems.at[at],
            )
        )
    for copy in copies:
        copy.start()
    for copy in copies:
        copy.wait()


def place_chunks(step, indices, chunks, stores, shapes, targets):
    if any((bottom - top) % 8 for _, _, (top, bottom), _, _ in targets):
        stores = stores or [jnp.zeros(shape, F32) for shape in shapes]
        for store, side, (top, bottom), (start, end), column in targets:
            stores[store] = lax.dynamic_update_slice(
                stores[store],
                chunks[side][top:bottom, start:end].astype(F32),
                (indices[step, side] * (bottom - top), column),
            )
        return stores
    given = stores or []
    return list(
        pl.pallas_call(
            functools.partial(place_kernel, step, targets, len(shapes)),
            out_shape=[in_hbm(shape, F32) for shape in shapes],
            in_specs=[pl.BlockSpec(memory_space=pltpu.SMEM)]
            + [pl.BlockSpec(memory_space=pltpu.VMEM)] * 2
            + [pl.BlockSpec(memory_space=pl.ANY)] * len(given),
            out_specs=[pl.BlockSpec(memory_space=pl.ANY)] * len(shapes),
            scratch_shapes=[pltpu.VMEM(chunk.shape, F32) for chunk in chunks]
            + [pltpu.SemaphoreType.DMA((len(targets),))],
            input_output_aliases={3 + at: at for at in range(len(given))},
            compiler_params=pltpu.CompilerParams(vmem_limit_bytes=8 * 1024 * 1024),
            cost_estimate=NO_COST,
            name="place_chunks",
        )(indices, *chunks, *from_hbm(*given))
    )


def gather_over_rings(rings, indices, chunks, shapes, targets):
    stores = place_chunks(0, indices, chunks, None, shapes, targets)
    earlier = []
    for step in range(1, rings[0].count):
        chunks = [ring.send(chunk) for ring, chunk in zip(rings, after(chunks, *earlier))]
        earlier = stores
        stores = place_chunks(step, indices, chunks, stores, shapes, targets)
    return stores


def per_device(
    hidden_in,
    segments,
    positions,
    out_grad,
    attn_gain,
    w_query,
    w_key,
    w_value,
    query_gain,
    key_gain,
    w_out,
    ffn_gain,
    w_gate,
    w_up,
    w_down,
):
    copies = lax.axis_size("replica")
    member = lax.axis_index("group")
    y_at = member // 2
    core = lax.rem(member, 2)
    on_low_y = y_at == 0
    on_low_core = core == 0
    span, width = hidden_in.shape[1:]
    hidden_units = w_down.shape[0]

    def by_y(mine, other):
        return jnp.where(on_low_y, mine, other), jnp.where(on_low_y, other, mine)

    def by_core(mine, other):
        return jnp.where(on_low_core, mine, other), jnp.where(on_low_core, other, mine)

    def at_y(pair_low, pair_high):
        return jnp.where(on_low_y, pair_low, pair_high), jnp.where(on_low_y, pair_high, pair_low)

    def at_core(low, high):
        return jnp.where(on_low_core, low, high), jnp.where(on_low_core, high, low)

    def quarters(weight):
        size = weight.shape[1] // 4
        return [weight[:, at * size : (at + 1) * size] for at in range(4)]

    def core_columns(*weights):
        parts = [quarters(weight) for weight in weights]
        low = [part[0] for part in parts] + [part[2] for part in parts]
        high = [part[1] for part in parts] + [part[3] for part in parts]
        return at_core(jnp.concatenate(low, 1), jnp.concatenate(high, 1))

    def own_and_other(rows):
        parts = rows.reshape(2, 2, span, rows.shape[-1])
        mine, other = at_core(parts[:, 0], parts[:, 1])
        return mine.reshape(2 * span, -1), other.reshape(2 * span, -1)

    def in_order(mine, at_y, sibling, across):
        here = jnp.concatenate(by_core(mine, sibling), 0)
        there = jnp.concatenate(by_core(at_y, across), 0)
        return jnp.concatenate(by_y(here, there), 0)

    replica = lax.axis_index("replica")
    bit_low = lax.rem(replica, 2)
    bit_high = lax.rem(replica // 2, 2)

    def swap_replica(value, bit):
        return lax.ppermute(value, "replica", [(at, at ^ bit) for at in range(copies)])

    seq_mine, seq_other = at_y(hidden_in[0], hidden_in[1])
    seq_got = swap_y(seq_other)

    small = jnp.concatenate(
        [
            attn_gain.astype(F32)[None],
            ffn_gain.astype(F32)[None],
            segments.astype(F32),
            positions.astype(F32),
        ],
        0,
    )
    small_got = swap_y(small)
    w_query, w_key, w_value = after((w_query, w_key, w_value), seq_other, small)
    kv_rows = jnp.concatenate([w_key, w_value], 1)
    half_send = jnp.where(bit_low == 0, w_query, kv_rows)
    half_got = swap_y(half_send)
    w_query, w_key, w_value, w_gate, w_up = after(
        (w_query, w_key, w_value, w_gate, w_up), half_send
    )
    mine_cols, other_cols = core_columns(w_query, w_key, w_value)
    rows_core = swap_core(other_cols)

    def unit_columns(weight, owner):
        return lax.dynamic_slice(weight, (0, owner * hidden_units), (span, hidden_units))

    target = member ^ (2 + bit_high)
    piece_send = jnp.where(bit_low == 0, unit_columns(w_gate, target), unit_columns(w_up, target))
    pieces = {
        0: lax.ppermute(
            piece_send,
            ("replica", "group"),
            [
                (4 * at + of, 4 * at + (of ^ (2 + (at // 2) % 2)))
                for at in range(copies)
                for of in range(4)
            ],
        )
    }

    small_low, small_high = by_y(small, small_got)
    small_two = jnp.stack([small_low, small_high])
    small_even, small_odd = by_core(small_two, swap_core(small_two))
    small_all = jnp.stack([small_even, small_odd], 1).reshape(4, 6, span)
    small_rows = small_all.transpose(1, 0, 2).reshape(6, 4 * span)
    gain_one = small_rows[0]
    gain_two = small_rows[1]
    seg = jnp.where(on_low_y, small_rows[2], small_rows[3])
    place = jnp.where(on_low_y, small_rows[4], small_rows[5])

    own_low, own_high = by_y(seq_mine, seq_got)
    own_in = jnp.stack([own_low, own_high])
    all_even, all_odd = by_core(own_in, swap_core(own_in))
    all_in = jnp.stack([all_even, all_odd], 1).reshape(4 * span, width)
    normed_all, inv_all = norm_rows(all_in.astype(F32))
    hidden_one = (normed_all * gain_one).astype(BF)
    freq = THETA ** (-(jnp.arange(HALF, dtype=F32) * 2.0 / HD))
    angle = freq[:, None] * place[None, :]
    cosine, sine = jnp.cos(angle), jnp.sin(angle)
    gains = jnp.stack([query_gain, key_gain], 1).astype(F32)
    seg_row = seg[None, :]
    seg_col = seg[:, None]
    unit_core = swap_core(
        jnp.concatenate([unit_columns(w_gate, member ^ 1), unit_columns(w_up, member ^ 1)], 1)
    )

    half_swapped = swap_replica(half_got, 1)
    query_y = jnp.where(bit_low == 0, half_got, half_swapped)
    rest_y = jnp.where(bit_low == 0, half_swapped, half_got)
    mine_y, other_y = core_columns(query_y, rest_y[:, : width // 2], rest_y[:, width // 2 :])
    rows_cross = swap_core(after(other_y, pieces[0]))
    w_attn = in_order(mine_cols, mine_y, rows_core, rows_cross)
    pieces[1] = swap_replica(pieces[0], 1)
    pieces[2] = swap_replica(pieces[0], 2)
    w_out_send, dy_send = after((w_out, out_grad), pieces[0])
    out_got = swap_y(w_out_send)
    dy_got = swap_y(dy_send)

    rot, key_rot, value_low, value_t, head_normed, head_inv = project(
        hidden_one, w_attn, cosine, sine, gains
    )
    pieces[1], pieces[2], out_got, rot = after((pieces[1], pieces[2], out_got, rot), rot)
    pieces[3] = swap_replica(pieces[2], 1)
    rot = after(rot, pieces[1], pieces[2], out_got)
    mixed, log_total, w_mix, mix_mine, mix_other = attention_forward(
        rot, key_rot, value_t, seg_row, seg_col, jnp.stack([y_at, core]), w_out, out_got
    )
    mix_other, pieces[3], dy_got = after((mix_other, pieces[3], dy_got), mixed)
    mix_got = swap_core(mix_other)
    dy_got, mix_got = after((dy_got, mix_got), mix_got)

    inputs = own_in.reshape(2 * span, width)
    middle, hidden_two = by_rows(
        middle_kernel, "middle", [inputs, mix_mine, mix_got], [gain_two[None]], [F32, BF]
    )
    h2_got = swap_y(hidden_two)
    h2_sib = swap_core(hidden_two)
    dy_sib = swap_core(out_grad)
    dy_sib_got = swap_core(dy_got)
    units = hidden_units
    fours = bit_low + 2 * bit_high
    kinds = [fours ^ at for at in range(4)]
    places = [member * span, (member ^ 1) * span]
    places += [(member ^ (2 + kind // 2)) * span for kind in kinds]
    places += [lax.rem(kind, 2) * units for kind in kinds]

    def ffn(seq, h2):
        head = [seq, y_at * span, (1 - y_at) * span, member * units]
        return feed_forward(
            jnp.stack(head + places),
            h2,
            (out_grad, dy_got, dy_sib, dy_sib_got),
            (w_gate, w_up, unit_core, *[pieces[at] for at in range(4)]),
            w_down,
        )

    act_own, act_sib, grad_own, grad_sib, back_own, back_sib, dy_own, dy_sib_own = ffn(
        y_at, (hidden_two, h2_sib)
    )
    sib_got = swap_core(back_sib)
    h2_near = (hidden_two, h2_sib)
    h2_next = after(h2_got, sib_got)
    h2_far = (h2_next, swap_core(h2_next))
    act_next, act_diag, grad_next, grad_diag, back_next, back_diag, dy_next, dy_diag = ffn(
        1 - y_at, h2_far
    )
    dh2_send = (back_next + swap_core(back_diag).astype(F32)).astype(BF)
    dh2_got = swap_y(dh2_send)
    grads = after((grad_own, grad_sib, grad_next, grad_diag), dh2_send)
    ffn_grad = weight_grad((*h2_near, *h2_far), grads)
    down_grad = weight_grad(
        after((act_own, act_sib, act_next, act_diag), ffn_grad),
        (dy_own, dy_sib_own, dy_next, dy_diag),
    )
    ffn_part = lax.psum_scatter(
        ffn_grad.reshape(4, span, 2 * units), "replica", scatter_dimension=1, tiled=True
    )
    dh2_got = after(dh2_got, down_grad)

    def chunk_pair(rows):
        parts = rows.reshape(2, span, width)
        return at_y(parts[0], parts[1])

    grad_middle, grad_branch, ffn_gain_part = by_rows(
        middle_grad_kernel,
        "middle_grad",
        [back_own, sib_got, dh2_got, middle, dy_own],
        [gain_two[None]],
        [F32, BF],
        1,
    )
    grad_branch = grad_branch.reshape(2, span, width)
    branch_even, branch_odd = by_core(grad_branch, swap_core(grad_branch))
    branch_all = jnp.stack([branch_even, branch_odd], 1).reshape(4 * span, width)
    grad_mixed = contract(branch_all, w_mix, 1, 1).astype(BF)
    mix_grad = contract(mixed, branch_all, 0, 0)
    mix_here, mix_there = at_y(mix_grad[:span], mix_grad[span:])
    mix_there = mix_there.astype(BF)
    mix_grad_got = swap_y(mix_there)
    grad_mixed = after(grad_mixed, mix_there)
    head_grads = []
    head_gain_part = 0.0
    rows_here = []
    rows_got = []
    for part in range(2):
        grad_heads, gain_part = attention_backward(
            part,
            grad_mixed,
            rot,
            key_rot,
            value_low,
            head_normed,
            head_inv,
            log_total,
            cosine,
            sine,
            seg_row,
            seg_col,
            gains,
        )
        head_gain_part = head_gain_part + gain_part
        head_grads.append(grad_heads)
        attn_grad = contract(hidden_one, grad_heads, 0, 0).reshape(2, 2 * span, -1)
        here, there = at_y(attn_grad[0], attn_grad[1])
        there = there.astype(BF)
        rows_here.append(here)
        rows_got.append(swap_y(there))
        grad_mixed = after(grad_mixed, there)
    head_grads = jnp.concatenate(after(head_grads, grad_mixed), 1)
    back_one = contract(head_grads, w_attn, 1, 1)
    one_mine, one_other = own_and_other(back_one)
    grad_hidden_one = one_mine + swap_core(one_other.astype(BF)).astype(F32)
    inputs = inputs.astype(F32)
    inv_one, _ = own_and_other(inv_all)
    normed_one = inputs * inv_one
    attn_gain_part = jnp.sum(grad_hidden_one * normed_one, 0)
    grad_input = grad_middle + norm_back(grad_hidden_one * gain_one, normed_one, inv_one)
    input_here, input_there = chunk_pair(grad_input)
    input_back = swap_y(input_there.astype(BF))

    acts = after((act_own, act_sib, act_next, act_diag), back_one)
    out_own, out_sib, out_next, out_diag = [
        jnp.dot(act, w_down, preferred_element_type=F32) for act in acts
    ]
    out_own = middle + out_own + swap_core(out_sib.astype(BF)).astype(F32)
    out_next = out_next + swap_core(out_diag.astype(BF)).astype(F32)

    own_here, own_there = chunk_pair(out_own)
    next_here, next_there = chunk_pair(out_next)
    out_back = swap_y(jnp.stack([own_there, next_there]).astype(BF))
    right, left = Ring(1), Ring(-1)
    rows = span // copies
    indices = jnp.stack(
        [jnp.stack([ring.chunk_at(step) for ring in (right, left)]) for step in range(copies)]
    )
    half = width // 2
    head_sum = jnp.stack(
        [
            *jnp.concatenate(
                [here + got.astype(F32) for here, got in zip(rows_here, rows_got)], 1
            ).reshape(2, span, width),
            mix_here + mix_grad_got.astype(F32),
        ]
    )
    sums_right, sums_left = sum_over_rings((right, left), indices, (down_grad, head_sum))
    down_rows = units // copies

    def all_heads(part):
        owners = part[down_rows : down_rows + 2 * rows].reshape(2, rows, half)
        mine, other = at_core(owners[0], owners[1])
        both = by_core(mine, swap_core(other))
        return jnp.concatenate([part[:down_rows], *both, part[down_rows + 2 * rows :]])

    def own_rows(part):
        parts = part.reshape(2, 2, rows, 2 * units)
        mine, other = at_core(parts[:, 0], parts[:, 1])
        both_cores = jnp.stack(by_core(mine, swap_core(other)), 1)
        here, there = at_y(both_cores[0], both_cores[1])
        all_units = by_y(here, swap_y(there))
        blocks = [block[at] for block in all_units for at in range(2)]
        return [
            jnp.concatenate([block[:, start : start + units] for block in blocks], 1)
            for start in (0, units)
        ]

    w_gate_grad, w_up_grad = gather_over_rings(
        (right, left),
        indices,
        own_rows(ffn_part),
        [w_gate.shape, w_up.shape],
        [(side, side, (0, rows), (0, 4 * units), 0) for side in range(2)],
    )
    targets = []
    for side in range(2):
        targets.append((0, side, (0, down_rows), (0, half), side * half))
        for at in range(2):
            top = down_rows + at * rows
            place_rows = (top, top + rows)
            half_at = side * span + at * span // 2
            targets += [
                (1, side, place_rows, (0, span), side * 2 * span + at * span),
                (2, side, place_rows, (span, span + span // 2), half_at),
                (3, side, place_rows, (span + span // 2, 2 * span), half_at),
            ]
        top = down_rows + 2 * rows
        targets.append((4, side, (top, top + rows), (0, half), side * half))
    w_down_grad, w_query_grad, w_key_grad, w_value_grad, w_out_grad = gather_over_rings(
        (right, left),
        indices,
        [all_heads(sums_right), all_heads(sums_left)],
        [value.shape for value in (w_down, w_query, w_key, w_value, w_out)],
        targets,
    )

    sums = jnp.concatenate([attn_gain_part, ffn_gain_part[0], head_gain_part.T.reshape(-1)])
    sums = after(sums.reshape(-1, 128), sums_right)
    sums = sums + swap_core(sums)
    sums = sums + swap_y(sums)
    step = 1
    while step < copies:
        sums = sums + lax.ppermute(sums, "replica", [(at, at ^ step) for at in range(copies)])
        step *= 2
    sums = sums.reshape(-1)
    attn_gain_grad = lax.dynamic_slice(sums, (member * span,), (span,))
    ffn_gain_grad = lax.dynamic_slice(sums, (width + member * span,), (span,))
    query_gain_grad = sums[2 * width : 2 * width + HD]
    key_gain_grad = sums[2 * width + HD : 2 * width + 2 * HD]

    out_back, input_back = after((out_back, input_back), sums_right)
    out_back, input_back = out_back.astype(F32), input_back.astype(F32)
    input_grad = jnp.stack(by_y(input_here, input_back))
    block_out = jnp.stack(by_y(own_here + out_back[1], next_here + out_back[0])).astype(BF)

    return (
        block_out,
        input_grad,
        attn_gain_grad,
        w_query_grad,
        w_key_grad,
        w_value_grad,
        query_gain_grad,
        key_gain_grad,
        w_out_grad,
        ffn_gain_grad,
        w_gate_grad,
        w_up_grad,
        w_down_grad,
    )


def solution(mesh):
    rows = P("group", None)
    tokens = P("replica", "group", None)
    placed = (
        tokens,
        P("replica", "group"),
        P("replica", "group"),
        tokens,
        P("group"),
        rows,
        rows,
        rows,
        P(),
        P(),
        rows,
        P("group"),
        rows,
        rows,
        rows,
    )
    return jax.shard_map(
        per_device,
        mesh=mesh,
        in_specs=placed,
        out_specs=(
            tokens,
            tokens,
            P("group"),
            rows,
            rows,
            rows,
            P(),
            P(),
            rows,
            P("group"),
            rows,
            rows,
            rows,
        ),
        check_vma=False,
    )
```

```python
import functools

import jax
import jax.numpy as jnp
from jax import lax
from jax.experimental import pallas as pl
from jax.experimental.pallas import tpu as pltpu
from jax.sharding import PartitionSpec as P

HEADS = 8
PAIRS = 4
HD = 64
HALF = 32
SPAN = 256
LANES = 128

EPS = 1e-05
THETA = 1000000.0
NEG = -1e30

BF = jnp.bfloat16
F32 = jnp.float32
NO_COST = pl.CostEstimate(flops=0, bytes_accessed=0, transcendentals=0)

Y_SWAP = [(0, 2), (2, 0), (1, 3), (3, 1)]
CORE_SWAP = [(0, 1), (1, 0), (2, 3), (3, 2)]
CROSS_SWAP = [(0, 3), (3, 0), (1, 2), (2, 1)]


def contract(left, right, left_dim, right_dim):
    return lax.dot_general(
        left, right, (((left_dim,), (right_dim,)), ((), ())), preferred_element_type=F32
    )


def visible_block(seg_col, seg_row, block):
    end = (block + 1) * SPAN
    key_at = lax.broadcasted_iota(jnp.int32, (end, SPAN), 0)
    query_at = lax.broadcasted_iota(jnp.int32, (end, SPAN), 1) + block * SPAN
    return (seg_col[0:end, :] == seg_row[:, block * SPAN : end]) & (key_at <= query_at)


def project_kernel(
    hidden_ref,
    weight_ref,
    cos_ref,
    sin_ref,
    gain_ref,
    rot_ref,
    key_ref,
    value_ref,
    value_t_ref,
    normed_ref,
    inv_ref,
):
    blocks = hidden_ref.shape[0] // SPAN
    heads = HEADS + PAIRS
    for block in range(blocks):
        span = slice(block * SPAN, (block + 1) * SPAN)
        raw = jnp.dot(hidden_ref[span, :], weight_ref[...], preferred_element_type=F32)
        raw_t = raw.T
        for half in range(2):
            cols = slice(half * 2 * SPAN + 3 * LANES, (half + 1) * 2 * SPAN)
            place = slice(half * LANES, (half + 1) * LANES)
            value_ref[span, place] = raw[:, cols].astype(BF)
            value_t_ref[place, span] = raw_t[cols, :].astype(BF)
        cosine = cos_ref[:, span]
        sine = sin_ref[:, span]
        for head in range(heads):
            rows = slice(head * HD, (head + 1) * HD)
            if head < HEADS:
                at = head // 4 * 2 * SPAN + head % 4 * HD
            else:
                at = (head - HEADS) // 2 * 2 * SPAN + SPAN + head % 2 * HD
            part = raw_t[at : at + HD, :]
            inv = lax.rsqrt(jnp.mean(part * part, 0, keepdims=True) + EPS)
            normed = part * inv
            normed_ref[rows, span] = normed
            inv_ref[head : head + 1, span] = inv
            kind = 0 if head < HEADS else 1
            scaled = normed * gain_ref[:, kind : kind + 1]
            first = scaled[:HALF, :]
            second = scaled[HALF:, :]
            turned = jnp.concatenate(
                [first * cosine - second * sine, second * cosine + first * sine], 0
            )
            if head < HEADS:
                rot_ref[rows, span] = turned.astype(BF) * BF(HD**-0.5)
            else:
                rot_ref[rows, span] = turned.astype(BF)
    for pair in range(PAIRS):
        rows = slice((HEADS + pair) * HD, (HEADS + pair + 1) * HD)
        key_ref[pair] = rot_ref[rows, :].astype(F32).T.astype(BF)


def forward_kernel(
    rot_ref,
    key_ref,
    value_t_ref,
    seg_row_ref,
    seg_col_ref,
    at_ref,
    w_own_ref,
    w_got_ref,
    mixed_ref,
    log_ref,
    w_mix_ref,
    mine_ref,
    other_ref,
    mixed_t,
):
    w_mix_ref[pl.ds(pl.multiple_of(at_ref[0] * SPAN, SPAN), SPAN), :] = w_own_ref[...]
    w_mix_ref[pl.ds(pl.multiple_of((1 - at_ref[0]) * SPAN, SPAN), SPAN), :] = w_got_ref[...]
    for block in range(mixed_ref.shape[0] // SPAN):
        end = (block + 1) * SPAN
        span = slice(block * SPAN, end)
        visible = visible_block(seg_col_ref[...], seg_row_ref[...], block)

        def one_head(head, carry, end=end, span=span, visible=visible):
            pair = head // 2
            rows = pl.ds(pl.multiple_of(head * HD, HD), HD)
            score = jnp.dot(
                key_ref[pair, 0:end, :], rot_ref[rows, span], preferred_element_type=F32
            )
            score = jnp.where(visible, score, NEG)
            top = jnp.max(score, 0, keepdims=True)
            weight = jnp.exp(score - top)
            total = jnp.sum(weight, 0, keepdims=True)
            log_ref[pl.ds(head, 1), span] = top + jnp.log(total)
            prob = (weight * (1.0 / total)).astype(BF)
            values_t = value_t_ref[pl.ds(pl.multiple_of(pair * HD, HD), HD), 0:end]
            mixed_t[rows, :] = jnp.dot(values_t, prob, preferred_element_type=F32)
            return carry

        lax.fori_loop(0, HEADS, one_head, 0)
        for pair in range(PAIRS):
            cols = slice(pair * 2 * HD, (pair + 1) * 2 * HD)
            mixed_ref[span, cols] = mixed_t[cols, :].T.astype(BF)
    core = at_ref[1]
    for part in range(2):
        span = slice(part * SPAN, (part + 1) * SPAN)
        for where, out in ((core, mine_ref), (1 - core, other_ref)):
            rows = pl.ds(pl.multiple_of((2 * part + where) * SPAN, SPAN), SPAN)
            out[span, :] = jnp.dot(
                mixed_ref[rows, :], w_mix_ref[...], preferred_element_type=F32
            ).astype(out.dtype)


def backward_kernel(
    half,
    grad_ref,
    query_ref,
    key_t_ref,
    key_ref,
    value_ref,
    query_normed_ref,
    key_normed_ref,
    inv_ref,
    log_ref,
    cos_ref,
    sin_ref,
    seg_row_ref,
    seg_col_ref,
    gain_ref,
    out_ref,
    gain_grad_ref,
    grad_t,
    head_grad,
    value_one,
    key_sum,
    value_sum,
    out_t,
):
    length = grad_ref.shape[0]
    heads = HEADS // 2
    pairs = PAIRS // 2
    for part in range(pairs):
        cols = slice(part * 2 * HD, (part + 1) * 2 * HD)
        grad_t[cols, :] = grad_ref[:, cols].astype(F32).T.astype(BF)
    values_t = value_ref[...].astype(F32).T
    for pair in range(pairs):
        value_one[pair] = values_t[pair * HD : (pair + 1) * HD, :].T.astype(BF)
    left_lane = lax.broadcasted_iota(jnp.int32, (SPAN, 2 * HD), 1) < HD
    zero = jnp.zeros((SPAN, 2 * HD), BF)

    def one_pair(pair, carry):
        key_sum[...] = jnp.zeros_like(key_sum)
        value_sum[...] = jnp.zeros_like(value_sum)
        keys_t = key_t_ref[pl.ds(pl.multiple_of(pair * HD, HD), HD), :]
        both = pl.ds(pl.multiple_of(pair * 2 * HD, 2 * HD), 2 * HD)
        for block in range(length // SPAN):
            end = (block + 1) * SPAN
            span = slice(block * SPAN, end)
            visible = visible_block(seg_col_ref[...], seg_row_ref[...], block)
            queries = query_ref[both, span].astype(F32).T.astype(BF)
            grads = grad_ref[span, both]
            for side in range(2):
                head = pair * 2 + side
                rows = pl.ds(pl.multiple_of(head * HD, HD), HD)
                score = jnp.dot(
                    key_ref[pair, 0:end, :], query_ref[rows, span], preferred_element_type=F32
                )
                logs = log_ref[pl.ds(half * heads + head, 1), span]
                prob = jnp.where(visible, jnp.exp(score - logs), 0.0)
                grad_prob = jnp.dot(
                    value_one[pair, 0:end, :], grad_t[rows, span], preferred_element_type=F32
                )
                inner = jnp.sum(prob * grad_prob, 0, keepdims=True)
                grad_score = (prob * (grad_prob - inner)).astype(BF)
                mine = left_lane if side == 0 else jnp.logical_not(left_lane)
                value_sum[0:end, :] += jnp.dot(
                    prob.astype(BF), jnp.where(mine, grads, zero), preferred_element_type=F32
                )
                key_sum[0:end, :] += jnp.dot(
                    grad_score, jnp.where(mine, queries, zero), preferred_element_type=F32
                )
                head_grad[rows, span] = jnp.dot(
                    keys_t[:, 0:end], grad_score, preferred_element_type=F32
                ) * (HD**-0.5)
        key_t = key_sum[...].T
        value_t = value_sum[...].T
        key_rows = pl.ds(pl.multiple_of((heads + pair) * HD, HD), HD)
        head_grad[key_rows, :] = key_t[:HD, :] + key_t[HD:, :]
        value_rows = pl.ds(pl.multiple_of((heads + pairs + pair) * HD, HD), HD)
        out_t[value_rows, :] = value_t[:HD, :] + value_t[HD:, :]
        return carry

    lax.fori_loop(0, pairs, one_pair, 0)

    cosine = cos_ref[...]
    sine = sin_ref[...]
    gain_sums = [jnp.zeros((HD, length), F32), jnp.zeros((HD, length), F32)]
    for head in range(heads + pairs):
        rows = slice(head * HD, (head + 1) * HD)
        kind = 0 if head < heads else 1
        part = head_grad[rows, :]
        first = part[:HALF, :]
        second = part[HALF:, :]
        turned = jnp.concatenate(
            [first * cosine + second * sine, second * cosine - first * sine], 0
        )
        if kind == 0:
            normed = query_normed_ref[rows, :]
            line = half * heads + head
        else:
            normed = key_normed_ref[(head - heads) * HD : (head - heads + 1) * HD, :]
            line = HEADS + half * pairs + head - heads
        gain_sums[kind] = gain_sums[kind] + turned * normed
        scaled = turned * gain_ref[:, kind : kind + 1]
        mean = jnp.mean(scaled * normed, 0, keepdims=True)
        out_t[rows, :] = inv_ref[line : line + 1, :] * (scaled - normed * mean)
    for kind in range(2):
        gain_grad_ref[:, kind : kind + 1] = jnp.sum(gain_sums[kind], 1, keepdims=True)
    for part in range(out_t.shape[0] // (2 * HD)):
        cols = slice(part * 2 * HD, (part + 1) * 2 * HD)
        out_ref[:, cols] = out_t[cols, :].T.astype(BF)


def in_hbm(shape, kind):
    return pltpu.HBM(shape, kind)


def from_hbm(*operands):
    return [
        pltpu.with_memory_space_constraint(value, pltpu.HBM) if value.size >= 2**16 else value
        for value in operands
    ]


def whole_refs(count):
    return [pl.BlockSpec(memory_space=pltpu.VMEM)] * count


def project(hidden, weight, cosine, sine, gains):
    length = hidden.shape[0]
    rows = (HEADS + PAIRS) * HD
    outs = [
        ((rows, length), BF),
        ((PAIRS, length, HD), BF),
        ((length, PAIRS * HD), BF),
        ((PAIRS * HD, length), BF),
        ((rows, length), F32),
        ((16, length), F32),
    ]
    return pl.pallas_call(
        project_kernel,
        out_shape=[in_hbm(shape, kind) for shape, kind in outs],
        in_specs=whole_refs(5),
        out_specs=whole_refs(len(outs)),
        compiler_params=pltpu.CompilerParams(vmem_limit_bytes=24 * 1024 * 1024),
        cost_estimate=NO_COST,
        name="project",
    )(*from_hbm(hidden, weight), cosine, sine, gains)


def attention_forward(rot, key, value_t, seg_row, seg_col, at, w_own, w_got):
    length = rot.shape[1]
    width = w_own.shape[1]
    outs = [
        ((length, HEADS * HD), BF),
        ((HEADS, length), F32),
        ((HEADS * HD, width), BF),
        ((length // 2, width), F32),
        ((length // 2, width), BF),
    ]
    return pl.pallas_call(
        forward_kernel,
        out_shape=[in_hbm(shape, kind) for shape, kind in outs],
        in_specs=whole_refs(5) + [pl.BlockSpec(memory_space=pltpu.SMEM)] + whole_refs(2),
        out_specs=whole_refs(len(outs)),
        scratch_shapes=[pltpu.VMEM((HEADS * HD, SPAN), F32)],
        compiler_params=pltpu.CompilerParams(vmem_limit_bytes=24 * 1024 * 1024),
        cost_estimate=NO_COST,
        name="attention_forward",
    )(*from_hbm(rot, key, value_t), seg_row, seg_col, at, *from_hbm(w_own, w_got))


def middle_kernel(inputs_ref, mine_ref, got_ref, gain_ref, middle_ref, hidden_ref):
    middle = inputs_ref[...].astype(F32) + mine_ref[...] + got_ref[...].astype(F32)
    middle_ref[...] = middle
    normed, _ = norm_rows(middle)
    hidden_ref[...] = (normed * gain_ref[...]).astype(BF)


def by_rows(kernel, name, rows_in, whole_in, rows_out, sums_out=0):
    rows, width = rows_in[0].shape
    tile = 2 * LANES
    block = pl.BlockSpec((tile, width), lambda at: (at, 0))
    line = pl.BlockSpec((1, width), lambda at: (0, 0))
    return pl.pallas_call(
        kernel,
        grid=(rows // tile,),
        out_shape=[in_hbm((rows, width), kind) for kind in rows_out]
        + [jax.ShapeDtypeStruct((1, width), F32)] * sums_out,
        in_specs=[block] * len(rows_in) + [line] * len(whole_in),
        out_specs=[block] * len(rows_out) + [line] * sums_out,
        compiler_params=pltpu.CompilerParams(vmem_limit_bytes=16 * 1024 * 1024),
        cost_estimate=NO_COST,
        name=name,
    )(*[from_hbm(value)[0] if value.dtype == F32 else value for value in rows_in], *whole_in)


def middle_grad_kernel(
    own_ref, sib_ref, got_ref, middle_ref, dy_ref, gain_ref, grad_ref, branch_ref, gain_grad_ref
):
    dh2 = own_ref[...] + sib_ref[...].astype(F32) + got_ref[...].astype(F32)
    normed, inv = norm_rows(middle_ref[...])

    @pl.when(pl.program_id(0) == 0)
    def _():
        gain_grad_ref[...] = jnp.zeros_like(gain_grad_ref)

    gain_grad_ref[...] += jnp.sum(dh2 * normed, 0, keepdims=True)
    grad = dy_ref[...].astype(F32) + norm_back(dh2 * gain_ref[...], normed, inv)
    grad_ref[...] = grad
    branch_ref[...] = grad.astype(BF)


def attention_backward(half, grad, rot, key, value, normed, inv, log, cosine, sine, seg_row, seg_col, gains):
    length = grad.shape[0]
    queries = HEADS * HD // 2
    keys = PAIRS * HD // 2
    width = queries + 2 * keys

    def rows_of(count, at):
        return pl.BlockSpec((count, length), lambda step: (at, 0))

    def columns_of(count):
        return pl.BlockSpec((length, count), lambda step: (0, half))

    key_at = 2 * queries // keys + half
    return pl.pallas_call(
        functools.partial(backward_kernel, half),
        grid=(1,),
        out_shape=[
            in_hbm((length, width), BF),
            jax.ShapeDtypeStruct((HD, 2), F32),
        ],
        in_specs=[
            columns_of(queries),
            rows_of(queries, half),
            rows_of(keys, key_at),
            pl.BlockSpec((PAIRS // 2, length, HD), lambda step: (half, 0, 0)),
            columns_of(keys),
            rows_of(queries, half),
            rows_of(keys, key_at),
        ]
        + whole_refs(7),
        out_specs=whole_refs(2),
        scratch_shapes=[
            pltpu.VMEM((queries, length), BF),
            pltpu.VMEM((queries + keys, length), F32),
            pltpu.VMEM((PAIRS // 2, length, HD), BF),
            pltpu.VMEM((length, 2 * HD), F32),
            pltpu.VMEM((length, 2 * HD), F32),
            pltpu.VMEM((width, length), F32),
        ],
        compiler_params=pltpu.CompilerParams(vmem_limit_bytes=28 * 1024 * 1024),
        cost_estimate=NO_COST,
        name="attention_backward",
    )(
        *from_hbm(grad, rot, rot, key, value, normed, normed),
        inv,
        log,
        cosine,
        sine,
        seg_row,
        seg_col,
        gains,
    )


def feed_forward_kernel(
    at_ref,
    h2_a,
    h2_b,
    dy_a,
    dy_a_got,
    dy_b,
    dy_b_got,
    w_gate,
    w_up,
    w_sib,
    piece_0,
    piece_1,
    piece_2,
    piece_3,
    w_down,
    act_a,
    act_b,
    grad_a,
    grad_b,
    back_a,
    back_b,
    dy_out_a,
    dy_out_b,
    h2_v,
    dy_v,
    in_v,
    down_v,
    act_v,
    grad_v,
    back_own,
    back_sib,
    grad_act,
    load_sems,
    store_sems,
):
    units = down_v.shape[0]

    def rows_at(index):
        return pl.ds(pl.multiple_of(at_ref[index], SPAN), SPAN)

    def units_at(index):
        return pl.ds(pl.multiple_of(at_ref[index], LANES), units)

    loads = []

    def load(source, target):
        loads.append(pltpu.make_async_copy(source, target, load_sems.at[len(loads)]))
        loads[-1].start()

    def load_dy(part, own, got):
        load(own.at[at_ref[0]], dy_v.at[part, rows_at(1)])
        load(got.at[at_ref[0]], dy_v.at[part, rows_at(2)])

    load_dy(0, dy_a, dy_a_got)
    load(w_down, down_v)
    load(h2_a, h2_v.at[0])
    load(w_gate.at[:, units_at(3)], in_v.at[rows_at(4), 0:units])
    load(w_up.at[:, units_at(3)], in_v.at[rows_at(4), units : 2 * units])
    load(w_sib, in_v.at[rows_at(5)])
    for at, piece in enumerate((piece_0, piece_1, piece_2, piece_3)):
        load(piece, in_v.at[rows_at(6 + at), units_at(10 + at)])
    weights_end = len(loads)
    load_dy(1, dy_b, dy_b_got)
    load(h2_b, h2_v.at[1])
    stores = []
    for part in range(2):
        for at in range(3) if part == 0 else range(weights_end, weights_end + 2):
            loads[at].wait()
        for start in range(0, units, 256):
            end = min(start + 256, units)
            grad_act[:, start:end] = contract(dy_v[part], down_v[start:end, :], 1, 1)
        for at in range(3, weights_end) if part == 0 else [weights_end + 2]:
            loads[at].wait()
        for start in range(0, units, LANES):
            gate_cols = slice(start, start + LANES)
            up_cols = slice(units + start, units + start + LANES)
            weight = jnp.concatenate([in_v[:, gate_cols], in_v[:, up_cols]], 1)
            both = jnp.dot(h2_v[part], weight, preferred_element_type=F32)
            gate, up = both[:, :LANES], both[:, LANES:]
            sig = jax.nn.sigmoid(gate)
            silu = gate * sig
            grad = grad_act[:, gate_cols]
            act_v[part, :, gate_cols] = (silu * up).astype(BF)
            grad_gate = grad * up * sig * (1.0 + gate * (1.0 - sig))
            grad_v[part, :, gate_cols] = grad_gate.astype(BF)
            grad_v[part, :, up_cols] = (grad * silu).astype(BF)
        back = contract(grad_v[part], in_v[...], 1, 1)
        if part == 0:
            back_own[...] = back
        else:
            back_sib[...] = back.astype(BF)
        for at, (source, target) in enumerate(
            [
                (act_v.at[part], (act_a, act_b)[part]),
                (grad_v.at[part], (grad_a, grad_b)[part]),
                ((back_own, back_sib)[part], (back_a, back_b)[part]),
                (dy_v.at[part], (dy_out_a, dy_out_b)[part]),
            ]
        ):
            stores.append(pltpu.make_async_copy(source, target, store_sems.at[part * 4 + at]))
            stores[-1].start()
    for store in stores:
        store.wait()


def feed_forward(at, h2, dy, weights, w_down):
    rows, width = h2[0].shape
    units = w_down.shape[0]
    outs = (
        [((rows, units), BF)] * 2
        + [((rows, 2 * units), BF)] * 2
        + [((rows, width), F32), ((rows, width), BF)]
        + [((rows, width), BF)] * 2
    )
    operands = from_hbm(*h2, *dy, *weights, w_down)
    return pl.pallas_call(
        feed_forward_kernel,
        out_shape=[in_hbm(shape, kind) for shape, kind in outs],
        in_specs=[pl.BlockSpec(memory_space=pltpu.SMEM)]
        + [pl.BlockSpec(memory_space=pl.ANY)] * len(operands),
        out_specs=[pl.BlockSpec(memory_space=pl.ANY)] * len(outs),
        scratch_shapes=[
            pltpu.VMEM((2, rows, width), BF),
            pltpu.VMEM((2, rows, width), BF),
            pltpu.VMEM((width, 2 * units), BF),
            pltpu.VMEM(w_down.shape, BF),
            pltpu.VMEM((2, rows, units), BF),
            pltpu.VMEM((2, rows, 2 * units), BF),
            pltpu.VMEM((rows, width), F32),
            pltpu.VMEM((rows, width), BF),
            pltpu.VMEM((rows, units), F32),
            pltpu.SemaphoreType.DMA((14,)),
            pltpu.SemaphoreType.DMA((8,)),
        ],
        compiler_params=pltpu.CompilerParams(vmem_limit_bytes=36 * 1024 * 1024),
        cost_estimate=NO_COST,
        name="feed_forward",
    )(at, *operands)


def weight_grad_kernel(count, *refs):
    left, right = refs[:count], refs[count : 2 * count]
    out, left_t = refs[-2:]

    @pl.when(pl.program_id(0) == 0)
    def _():
        for at in range(count):
            left_t[at] = left[at][...].T

    total = jnp.dot(left_t[0], right[0][...], preferred_element_type=F32)
    for at in range(1, count):
        total += jnp.dot(left_t[at], right[at][...], preferred_element_type=F32)
    out[...] = total.astype(BF)


def weight_grad(left, right):
    rows, height = left[0].shape
    width = right[0].shape[1]
    count = len(left)
    step = SPAN
    return pl.pallas_call(
        functools.partial(weight_grad_kernel, count),
        grid=(width // step,),
        out_shape=in_hbm((height, width), BF),
        in_specs=[pl.BlockSpec((rows, height), lambda at: (0, 0))] * count
        + [pl.BlockSpec((rows, step), lambda at: (0, at))] * count,
        out_specs=pl.BlockSpec((height, step), lambda at: (0, at)),
        scratch_shapes=[pltpu.VMEM((count, height, rows), BF)],
        compiler_params=pltpu.CompilerParams(vmem_limit_bytes=24 * 1024 * 1024),
        cost_estimate=NO_COST,
        name="weight_grad",
    )(*from_hbm(*left, *right))


def norm_rows(inputs):
    inv = lax.rsqrt(jnp.mean(inputs * inputs, -1, keepdims=True) + EPS)
    return (inputs * inv, inv)


def norm_back(grad, normed, inv):
    return inv * (grad - normed * jnp.mean(grad * normed, -1, keepdims=True))


def swap_y(value):
    return lax.ppermute(value, "group", Y_SWAP)


def swap_cross(value):
    return lax.ppermute(value, "group", CROSS_SWAP)


def swap_core(value):
    return lax.ppermute(value, "group", CORE_SWAP)


def after(value, *earlier):
    return lax.optimization_barrier((value, earlier))[0]


def cycle_of(count):
    return list(range(0, count, 2)) + list(range(count - 1, 0, -2))


class Ring:
    def __init__(self, way):
        count = lax.axis_size("replica")
        cycle = cycle_of(count)[::way]
        self.count = count
        self.way = way
        self.hops = [(cycle[at], cycle[(at + 1) % count]) for at in range(count)]
        mine = lax.axis_index("replica")
        self.place = jnp.where(lax.rem(mine, 2) == 0, mine // 2, count - 1 - mine // 2)

    def chunk_at(self, back):
        at = lax.rem(self.place - self.way * back + self.count, self.count)
        return jnp.where(at < self.count // 2, 2 * at, 2 * (self.count - 1 - at) + 1)

    def send(self, value):
        return lax.ppermute(value, "replica", self.hops)


def pick_kernel(step, count, index_ref, *refs):
    sources = refs[:count]
    outs, shares, sems = refs[-count - 3 : -count - 1], refs[-count - 1 : -1], refs[-1]
    arrived = refs[count : -count - 3]
    copies = []
    for side in range(2):
        for at, (source, share) in enumerate(zip(sources, shares)):
            _, _, rows, half = share.shape
            row = pl.multiple_of(index_ref[step, side] * rows, 8)
            copies.append(
                pltpu.make_async_copy(
                    source.at[:, pl.ds(row, rows), side * half : (side + 1) * half],
                    share.at[side],
                    sems.at[side, at],
                )
            )
    for copy in copies:
        copy.start()
    for copy in copies:
        copy.wait()
    for side in range(2):
        start = 0
        for share in shares:
            _, kinds, rows, _ = share.shape
            for kind in range(kinds):
                span = slice(start, start + rows)
                part = share[side, kind].astype(F32)
                if arrived:
                    part = part + arrived[side][span, :].astype(F32)
                outs[side][span, :] = part.astype(BF)
                start += rows


def pick_chunks(step, indices, sources, arrived):
    copies = indices.shape[0]
    rows = [source.shape[1] // copies for source in sources]
    half = sources[0].shape[2] // 2
    if any(count % 16 for count in rows):
        moving = []
        for side in range(2):
            parts = [
                lax.dynamic_slice(
                    source,
                    (0, indices[step, side] * count, side * half),
                    (source.shape[0], count, half),
                ).reshape(-1, half)
                for source, count in zip(sources, rows)
            ]
            part = jnp.concatenate([part.astype(F32) for part in parts])
            if arrived:
                part = part + arrived[side].astype(F32)
            moving.append(part.astype(BF))
        return moving
    total = sum(source.shape[0] * count for source, count in zip(sources, rows))
    return pl.pallas_call(
        functools.partial(pick_kernel, step, len(sources)),
        out_shape=[jax.ShapeDtypeStruct((total, half), BF)] * 2,
        in_specs=[pl.BlockSpec(memory_space=pltpu.SMEM)]
        + [pl.BlockSpec(memory_space=pl.ANY)] * len(sources)
        + whole_refs(len(arrived)),
        out_specs=whole_refs(2),
        scratch_shapes=[
            pltpu.VMEM((2, source.shape[0], count, half), source.dtype)
            for source, count in zip(sources, rows)
        ]
        + [pltpu.SemaphoreType.DMA((2, len(sources)))],
        compiler_params=pltpu.CompilerParams(vmem_limit_bytes=8 * 1024 * 1024),
        cost_estimate=NO_COST,
        name="pick_chunks",
    )(indices, *from_hbm(*sources), *arrived)


class RingSum:
    def __init__(self, rings, indices, sources):
        self.rings, self.indices, self.sources = rings, indices, sources
        self.moving = pick_chunks(1, indices, sources, [])
        self.step = 1

    def advance(self, *earlier):
        count = self.rings[0].count
        if self.step == count:
            return
        self.step += 1
        arrived = [ring.send(chunk) for ring, chunk in zip(self.rings, self.moving)]
        arrived = after(arrived, *earlier)
        self.moving = pick_chunks(self.step % count, self.indices, self.sources, arrived)

    def finish(self):
        while self.step < self.rings[0].count:
            self.advance()
        return self.moving


def place_kernel(step, targets, stores, index_ref, *refs):
    chunks = refs[:2]
    outs = refs[-3 - stores : -3]
    wide = refs[-3:-1]
    sems = refs[-1]
    for side in range(2):
        wide[side][...] = chunks[side][...].astype(F32)
    copies = []
    for at, (store, side, (top, bottom), (start, end), column) in enumerate(targets):
        rows = bottom - top
        row = pl.multiple_of(index_ref[step, side] * rows, 8)
        copies.append(
            pltpu.make_async_copy(
                wide[side].at[top:bottom, start:end],
                outs[store].at[pl.ds(row, rows), column : column + end - start],
                sems.at[at],
            )
        )
    for copy in copies:
        copy.start()
    for copy in copies:
        copy.wait()


def place_chunks(step, indices, chunks, stores, shapes, targets):
    if any((bottom - top) % 8 for _, _, (top, bottom), _, _ in targets):
        stores = stores or [jnp.zeros(shape, F32) for shape in shapes]
        for store, side, (top, bottom), (start, end), column in targets:
            stores[store] = lax.dynamic_update_slice(
                stores[store],
                chunks[side][top:bottom, start:end].astype(F32),
                (indices[step, side] * (bottom - top), column),
            )
        return stores
    given = stores or []
    return list(
        pl.pallas_call(
            functools.partial(place_kernel, step, targets, len(shapes)),
            out_shape=[in_hbm(shape, F32) for shape in shapes],
            in_specs=[pl.BlockSpec(memory_space=pltpu.SMEM)]
            + [pl.BlockSpec(memory_space=pltpu.VMEM)] * 2
            + [pl.BlockSpec(memory_space=pl.ANY)] * len(given),
            out_specs=[pl.BlockSpec(memory_space=pl.ANY)] * len(shapes),
            scratch_shapes=[pltpu.VMEM(chunk.shape, F32) for chunk in chunks]
            + [pltpu.SemaphoreType.DMA((len(targets),))],
            input_output_aliases={3 + at: at for at in range(len(given))},
            compiler_params=pltpu.CompilerParams(vmem_limit_bytes=8 * 1024 * 1024),
            cost_estimate=NO_COST,
            name="place_chunks",
        )(indices, *chunks, *from_hbm(*given))
    )


class RingGather:
    def __init__(self, rings, indices, chunks, shapes, targets):
        self.rings, self.indices, self.chunks = rings, indices, chunks
        self.shapes, self.targets = shapes, targets
        self.stores = place_chunks(0, indices, chunks, None, shapes, targets)
        self.earlier = []
        self.step = 0

    def advance(self, steps):
        while steps and self.step + 1 < self.rings[0].count:
            steps -= 1
            self.step += 1
            held = after(self.chunks, *self.earlier)
            self.chunks = [ring.send(chunk) for ring, chunk in zip(self.rings, held)]
            self.earlier = self.stores
            self.stores = place_chunks(
                self.step, self.indices, self.chunks, self.stores, self.shapes, self.targets
            )
        return self.stores


def per_device(
    hidden_in,
    segments,
    positions,
    out_grad,
    attn_gain,
    w_query,
    w_key,
    w_value,
    query_gain,
    key_gain,
    w_out,
    ffn_gain,
    w_gate,
    w_up,
    w_down,
):
    copies = lax.axis_size("replica")
    member = lax.axis_index("group")
    y_at = member // 2
    core = lax.rem(member, 2)
    on_low_y = y_at == 0
    on_low_core = core == 0
    span, width = hidden_in.shape[1:]
    hidden_units = w_down.shape[0]

    def by_y(mine, other):
        return jnp.where(on_low_y, mine, other), jnp.where(on_low_y, other, mine)

    def by_core(mine, other):
        return jnp.where(on_low_core, mine, other), jnp.where(on_low_core, other, mine)

    def at_y(pair_low, pair_high):
        return jnp.where(on_low_y, pair_low, pair_high), jnp.where(on_low_y, pair_high, pair_low)

    def at_core(low, high):
        return jnp.where(on_low_core, low, high), jnp.where(on_low_core, high, low)

    def quarters(weight):
        size = weight.shape[1] // 4
        return [weight[:, at * size : (at + 1) * size] for at in range(4)]

    def core_columns(*weights):
        parts = [quarters(weight) for weight in weights]
        low = [part[0] for part in parts] + [part[2] for part in parts]
        high = [part[1] for part in parts] + [part[3] for part in parts]
        return at_core(jnp.concatenate(low, 1), jnp.concatenate(high, 1))

    def own_and_other(rows):
        parts = rows.reshape(2, 2, span, rows.shape[-1])
        mine, other = at_core(parts[:, 0], parts[:, 1])
        return mine.reshape(2 * span, -1), other.reshape(2 * span, -1)

    def in_order(mine, at_y, sibling, across):
        here = jnp.concatenate(by_core(mine, sibling), 0)
        there = jnp.concatenate(by_core(at_y, across), 0)
        return jnp.concatenate(by_y(here, there), 0)

    replica = lax.axis_index("replica")
    bit_low = lax.rem(replica, 2)
    bit_high = lax.rem(replica // 2, 2)

    def swap_replica(value, bit):
        return lax.ppermute(value, "replica", [(at, at ^ bit) for at in range(copies)])

    seq_mine, seq_other = at_y(hidden_in[0], hidden_in[1])
    seq_got = swap_y(seq_other)

    small = jnp.concatenate(
        [
            attn_gain.astype(F32)[None],
            ffn_gain.astype(F32)[None],
            segments.astype(F32),
            positions.astype(F32),
        ],
        0,
    )
    small_got = swap_y(small)
    w_query, w_key, w_value = after((w_query, w_key, w_value), seq_other, small)
    kv_rows = jnp.concatenate([w_key, w_value], 1)
    half_send = jnp.where(bit_low == 0, w_query, kv_rows)
    half_got = swap_y(half_send)
    w_query, w_key, w_value, w_gate, w_up = after(
        (w_query, w_key, w_value, w_gate, w_up), half_send
    )
    mine_cols, other_cols = core_columns(w_query, w_key, w_value)
    rows_core = swap_core(other_cols)

    def unit_columns(weight, owner):
        return lax.dynamic_slice(weight, (0, owner * hidden_units), (span, hidden_units))

    target = member ^ (2 + bit_high)
    piece_send = jnp.where(bit_low == 0, unit_columns(w_gate, target), unit_columns(w_up, target))
    pieces = {
        0: lax.ppermute(
            piece_send,
            ("replica", "group"),
            [
                (4 * at + of, 4 * at + (of ^ (2 + (at // 2) % 2)))
                for at in range(copies)
                for of in range(4)
            ],
        )
    }

    small_low, small_high = by_y(small, small_got)
    small_two = jnp.stack([small_low, small_high])
    small_even, small_odd = by_core(small_two, swap_core(small_two))
    small_all = jnp.stack([small_even, small_odd], 1).reshape(4, 6, span)
    small_rows = small_all.transpose(1, 0, 2).reshape(6, 4 * span)
    gain_one = small_rows[0]
    gain_two = small_rows[1]
    seg = jnp.where(on_low_y, small_rows[2], small_rows[3])
    place = jnp.where(on_low_y, small_rows[4], small_rows[5])

    own_low, own_high = by_y(seq_mine, seq_got)
    own_in = jnp.stack([own_low, own_high])
    all_even, all_odd = by_core(own_in, swap_core(own_in))
    all_in = jnp.stack([all_even, all_odd], 1).reshape(4 * span, width)
    normed_all, inv_all = norm_rows(all_in.astype(F32))
    hidden_one = (normed_all * gain_one).astype(BF)
    freq = THETA ** (-(jnp.arange(HALF, dtype=F32) * 2.0 / HD))
    angle = freq[:, None] * place[None, :]
    cosine, sine = jnp.cos(angle), jnp.sin(angle)
    gains = jnp.stack([query_gain, key_gain], 1).astype(F32)
    seg_row = seg[None, :]
    seg_col = seg[:, None]
    unit_core = swap_core(
        jnp.concatenate([unit_columns(w_gate, member ^ 1), unit_columns(w_up, member ^ 1)], 1)
    )

    half_swapped = swap_replica(half_got, 1)
    query_y = jnp.where(bit_low == 0, half_got, half_swapped)
    rest_y = jnp.where(bit_low == 0, half_swapped, half_got)
    mine_y, other_y = core_columns(query_y, rest_y[:, : width // 2], rest_y[:, width // 2 :])
    rows_cross = swap_core(after(other_y, pieces[0]))
    w_attn = in_order(mine_cols, mine_y, rows_core, rows_cross)
    pieces[1] = swap_replica(pieces[0], 1)
    pieces[2] = swap_replica(pieces[0], 2)
    w_out_send, dy_send = after((w_out, out_grad), pieces[0])
    out_got = swap_y(w_out_send)
    dy_got = swap_y(dy_send)

    rot, key_rot, value_low, value_t, head_normed, head_inv = project(
        hidden_one, w_attn, cosine, sine, gains
    )
    pieces[1], pieces[2], out_got, rot = after((pieces[1], pieces[2], out_got, rot), rot)
    pieces[3] = swap_replica(pieces[2], 1)
    rot = after(rot, pieces[1], pieces[2], out_got)
    mixed, log_total, w_mix, mix_mine, mix_other = attention_forward(
        rot, key_rot, value_t, seg_row, seg_col, jnp.stack([y_at, core]), w_out, out_got
    )
    mix_other, pieces[3], dy_got = after((mix_other, pieces[3], dy_got), mixed)
    mix_got = swap_core(mix_other)
    dy_got, mix_got = after((dy_got, mix_got), mix_got)

    inputs = own_in.reshape(2 * span, width)
    middle, hidden_two = by_rows(
        middle_kernel, "middle", [inputs, mix_mine, mix_got], [gain_two[None]], [F32, BF]
    )
    h2_got = swap_y(hidden_two)
    h2_sib = swap_core(hidden_two)
    dy_sib = swap_core(out_grad)
    dy_sib_got = swap_core(dy_got)
    units = hidden_units
    fours = bit_low + 2 * bit_high
    kinds = [fours ^ at for at in range(4)]
    places = [member * span, (member ^ 1) * span]
    places += [(member ^ (2 + kind // 2)) * span for kind in kinds]
    places += [lax.rem(kind, 2) * units for kind in kinds]

    def ffn(seq, h2):
        head = [seq, y_at * span, (1 - y_at) * span, member * units]
        return feed_forward(
            jnp.stack(head + places),
            h2,
            (out_grad, dy_got, dy_sib, dy_sib_got),
            (w_gate, w_up, unit_core, *[pieces[at] for at in range(4)]),
            w_down,
        )

    act_own, act_sib, grad_own, grad_sib, back_own, back_sib, dy_own, dy_sib_own = ffn(
        y_at, (hidden_two, h2_sib)
    )
    sib_got = swap_core(back_sib)
    h2_near = (hidden_two, h2_sib)
    h2_next = after(h2_got, sib_got)
    h2_far = (h2_next, swap_core(h2_next))
    act_next, act_diag, grad_next, grad_diag, back_next, back_diag, dy_next, dy_diag = ffn(
        1 - y_at, h2_far
    )
    dh2_send = (back_next + swap_core(back_diag).astype(F32)).astype(BF)
    dh2_got = swap_y(dh2_send)
    grads = after((grad_own, grad_sib, grad_next, grad_diag), dh2_send)
    ffn_grad = weight_grad((*h2_near, *h2_far), grads)
    down_grad = weight_grad(
        after((act_own, act_sib, act_next, act_diag), ffn_grad),
        (dy_own, dy_sib_own, dy_next, dy_diag),
    )
    right, left = Ring(1), Ring(-1)
    rows = span // copies
    indices = jnp.stack(
        [jnp.stack([ring.chunk_at(step) for ring in (right, left)]) for step in range(copies)]
    )
    unit_sum = RingSum((right, left), indices, [ffn_grad.reshape(4, span, 2 * units)])
    dh2_got = after(dh2_got, down_grad, *unit_sum.moving)

    def chunk_pair(rows):
        parts = rows.reshape(2, span, width)
        return at_y(parts[0], parts[1])

    grad_middle, grad_branch, ffn_gain_part = by_rows(
        middle_grad_kernel,
        "middle_grad",
        [back_own, sib_got, dh2_got, middle, dy_own],
        [gain_two[None]],
        [F32, BF],
        1,
    )
    unit_sum.advance(grad_branch)
    grad_branch = after(grad_branch, *unit_sum.moving)
    grad_branch = grad_branch.reshape(2, span, width)
    branch_even, branch_odd = by_core(grad_branch, swap_core(grad_branch))
    branch_all = jnp.stack([branch_even, branch_odd], 1).reshape(4 * span, width)
    grad_mixed = contract(branch_all, w_mix, 1, 1).astype(BF)
    mix_grad = contract(mixed, branch_all, 0, 0)
    mix_here, mix_there = at_y(mix_grad[:span], mix_grad[span:])
    mix_there = mix_there.astype(BF)
    mix_grad_got = swap_y(mix_there)
    unit_sum.advance(grad_mixed, mix_there)
    grad_mixed = after(grad_mixed, mix_there, *unit_sum.moving)
    head_grads = []
    head_gain_part = 0.0
    rows_here = []
    rows_got = []
    for part in range(2):
        grad_heads, gain_part = attention_backward(
            part,
            grad_mixed,
            rot,
            key_rot,
            value_low,
            head_normed,
            head_inv,
            log_total,
            cosine,
            sine,
            seg_row,
            seg_col,
            gains,
        )
        head_gain_part = head_gain_part + gain_part
        unit_sum.advance(grad_heads)
        grad_heads = after(grad_heads, *unit_sum.moving)
        head_grads.append(grad_heads)
        attn_grad = contract(hidden_one, grad_heads, 0, 0).reshape(2, 2 * span, -1)
        here, there = at_y(attn_grad[0], attn_grad[1])
        there = there.astype(BF)
        rows_here.append(here)
        rows_got.append(swap_y(there))
        grad_mixed = after(grad_mixed, there)
    head_grads = jnp.concatenate(after(head_grads, grad_mixed), 1)
    back_one = contract(head_grads, w_attn, 1, 1)
    one_mine, one_other = own_and_other(back_one)
    grad_hidden_one = one_mine + swap_core(one_other.astype(BF)).astype(F32)
    inputs = inputs.astype(F32)
    inv_one, _ = own_and_other(inv_all)
    normed_one = inputs * inv_one
    attn_gain_part = jnp.sum(grad_hidden_one * normed_one, 0)
    grad_input = grad_middle + norm_back(grad_hidden_one * gain_one, normed_one, inv_one)
    input_here, input_there = chunk_pair(grad_input)
    input_back = swap_y(input_there.astype(BF))

    acts = after((act_own, act_sib, act_next, act_diag), back_one)
    out_own, out_sib, out_next, out_diag = [
        jnp.dot(act, w_down, preferred_element_type=F32) for act in acts
    ]
    out_own = middle + out_own + swap_core(out_sib.astype(BF)).astype(F32)
    out_next = out_next + swap_core(out_diag.astype(BF)).astype(F32)

    own_here, own_there = chunk_pair(out_own)
    next_here, next_there = chunk_pair(out_next)
    out_back = swap_y(jnp.stack([own_there, next_there]).astype(BF))
    half = width // 2
    head_sum = jnp.stack(
        [
            *jnp.concatenate(
                [here + got.astype(F32) for here, got in zip(rows_here, rows_got)], 1
            ).reshape(2, span, width),
            mix_here + mix_grad_got.astype(F32),
        ]
    )
    sums_right, sums_left = RingSum(
        (right, left), indices, [down_grad[None], head_sum]
    ).finish()
    gate_part, up_part = unit_sum.finish()
    down_rows = units // copies

    def all_heads(part):
        owners = part[down_rows : down_rows + 2 * rows].reshape(2, rows, half)
        mine, other = at_core(owners[0], owners[1])
        both = by_core(mine, swap_core(other))
        return jnp.concatenate([part[:down_rows], *both, part[down_rows + 2 * rows :]])

    def own_rows(part):
        parts = part.reshape(2, 2, rows, units)
        mine, other = at_core(parts[:, 0], parts[:, 1])
        both_cores = jnp.stack(by_core(mine, swap_core(other)), 1)
        here, there = at_y(both_cores[0], both_cores[1])
        all_units = by_y(here, swap_y(there))
        return jnp.concatenate([block[at] for block in all_units for at in range(2)], 1)

    units_gather = RingGather(
        (right, left),
        indices,
        [own_rows(gate_part), own_rows(up_part)],
        [w_gate.shape, w_up.shape],
        [(side, side, (0, rows), (0, 4 * units), 0) for side in range(2)],
    )
    sums_right, sums_left = after((sums_right, sums_left), units_gather.advance(copies // 2 - 1))
    targets = []
    for side in range(2):
        targets.append((0, side, (0, down_rows), (0, half), side * half))
        for at in range(2):
            top = down_rows + at * rows
            place_rows = (top, top + rows)
            half_at = side * span + at * span // 2
            targets += [
                (1, side, place_rows, (0, span), side * 2 * span + at * span),
                (2, side, place_rows, (span, span + span // 2), half_at),
                (3, side, place_rows, (span + span // 2, 2 * span), half_at),
            ]
        top = down_rows + 2 * rows
        targets.append((4, side, (top, top + rows), (0, half), side * half))
    heads_gather = RingGather(
        (right, left),
        indices,
        [all_heads(sums_right), all_heads(sums_left)],
        [value.shape for value in (w_down, w_query, w_key, w_value, w_out)],
        targets,
    )
    w_gate_grad, w_up_grad = units_gather.advance(copies)
    w_down_grad, w_query_grad, w_key_grad, w_value_grad, w_out_grad = heads_gather.advance(copies)

    sums = jnp.concatenate([attn_gain_part, ffn_gain_part[0], head_gain_part.T.reshape(-1)])
    sums = after(sums.reshape(-1, 128), sums_right)
    sums = sums + swap_core(sums)
    sums = sums + swap_y(sums)
    step = 1
    while step < copies:
        sums = sums + lax.ppermute(sums, "replica", [(at, at ^ step) for at in range(copies)])
        step *= 2
    sums = sums.reshape(-1)
    attn_gain_grad = lax.dynamic_slice(sums, (member * span,), (span,))
    ffn_gain_grad = lax.dynamic_slice(sums, (width + member * span,), (span,))
    query_gain_grad = sums[2 * width : 2 * width + HD]
    key_gain_grad = sums[2 * width + HD : 2 * width + 2 * HD]

    out_back, input_back = after((out_back, input_back), sums_right)
    out_back, input_back = out_back.astype(F32), input_back.astype(F32)
    input_grad = jnp.stack(by_y(input_here, input_back))
    block_out = jnp.stack(by_y(own_here + out_back[1], next_here + out_back[0])).astype(BF)

    return (
        block_out,
        input_grad,
        attn_gain_grad,
        w_query_grad,
        w_key_grad,
        w_value_grad,
        query_gain_grad,
        key_gain_grad,
        w_out_grad,
        ffn_gain_grad,
        w_gate_grad,
        w_up_grad,
        w_down_grad,
    )


def solution(mesh):
    rows = P("group", None)
    tokens = P("replica", "group", None)
    placed = (
        tokens,
        P("replica", "group"),
        P("replica", "group"),
        tokens,
        P("group"),
        rows,
        rows,
        rows,
        P(),
        P(),
        rows,
        P("group"),
        rows,
        rows,
        rows,
    )
    return jax.shard_map(
        per_device,
        mesh=mesh,
        in_specs=placed,
        out_specs=(
            tokens,
            tokens,
            P("group"),
            rows,
            rows,
            rows,
            P(),
            P(),
            rows,
            P("group"),
            rows,
            rows,
            rows,
        ),
        check_vma=False,
    )
```

```python
import functools

import jax
import jax.numpy as jnp
from jax import lax
from jax.experimental import pallas as pl
from jax.experimental.pallas import tpu as pltpu
from jax.sharding import PartitionSpec as P

HEADS = 8
PAIRS = 4
HD = 64
HALF = 32
SPAN = 256
LANES = 128

EPS = 1e-05
THETA = 1000000.0
NEG = -1e30

BF = jnp.bfloat16
F32 = jnp.float32
NO_COST = pl.CostEstimate(flops=0, bytes_accessed=0, transcendentals=0)

Y_SWAP = [(0, 2), (2, 0), (1, 3), (3, 1)]
CORE_SWAP = [(0, 1), (1, 0), (2, 3), (3, 2)]
CROSS_SWAP = [(0, 3), (3, 0), (1, 2), (2, 1)]


def contract(left, right, left_dim, right_dim):
    return lax.dot_general(
        left, right, (((left_dim,), (right_dim,)), ((), ())), preferred_element_type=F32
    )


def visible_block(seg_col, seg_row, block):
    end = (block + 1) * SPAN
    key_at = lax.broadcasted_iota(jnp.int32, (end, SPAN), 0)
    query_at = lax.broadcasted_iota(jnp.int32, (end, SPAN), 1) + block * SPAN
    return (seg_col[0:end, :] == seg_row[:, block * SPAN : end]) & (key_at <= query_at)


def project_kernel(
    hidden_ref,
    weight_ref,
    cos_ref,
    sin_ref,
    gain_ref,
    rot_ref,
    key_ref,
    value_ref,
    value_t_ref,
    normed_ref,
    inv_ref,
):
    raw = jnp.dot(hidden_ref[...], weight_ref[...], preferred_element_type=F32)
    raw_t = raw.T
    for half in range(2):
        cols = slice(half * 2 * SPAN + 3 * LANES, (half + 1) * 2 * SPAN)
        place = slice(half * LANES, (half + 1) * LANES)
        value_ref[:, place] = raw[:, cols].astype(BF)
        value_t_ref[place, :] = raw_t[cols, :].astype(BF)
    cosine = cos_ref[...]
    sine = sin_ref[...]
    for head in range(HEADS + PAIRS):
        rows = slice(head * HD, (head + 1) * HD)
        if head < HEADS:
            at = head // 4 * 2 * SPAN + head % 4 * HD
        else:
            at = (head - HEADS) // 2 * 2 * SPAN + SPAN + head % 2 * HD
        part = raw_t[at : at + HD, :]
        inv = lax.rsqrt(jnp.mean(part * part, 0, keepdims=True) + EPS)
        normed = part * inv
        normed_ref[rows, :] = normed
        inv_ref[head : head + 1, :] = inv
        kind = 0 if head < HEADS else 1
        scaled = normed * gain_ref[:, kind : kind + 1]
        first = scaled[:HALF, :]
        second = scaled[HALF:, :]
        turned = jnp.concatenate(
            [first * cosine - second * sine, second * cosine + first * sine], 0
        ).astype(BF)
        if head < HEADS:
            rot_ref[rows, :] = turned * BF(HD**-0.5)
        else:
            rot_ref[rows, :] = turned
            key_ref[head - HEADS] = turned.astype(F32).T.astype(BF)


def forward_kernel(
    rot_ref,
    key_ref,
    value_t_ref,
    seg_row_ref,
    seg_col_ref,
    at_ref,
    w_own_ref,
    w_got_ref,
    mixed_ref,
    log_ref,
    w_mix_ref,
    mine_ref,
    other_ref,
    mixed_t,
):
    w_mix_ref[pl.ds(pl.multiple_of(at_ref[0] * SPAN, SPAN), SPAN), :] = w_own_ref[...]
    w_mix_ref[pl.ds(pl.multiple_of((1 - at_ref[0]) * SPAN, SPAN), SPAN), :] = w_got_ref[...]
    for block in range(mixed_ref.shape[0] // SPAN):
        end = (block + 1) * SPAN
        span = slice(block * SPAN, end)
        visible = visible_block(seg_col_ref[...], seg_row_ref[...], block)

        def one_head(head, carry, end=end, span=span, visible=visible):
            pair = head // 2
            rows = pl.ds(pl.multiple_of(head * HD, HD), HD)
            score = jnp.dot(
                key_ref[pair, 0:end, :], rot_ref[rows, span], preferred_element_type=F32
            )
            score = jnp.where(visible, score, NEG)
            top = jnp.max(score, 0, keepdims=True)
            weight = jnp.exp(score - top)
            total = jnp.sum(weight, 0, keepdims=True)
            log_ref[pl.ds(head, 1), span] = top + jnp.log(total)
            prob = (weight * (1.0 / total)).astype(BF)
            values_t = value_t_ref[pl.ds(pl.multiple_of(pair * HD, HD), HD), 0:end]
            mixed_t[rows, :] = jnp.dot(values_t, prob, preferred_element_type=F32)
            return carry

        lax.fori_loop(0, HEADS, one_head, 0)
        for pair in range(PAIRS):
            cols = slice(pair * 2 * HD, (pair + 1) * 2 * HD)
            mixed_ref[span, cols] = mixed_t[cols, :].T.astype(BF)
    core = at_ref[1]
    for part in range(2):
        span = slice(part * SPAN, (part + 1) * SPAN)
        for where, out in ((core, mine_ref), (1 - core, other_ref)):
            rows = pl.ds(pl.multiple_of((2 * part + where) * SPAN, SPAN), SPAN)
            out[span, :] = jnp.dot(
                mixed_ref[rows, :], w_mix_ref[...], preferred_element_type=F32
            ).astype(out.dtype)


def backward_kernel(
    half,
    grad_ref,
    query_ref,
    key_t_ref,
    key_ref,
    value_ref,
    query_normed_ref,
    key_normed_ref,
    inv_ref,
    log_ref,
    cos_ref,
    sin_ref,
    seg_row_ref,
    seg_col_ref,
    gain_ref,
    out_ref,
    gain_grad_ref,
    grad_t,
    head_grad,
    value_one,
    key_sum,
    value_sum,
    out_t,
):
    length = grad_ref.shape[0]
    heads = HEADS // 2
    pairs = PAIRS // 2
    for part in range(pairs):
        cols = slice(part * 2 * HD, (part + 1) * 2 * HD)
        grad_t[cols, :] = grad_ref[:, cols].astype(F32).T.astype(BF)
    values_t = value_ref[...].astype(F32).T
    for pair in range(pairs):
        value_one[pair] = values_t[pair * HD : (pair + 1) * HD, :].T.astype(BF)
    left_lane = lax.broadcasted_iota(jnp.int32, (SPAN, 2 * HD), 1) < HD
    zero = jnp.zeros((SPAN, 2 * HD), BF)

    def one_pair(pair, carry):
        key_sum[...] = jnp.zeros_like(key_sum)
        value_sum[...] = jnp.zeros_like(value_sum)
        keys_t = key_t_ref[pl.ds(pl.multiple_of(pair * HD, HD), HD), :]
        both = pl.ds(pl.multiple_of(pair * 2 * HD, 2 * HD), 2 * HD)
        for block in range(length // SPAN):
            end = (block + 1) * SPAN
            span = slice(block * SPAN, end)
            visible = visible_block(seg_col_ref[...], seg_row_ref[...], block)
            queries = query_ref[both, span].astype(F32).T.astype(BF)
            grads = grad_ref[span, both]
            for side in range(2):
                head = pair * 2 + side
                rows = pl.ds(pl.multiple_of(head * HD, HD), HD)
                score = jnp.dot(
                    key_ref[pair, 0:end, :], query_ref[rows, span], preferred_element_type=F32
                )
                logs = log_ref[pl.ds(half * heads + head, 1), span]
                prob = jnp.where(visible, jnp.exp(score - logs), 0.0)
                grad_prob = jnp.dot(
                    value_one[pair, 0:end, :], grad_t[rows, span], preferred_element_type=F32
                )
                inner = jnp.sum(prob * grad_prob, 0, keepdims=True)
                grad_score = (prob * (grad_prob - inner)).astype(BF)
                mine = left_lane if side == 0 else jnp.logical_not(left_lane)
                value_sum[0:end, :] += jnp.dot(
                    prob.astype(BF), jnp.where(mine, grads, zero), preferred_element_type=F32
                )
                key_sum[0:end, :] += jnp.dot(
                    grad_score, jnp.where(mine, queries, zero), preferred_element_type=F32
                )
                head_grad[rows, span] = jnp.dot(
                    keys_t[:, 0:end], grad_score, preferred_element_type=F32
                ) * (HD**-0.5)
        key_t = key_sum[...].T
        value_t = value_sum[...].T
        key_rows = pl.ds(pl.multiple_of((heads + pair) * HD, HD), HD)
        head_grad[key_rows, :] = key_t[:HD, :] + key_t[HD:, :]
        value_rows = pl.ds(pl.multiple_of((heads + pairs + pair) * HD, HD), HD)
        out_t[value_rows, :] = value_t[:HD, :] + value_t[HD:, :]
        return carry

    lax.fori_loop(0, pairs, one_pair, 0)

    cosine = cos_ref[...]
    sine = sin_ref[...]
    gain_sums = [jnp.zeros((HD, length), F32), jnp.zeros((HD, length), F32)]
    for head in range(heads + pairs):
        rows = slice(head * HD, (head + 1) * HD)
        kind = 0 if head < heads else 1
        part = head_grad[rows, :]
        first = part[:HALF, :]
        second = part[HALF:, :]
        turned = jnp.concatenate(
            [first * cosine + second * sine, second * cosine - first * sine], 0
        )
        if kind == 0:
            normed = query_normed_ref[rows, :]
            line = half * heads + head
        else:
            normed = key_normed_ref[(head - heads) * HD : (head - heads + 1) * HD, :]
            line = HEADS + half * pairs + head - heads
        gain_sums[kind] = gain_sums[kind] + turned * normed
        scaled = turned * gain_ref[:, kind : kind + 1]
        mean = jnp.mean(scaled * normed, 0, keepdims=True)
        out_t[rows, :] = inv_ref[line : line + 1, :] * (scaled - normed * mean)
    for kind in range(2):
        gain_grad_ref[:, kind : kind + 1] = jnp.sum(gain_sums[kind], 1, keepdims=True)
    for part in range(out_t.shape[0] // (2 * HD)):
        cols = slice(part * 2 * HD, (part + 1) * 2 * HD)
        out_ref[:, cols] = out_t[cols, :].T.astype(BF)


def in_hbm(shape, kind):
    return pltpu.HBM(shape, kind)


def from_hbm(*operands):
    return [
        pltpu.with_memory_space_constraint(value, pltpu.HBM) if value.size >= 2**16 else value
        for value in operands
    ]


def whole_refs(count):
    return [pl.BlockSpec(memory_space=pltpu.VMEM)] * count


def project(hidden, weight, cosine, sine, gains):
    length = hidden.shape[0]
    rows = (HEADS + PAIRS) * HD
    outs = [
        ((rows, length), BF),
        ((PAIRS, length, HD), BF),
        ((length, PAIRS * HD), BF),
        ((PAIRS * HD, length), BF),
        ((rows, length), F32),
        ((16, length), F32),
    ]
    return pl.pallas_call(
        project_kernel,
        out_shape=[in_hbm(shape, kind) for shape, kind in outs],
        grid=(length // SPAN,),
        in_specs=[
            pl.BlockSpec((SPAN, hidden.shape[1]), lambda at: (at, 0)),
            pl.BlockSpec(weight.shape, lambda at: (0, 0)),
            pl.BlockSpec((HALF, SPAN), lambda at: (0, at)),
            pl.BlockSpec((HALF, SPAN), lambda at: (0, at)),
            pl.BlockSpec(gains.shape, lambda at: (0, 0)),
        ],
        out_specs=[
            pl.BlockSpec((rows, SPAN), lambda at: (0, at)),
            pl.BlockSpec((PAIRS, SPAN, HD), lambda at: (0, at, 0)),
            pl.BlockSpec((SPAN, PAIRS * HD), lambda at: (at, 0)),
            pl.BlockSpec((PAIRS * HD, SPAN), lambda at: (0, at)),
            pl.BlockSpec((rows, SPAN), lambda at: (0, at)),
            pl.BlockSpec((16, SPAN), lambda at: (0, at)),
        ],
        compiler_params=pltpu.CompilerParams(vmem_limit_bytes=24 * 1024 * 1024),
        cost_estimate=NO_COST,
        name="project",
    )(*from_hbm(hidden, weight), cosine, sine, gains)


def attention_forward(rot, key, value_t, seg_row, seg_col, at, w_own, w_got):
    length = rot.shape[1]
    width = w_own.shape[1]
    outs = [
        ((length, HEADS * HD), BF),
        ((HEADS, length), F32),
        ((HEADS * HD, width), BF),
        ((length // 2, width), F32),
        ((length // 2, width), BF),
    ]
    return pl.pallas_call(
        forward_kernel,
        out_shape=[in_hbm(shape, kind) for shape, kind in outs],
        in_specs=whole_refs(5) + [pl.BlockSpec(memory_space=pltpu.SMEM)] + whole_refs(2),
        out_specs=whole_refs(len(outs)),
        scratch_shapes=[pltpu.VMEM((HEADS * HD, SPAN), F32)],
        compiler_params=pltpu.CompilerParams(vmem_limit_bytes=24 * 1024 * 1024),
        cost_estimate=NO_COST,
        name="attention_forward",
    )(*from_hbm(rot, key, value_t), seg_row, seg_col, at, *from_hbm(w_own, w_got))


def middle_kernel(inputs_ref, mine_ref, got_ref, gain_ref, middle_ref, hidden_ref):
    middle = inputs_ref[...].astype(F32) + mine_ref[...] + got_ref[...].astype(F32)
    middle_ref[...] = middle
    normed, _ = norm_rows(middle)
    hidden_ref[...] = (normed * gain_ref[...]).astype(BF)


def by_rows(kernel, name, rows_in, whole_in, rows_out, sums_out=0):
    rows, width = rows_in[0].shape
    tile = 2 * LANES
    block = pl.BlockSpec((tile, width), lambda at: (at, 0))
    line = pl.BlockSpec((1, width), lambda at: (0, 0))
    return pl.pallas_call(
        kernel,
        grid=(rows // tile,),
        out_shape=[in_hbm((rows, width), kind) for kind in rows_out]
        + [jax.ShapeDtypeStruct((1, width), F32)] * sums_out,
        in_specs=[block] * len(rows_in) + [line] * len(whole_in),
        out_specs=[block] * len(rows_out) + [line] * sums_out,
        compiler_params=pltpu.CompilerParams(vmem_limit_bytes=16 * 1024 * 1024),
        cost_estimate=NO_COST,
        name=name,
    )(*[from_hbm(value)[0] if value.dtype == F32 else value for value in rows_in], *whole_in)


def middle_grad_kernel(
    own_ref, sib_ref, got_ref, middle_ref, dy_ref, gain_ref, grad_ref, branch_ref, gain_grad_ref
):
    dh2 = own_ref[...] + sib_ref[...].astype(F32) + got_ref[...].astype(F32)
    normed, inv = norm_rows(middle_ref[...])

    @pl.when(pl.program_id(0) == 0)
    def _():
        gain_grad_ref[...] = jnp.zeros_like(gain_grad_ref)

    gain_grad_ref[...] += jnp.sum(dh2 * normed, 0, keepdims=True)
    grad = dy_ref[...].astype(F32) + norm_back(dh2 * gain_ref[...], normed, inv)
    grad_ref[...] = grad
    branch_ref[...] = grad.astype(BF)


def attention_backward(half, grad, rot, key, value, normed, inv, log, cosine, sine, seg_row, seg_col, gains):
    length = grad.shape[0]
    queries = HEADS * HD // 2
    keys = PAIRS * HD // 2
    width = queries + 2 * keys

    def rows_of(count, at):
        return pl.BlockSpec((count, length), lambda step: (at, 0))

    def columns_of(count):
        return pl.BlockSpec((length, count), lambda step: (0, half))

    key_at = 2 * queries // keys + half
    return pl.pallas_call(
        functools.partial(backward_kernel, half),
        grid=(1,),
        out_shape=[
            in_hbm((length, width), BF),
            jax.ShapeDtypeStruct((HD, 2), F32),
        ],
        in_specs=[
            columns_of(queries),
            rows_of(queries, half),
            rows_of(keys, key_at),
            pl.BlockSpec((PAIRS // 2, length, HD), lambda step: (half, 0, 0)),
            columns_of(keys),
            rows_of(queries, half),
            rows_of(keys, key_at),
        ]
        + whole_refs(7),
        out_specs=whole_refs(2),
        scratch_shapes=[
            pltpu.VMEM((queries, length), BF),
            pltpu.VMEM((queries + keys, length), F32),
            pltpu.VMEM((PAIRS // 2, length, HD), BF),
            pltpu.VMEM((length, 2 * HD), F32),
            pltpu.VMEM((length, 2 * HD), F32),
            pltpu.VMEM((width, length), F32),
        ],
        compiler_params=pltpu.CompilerParams(vmem_limit_bytes=28 * 1024 * 1024),
        cost_estimate=NO_COST,
        name="attention_backward",
    )(
        *from_hbm(grad, rot, rot, key, value, normed, normed),
        inv,
        log,
        cosine,
        sine,
        seg_row,
        seg_col,
        gains,
    )


def feed_forward_kernel(
    at_ref,
    h2_a,
    h2_b,
    dy_a,
    dy_a_got,
    dy_b,
    dy_b_got,
    w_gate,
    w_up,
    w_sib,
    piece_0,
    piece_1,
    piece_2,
    piece_3,
    w_down,
    act_a,
    act_b,
    grad_a,
    grad_b,
    back_a,
    back_b,
    dy_out_a,
    dy_out_b,
    h2_t_a,
    h2_t_b,
    act_t_a,
    act_t_b,
    h2_v,
    dy_v,
    in_v,
    down_v,
    act_v,
    grad_v,
    back_own,
    back_sib,
    h2_t,
    act_t,
    grad_act,
    load_sems,
    store_sems,
):
    units = down_v.shape[0]

    def rows_at(index):
        return pl.ds(pl.multiple_of(at_ref[index], SPAN), SPAN)

    def units_at(index):
        return pl.ds(pl.multiple_of(at_ref[index], LANES), units)

    loads = []

    def load(source, target):
        loads.append(pltpu.make_async_copy(source, target, load_sems.at[len(loads)]))
        loads[-1].start()

    def load_dy(part, own, got):
        load(own.at[at_ref[0]], dy_v.at[part, rows_at(1)])
        load(got.at[at_ref[0]], dy_v.at[part, rows_at(2)])

    load_dy(0, dy_a, dy_a_got)
    load(w_down, down_v)
    load(h2_a, h2_v.at[0])
    load(w_gate.at[:, units_at(3)], in_v.at[rows_at(4), 0:units])
    load(w_up.at[:, units_at(3)], in_v.at[rows_at(4), units : 2 * units])
    load(w_sib, in_v.at[rows_at(5)])
    for at, piece in enumerate((piece_0, piece_1, piece_2, piece_3)):
        load(piece, in_v.at[rows_at(6 + at), units_at(10 + at)])
    weights_end = len(loads)
    load_dy(1, dy_b, dy_b_got)
    load(h2_b, h2_v.at[1])
    stores = []
    for part in range(2):
        for at in range(3) if part == 0 else range(weights_end, weights_end + 2):
            loads[at].wait()
        for start in range(0, units, 256):
            end = min(start + 256, units)
            grad_act[:, start:end] = contract(dy_v[part], down_v[start:end, :], 1, 1)
        for at in range(3, weights_end) if part == 0 else [weights_end + 2]:
            loads[at].wait()
        for start in range(0, units, LANES):
            gate_cols = slice(start, start + LANES)
            up_cols = slice(units + start, units + start + LANES)
            weight = jnp.concatenate([in_v[:, gate_cols], in_v[:, up_cols]], 1)
            both = jnp.dot(h2_v[part], weight, preferred_element_type=F32)
            gate, up = both[:, :LANES], both[:, LANES:]
            sig = jax.nn.sigmoid(gate)
            silu = gate * sig
            grad = grad_act[:, gate_cols]
            act_v[part, :, gate_cols] = (silu * up).astype(BF)
            grad_gate = grad * up * sig * (1.0 + gate * (1.0 - sig))
            grad_v[part, :, gate_cols] = grad_gate.astype(BF)
            grad_v[part, :, up_cols] = (grad * silu).astype(BF)
        h2_t[part] = h2_v[part].T
        act_t[part] = act_v[part].T
        back = contract(grad_v[part], in_v[...], 1, 1)
        if part == 0:
            back_own[...] = back
        else:
            back_sib[...] = back.astype(BF)
        for at, (source, target) in enumerate(
            [
                (act_v.at[part], (act_a, act_b)[part]),
                (grad_v.at[part], (grad_a, grad_b)[part]),
                ((back_own, back_sib)[part], (back_a, back_b)[part]),
                (dy_v.at[part], (dy_out_a, dy_out_b)[part]),
                (h2_t.at[part], (h2_t_a, h2_t_b)[part]),
                (act_t.at[part], (act_t_a, act_t_b)[part]),
            ]
        ):
            stores.append(pltpu.make_async_copy(source, target, store_sems.at[part * 6 + at]))
            stores[-1].start()
    for store in stores:
        store.wait()


def feed_forward(at, h2, dy, weights, w_down):
    rows, width = h2[0].shape
    units = w_down.shape[0]
    outs = (
        [((rows, units), BF)] * 2
        + [((rows, 2 * units), BF)] * 2
        + [((rows, width), F32), ((rows, width), BF)]
        + [((rows, width), BF)] * 2
        + [((width, rows), BF)] * 2
        + [((units, rows), BF)] * 2
    )
    operands = from_hbm(*h2, *dy, *weights, w_down)
    return pl.pallas_call(
        feed_forward_kernel,
        out_shape=[in_hbm(shape, kind) for shape, kind in outs],
        in_specs=[pl.BlockSpec(memory_space=pltpu.SMEM)]
        + [pl.BlockSpec(memory_space=pl.ANY)] * len(operands),
        out_specs=[pl.BlockSpec(memory_space=pl.ANY)] * len(outs),
        scratch_shapes=[
            pltpu.VMEM((2, rows, width), BF),
            pltpu.VMEM((2, rows, width), BF),
            pltpu.VMEM((width, 2 * units), BF),
            pltpu.VMEM(w_down.shape, BF),
            pltpu.VMEM((2, rows, units), BF),
            pltpu.VMEM((2, rows, 2 * units), BF),
            pltpu.VMEM((rows, width), F32),
            pltpu.VMEM((rows, width), BF),
            pltpu.VMEM((2, width, rows), BF),
            pltpu.VMEM((2, units, rows), BF),
            pltpu.VMEM((rows, units), F32),
            pltpu.SemaphoreType.DMA((14,)),
            pltpu.SemaphoreType.DMA((12,)),
        ],
        compiler_params=pltpu.CompilerParams(vmem_limit_bytes=44 * 1024 * 1024),
        cost_estimate=NO_COST,
        name="feed_forward",
    )(at, *operands)


def weight_grad_kernel(count, *refs):
    left, right = refs[:count], refs[count : 2 * count]
    out = refs[-1]
    total = jnp.dot(left[0][...], right[0][...], preferred_element_type=F32)
    for at in range(1, count):
        total += jnp.dot(left[at][...], right[at][...], preferred_element_type=F32)
    out[...] = total.astype(BF)


def weight_grad(left, right):
    height, rows = left[0].shape
    width = right[0].shape[1]
    count = len(left)
    step = SPAN
    return pl.pallas_call(
        functools.partial(weight_grad_kernel, count),
        grid=(width // step,),
        out_shape=in_hbm((height, width), BF),
        in_specs=[pl.BlockSpec((height, rows), lambda at: (0, 0))] * count
        + [pl.BlockSpec((rows, step), lambda at: (0, at))] * count,
        out_specs=pl.BlockSpec((height, step), lambda at: (0, at)),
        compiler_params=pltpu.CompilerParams(vmem_limit_bytes=24 * 1024 * 1024),
        cost_estimate=NO_COST,
        name="weight_grad",
    )(*from_hbm(*left, *right))


def norm_rows(inputs):
    inv = lax.rsqrt(jnp.mean(inputs * inputs, -1, keepdims=True) + EPS)
    return (inputs * inv, inv)


def norm_back(grad, normed, inv):
    return inv * (grad - normed * jnp.mean(grad * normed, -1, keepdims=True))


def swap_y(value):
    return lax.ppermute(value, "group", Y_SWAP)


def swap_cross(value):
    return lax.ppermute(value, "group", CROSS_SWAP)


def swap_core(value):
    return lax.ppermute(value, "group", CORE_SWAP)


def after(value, *earlier):
    return lax.optimization_barrier((value, earlier))[0]


def cycle_of(count):
    return list(range(0, count, 2)) + list(range(count - 1, 0, -2))


class Ring:
    def __init__(self, way):
        count = lax.axis_size("replica")
        cycle = cycle_of(count)[::way]
        self.count = count
        self.way = way
        self.hops = [(cycle[at], cycle[(at + 1) % count]) for at in range(count)]
        mine = lax.axis_index("replica")
        self.place = jnp.where(lax.rem(mine, 2) == 0, mine // 2, count - 1 - mine // 2)

    def chunk_at(self, back):
        at = lax.rem(self.place - self.way * back + self.count, self.count)
        return jnp.where(at < self.count // 2, 2 * at, 2 * (self.count - 1 - at) + 1)

    def send(self, value):
        return lax.ppermute(value, "replica", self.hops)


def pick_kernel(step, count, index_ref, *refs):
    sources = refs[:count]
    outs, shares, sems = refs[-count - 3 : -count - 1], refs[-count - 1 : -1], refs[-1]
    arrived = refs[count : -count - 3]
    copies = []
    for side in range(2):
        for at, (source, share) in enumerate(zip(sources, shares)):
            _, _, rows, half = share.shape
            row = pl.multiple_of(index_ref[step, side] * rows, 8)
            copies.append(
                pltpu.make_async_copy(
                    source.at[:, pl.ds(row, rows), side * half : (side + 1) * half],
                    share.at[side],
                    sems.at[side, at],
                )
            )
    for copy in copies:
        copy.start()
    for copy in copies:
        copy.wait()
    for side in range(2):
        start = 0
        for share in shares:
            _, kinds, rows, _ = share.shape
            for kind in range(kinds):
                span = slice(start, start + rows)
                part = share[side, kind].astype(F32)
                if arrived:
                    part = part + arrived[side][span, :].astype(F32)
                outs[side][span, :] = part.astype(BF)
                start += rows


def pick_chunks(step, indices, sources, arrived):
    copies = indices.shape[0]
    rows = [source.shape[1] // copies for source in sources]
    half = sources[0].shape[2] // 2
    if any(count % 16 for count in rows):
        moving = []
        for side in range(2):
            parts = [
                lax.dynamic_slice(
                    source,
                    (0, indices[step, side] * count, side * half),
                    (source.shape[0], count, half),
                ).reshape(-1, half)
                for source, count in zip(sources, rows)
            ]
            part = jnp.concatenate([part.astype(F32) for part in parts])
            if arrived:
                part = part + arrived[side].astype(F32)
            moving.append(part.astype(BF))
        return moving
    total = sum(source.shape[0] * count for source, count in zip(sources, rows))
    return pl.pallas_call(
        functools.partial(pick_kernel, step, len(sources)),
        out_shape=[jax.ShapeDtypeStruct((total, half), BF)] * 2,
        in_specs=[pl.BlockSpec(memory_space=pltpu.SMEM)]
        + [pl.BlockSpec(memory_space=pl.ANY)] * len(sources)
        + whole_refs(len(arrived)),
        out_specs=whole_refs(2),
        scratch_shapes=[
            pltpu.VMEM((2, source.shape[0], count, half), source.dtype)
            for source, count in zip(sources, rows)
        ]
        + [pltpu.SemaphoreType.DMA((2, len(sources)))],
        compiler_params=pltpu.CompilerParams(vmem_limit_bytes=8 * 1024 * 1024),
        cost_estimate=NO_COST,
        name="pick_chunks",
    )(indices, *from_hbm(*sources), *arrived)


class RingSum:
    def __init__(self, rings, indices, sources):
        self.rings, self.indices, self.sources = rings, indices, sources
        self.moving = pick_chunks(1, indices, sources, [])
        self.step = 1

    def advance(self, *earlier):
        count = self.rings[0].count
        if self.step == count:
            return
        self.step += 1
        arrived = [ring.send(chunk) for ring, chunk in zip(self.rings, self.moving)]
        arrived = after(arrived, *earlier)
        self.moving = pick_chunks(self.step % count, self.indices, self.sources, arrived)

    def finish(self):
        while self.step < self.rings[0].count:
            self.advance()
        return self.moving


def place_kernel(steps, targets, stores, index_ref, *refs):
    count = 2 * len(steps)
    chunks = refs[:count]
    outs = refs[-1 - count - stores : -1 - count]
    wide = refs[-1 - count : -1]
    sems = refs[-1]
    copies = []
    for turn, step in enumerate(steps):
        for side in range(2):
            wide[2 * turn + side][...] = chunks[2 * turn + side][...].astype(F32)
        for at, (store, side, (top, bottom), (start, end), column) in enumerate(targets):
            rows = bottom - top
            row = pl.multiple_of(index_ref[step, side] * rows, 8)
            copies.append(
                pltpu.make_async_copy(
                    wide[2 * turn + side].at[top:bottom, start:end],
                    outs[store].at[pl.ds(row, rows), column : column + end - start],
                    sems.at[turn, at],
                )
            )
            copies[-1].start()
    for copy in copies:
        copy.wait()


def place_chunks(steps, indices, chunks, stores, shapes, targets):
    if any((bottom - top) % 8 for _, _, (top, bottom), _, _ in targets):
        stores = stores or [jnp.zeros(shape, F32) for shape in shapes]
        for turn, step in enumerate(steps):
            for store, side, (top, bottom), (start, end), column in targets:
                stores[store] = lax.dynamic_update_slice(
                    stores[store],
                    chunks[2 * turn + side][top:bottom, start:end].astype(F32),
                    (indices[step, side] * (bottom - top), column),
                )
        return stores
    given = stores or []
    return list(
        pl.pallas_call(
            functools.partial(place_kernel, steps, targets, len(shapes)),
            out_shape=[in_hbm(shape, F32) for shape in shapes],
            in_specs=[pl.BlockSpec(memory_space=pltpu.SMEM)]
            + whole_refs(len(chunks))
            + [pl.BlockSpec(memory_space=pl.ANY)] * len(given),
            out_specs=[pl.BlockSpec(memory_space=pl.ANY)] * len(shapes),
            scratch_shapes=[pltpu.VMEM(chunk.shape, F32) for chunk in chunks]
            + [pltpu.SemaphoreType.DMA((len(steps), len(targets)))],
            input_output_aliases={1 + len(chunks) + at: at for at in range(len(given))},
            compiler_params=pltpu.CompilerParams(vmem_limit_bytes=12 * 1024 * 1024),
            cost_estimate=NO_COST,
            name="place_chunks",
        )(indices, *chunks, *from_hbm(*given))
    )


class RingGather:
    def __init__(self, rings, indices, chunks, shapes, targets):
        self.rings, self.indices, self.chunks = rings, indices, chunks
        self.shapes, self.targets = shapes, targets
        self.stores = []
        self.waiting = [(0, chunks)]
        self.placed = [[], []]
        self.step = 0

    def advance(self, steps):
        count = self.rings[0].count
        while steps and self.step + 1 < count:
            steps -= 1
            self.step += 1
            held = after(self.chunks, *self.placed.pop(0))
            self.chunks = [ring.send(chunk) for ring, chunk in zip(self.rings, held)]
            self.waiting.append((self.step, self.chunks))
            if len(self.waiting) == 2 or self.step + 1 == count:
                self.stores = place_chunks(
                    [step for step, _ in self.waiting],
                    self.indices,
                    [chunk for _, pair in self.waiting for chunk in pair],
                    self.stores,
                    self.shapes,
                    self.targets,
                )
                self.waiting = []
            self.placed.append(self.stores)
        return self.stores


def per_device(
    hidden_in,
    segments,
    positions,
    out_grad,
    attn_gain,
    w_query,
    w_key,
    w_value,
    query_gain,
    key_gain,
    w_out,
    ffn_gain,
    w_gate,
    w_up,
    w_down,
):
    copies = lax.axis_size("replica")
    member = lax.axis_index("group")
    y_at = member // 2
    core = lax.rem(member, 2)
    on_low_y = y_at == 0
    on_low_core = core == 0
    span, width = hidden_in.shape[1:]
    hidden_units = w_down.shape[0]

    def by_y(mine, other):
        return jnp.where(on_low_y, mine, other), jnp.where(on_low_y, other, mine)

    def by_core(mine, other):
        return jnp.where(on_low_core, mine, other), jnp.where(on_low_core, other, mine)

    def at_y(pair_low, pair_high):
        return jnp.where(on_low_y, pair_low, pair_high), jnp.where(on_low_y, pair_high, pair_low)

    def at_core(low, high):
        return jnp.where(on_low_core, low, high), jnp.where(on_low_core, high, low)

    def quarters(weight):
        size = weight.shape[1] // 4
        return [weight[:, at * size : (at + 1) * size] for at in range(4)]

    def core_columns(*weights):
        parts = [quarters(weight) for weight in weights]
        low = [part[0] for part in parts] + [part[2] for part in parts]
        high = [part[1] for part in parts] + [part[3] for part in parts]
        return at_core(jnp.concatenate(low, 1), jnp.concatenate(high, 1))

    def own_and_other(rows):
        parts = rows.reshape(2, 2, span, rows.shape[-1])
        mine, other = at_core(parts[:, 0], parts[:, 1])
        return mine.reshape(2 * span, -1), other.reshape(2 * span, -1)

    def in_order(mine, at_y, sibling, across):
        here = jnp.concatenate(by_core(mine, sibling), 0)
        there = jnp.concatenate(by_core(at_y, across), 0)
        return jnp.concatenate(by_y(here, there), 0)

    replica = lax.axis_index("replica")
    bit_low = lax.rem(replica, 2)
    bit_high = lax.rem(replica // 2, 2)

    def swap_replica(value, bit):
        return lax.ppermute(value, "replica", [(at, at ^ bit) for at in range(copies)])

    kv_rows = jnp.concatenate([w_key, w_value], 1)
    half_send = jnp.where(bit_low == 0, w_query, kv_rows)
    half_got = swap_y(half_send)
    small = after((attn_gain, ffn_gain, segments, positions), half_send)
    small = jnp.concatenate(
        [value.astype(F32)[None] for value in small[:2]]
        + [value.astype(F32) for value in small[2:]],
        0,
    )
    small_got = swap_y(small)

    hidden_first = after(hidden_in, half_send, small)
    seq_mine, seq_other = at_y(hidden_first[0], hidden_first[1])
    seq_got = swap_y(seq_other)
    w_query, w_key, w_value, w_gate, w_up = after(
        (w_query, w_key, w_value, w_gate, w_up), seq_other
    )
    mine_cols, other_cols = core_columns(w_query, w_key, w_value)
    rows_core = swap_core(other_cols)

    def unit_columns(weight, owner):
        return lax.dynamic_slice(weight, (0, owner * hidden_units), (span, hidden_units))

    target = member ^ (2 + bit_high)
    piece_send = jnp.where(bit_low == 0, unit_columns(w_gate, target), unit_columns(w_up, target))
    pieces = {
        0: lax.ppermute(
            piece_send,
            ("replica", "group"),
            [
                (4 * at + of, 4 * at + (of ^ (2 + (at // 2) % 2)))
                for at in range(copies)
                for of in range(4)
            ],
        )
    }

    small_low, small_high = by_y(small, small_got)
    small_two = jnp.stack([small_low, small_high])
    small_even, small_odd = by_core(small_two, swap_core(small_two))
    small_all = jnp.stack([small_even, small_odd], 1).reshape(4, 6, span)
    small_rows = small_all.transpose(1, 0, 2).reshape(6, 4 * span)
    gain_one = small_rows[0]
    gain_two = small_rows[1]
    seg = jnp.where(on_low_y, small_rows[2], small_rows[3])
    place = jnp.where(on_low_y, small_rows[4], small_rows[5])

    own_low, own_high = by_y(seq_mine, seq_got)
    own_in = jnp.stack([own_low, own_high])
    all_even, all_odd = by_core(own_in, swap_core(own_in))
    all_in = jnp.stack([all_even, all_odd], 1).reshape(4 * span, width)
    normed_all, inv_all = norm_rows(all_in.astype(F32))
    hidden_one = (normed_all * gain_one).astype(BF)
    freq = THETA ** (-(jnp.arange(HALF, dtype=F32) * 2.0 / HD))
    angle = freq[:, None] * place[None, :]
    cosine, sine = jnp.cos(angle), jnp.sin(angle)
    gains = jnp.stack([query_gain, key_gain], 1).astype(F32)
    seg_row = seg[None, :]
    seg_col = seg[:, None]
    unit_core = swap_core(
        jnp.concatenate([unit_columns(w_gate, member ^ 1), unit_columns(w_up, member ^ 1)], 1)
    )

    half_swapped = swap_replica(half_got, 1)
    query_y = jnp.where(bit_low == 0, half_got, half_swapped)
    rest_y = jnp.where(bit_low == 0, half_swapped, half_got)
    mine_y, other_y = core_columns(query_y, rest_y[:, : width // 2], rest_y[:, width // 2 :])
    rows_cross = swap_core(other_y)
    w_attn = in_order(mine_cols, mine_y, rows_core, rows_cross)
    w_out_send, dy_first = after((w_out, out_grad), other_y)
    out_got = swap_y(w_out_send)
    dy_sib = swap_core(dy_first)

    rot, key_rot, value_low, value_t, head_normed, head_inv = project(
        hidden_one, w_attn, cosine, sine, gains
    )
    pieces[0], rot, dy_send = after((pieces[0], rot, out_grad), rot, pieces[0])
    for bits in range(1, 4):
        pieces[bits] = swap_replica(pieces[0], bits)
    dy_got = swap_y(dy_send)
    rot, out_got, unit_core, dy_sib = after((rot, out_got, unit_core, dy_sib), pieces[0])
    mixed, log_total, w_mix, mix_mine, mix_other = attention_forward(
        rot, key_rot, value_t, seg_row, seg_col, jnp.stack([y_at, core]), w_out, out_got
    )
    mix_other, dy_got, pieces[1], pieces[2], pieces[3] = after(
        (mix_other, dy_got, pieces[1], pieces[2], pieces[3]), mixed
    )
    mix_got = swap_core(mix_other)
    dy_got, mix_got = after((dy_got, mix_got), mix_got)

    inputs = own_in.reshape(2 * span, width)
    middle, hidden_two = by_rows(
        middle_kernel, "middle", [inputs, mix_mine, mix_got], [gain_two[None]], [F32, BF]
    )
    h2_got = swap_y(hidden_two)
    h2_sib = swap_core(hidden_two)
    dy_sib_got = swap_core(dy_got)
    units = hidden_units
    fours = bit_low + 2 * bit_high
    kinds = [fours ^ at for at in range(4)]
    places = [member * span, (member ^ 1) * span]
    places += [(member ^ (2 + kind // 2)) * span for kind in kinds]
    places += [lax.rem(kind, 2) * units for kind in kinds]

    def ffn(seq, h2):
        head = [seq, y_at * span, (1 - y_at) * span, member * units]
        return feed_forward(
            jnp.stack(head + places),
            h2,
            (out_grad, dy_got, dy_sib, dy_sib_got),
            (w_gate, w_up, unit_core, *[pieces[at] for at in range(4)]),
            w_down,
        )

    (
        act_own,
        act_sib,
        grad_own,
        grad_sib,
        back_own,
        back_sib,
        dy_own,
        dy_sib_own,
        *h2_near_t,
        act_own_t,
        act_sib_t,
    ) = ffn(y_at, (hidden_two, h2_sib))
    sib_got = swap_core(back_sib)
    h2_next = after(h2_got, sib_got)
    h2_far = (h2_next, swap_core(h2_next))
    (
        act_next,
        act_diag,
        grad_next,
        grad_diag,
        back_next,
        back_diag,
        dy_next,
        dy_diag,
        *h2_far_t,
        act_next_t,
        act_diag_t,
    ) = ffn(1 - y_at, h2_far)
    dh2_send = (back_next + swap_core(back_diag).astype(F32)).astype(BF)
    dh2_got = swap_y(dh2_send)
    grads = after((grad_own, grad_sib, grad_next, grad_diag), dh2_send)
    ffn_grad = weight_grad((*h2_near_t, *h2_far_t), grads)
    down_grad = weight_grad(
        after((act_own_t, act_sib_t, act_next_t, act_diag_t), ffn_grad),
        (dy_own, dy_sib_own, dy_next, dy_diag),
    )
    right, left = Ring(1), Ring(-1)
    rows = span // copies
    indices = jnp.stack(
        [jnp.stack([ring.chunk_at(step) for ring in (right, left)]) for step in range(copies)]
    )
    unit_sum = RingSum((right, left), indices, [ffn_grad.reshape(4, span, 2 * units)])
    dh2_got = after(dh2_got, down_grad, *unit_sum.moving)

    def chunk_pair(rows):
        parts = rows.reshape(2, span, width)
        return at_y(parts[0], parts[1])

    grad_middle, grad_branch, ffn_gain_part = by_rows(
        middle_grad_kernel,
        "middle_grad",
        [back_own, sib_got, dh2_got, middle, dy_own],
        [gain_two[None]],
        [F32, BF],
        1,
    )
    unit_sum.advance(grad_branch)
    grad_branch = after(grad_branch, *unit_sum.moving)
    grad_branch = grad_branch.reshape(2, span, width)
    branch_even, branch_odd = by_core(grad_branch, swap_core(grad_branch))
    branch_all = jnp.stack([branch_even, branch_odd], 1).reshape(4 * span, width)
    grad_mixed = contract(branch_all, w_mix, 1, 1).astype(BF)
    mix_grad = contract(mixed, branch_all, 0, 0)
    mix_here, mix_there = at_y(mix_grad[:span], mix_grad[span:])
    mix_there = mix_there.astype(BF)
    mix_grad_got = swap_y(mix_there)
    unit_sum.advance(grad_mixed, mix_there)
    grad_mixed = after(grad_mixed, mix_there, *unit_sum.moving)
    head_grads = []
    head_gain_part = 0.0
    rows_here = []
    rows_got = []
    for part in range(2):
        grad_heads, gain_part = attention_backward(
            part,
            grad_mixed,
            rot,
            key_rot,
            value_low,
            head_normed,
            head_inv,
            log_total,
            cosine,
            sine,
            seg_row,
            seg_col,
            gains,
        )
        head_gain_part = head_gain_part + gain_part
        unit_sum.advance(grad_heads)
        grad_heads = after(grad_heads, *unit_sum.moving)
        head_grads.append(grad_heads)
        attn_grad = contract(hidden_one, grad_heads, 0, 0).reshape(2, 2 * span, -1)
        here, there = at_y(attn_grad[0], attn_grad[1])
        there = there.astype(BF)
        rows_here.append(here)
        rows_got.append(swap_y(there))
        grad_mixed = after(grad_mixed, there)
    head_grads = jnp.concatenate(after(head_grads, grad_mixed), 1)
    back_one = contract(head_grads, w_attn, 1, 1)
    one_mine, one_other = own_and_other(back_one)
    grad_hidden_one = one_mine + swap_core(one_other.astype(BF)).astype(F32)
    inputs = inputs.astype(F32)
    inv_one, _ = own_and_other(inv_all)
    normed_one = inputs * inv_one
    attn_gain_part = jnp.sum(grad_hidden_one * normed_one, 0)
    grad_input = grad_middle + norm_back(grad_hidden_one * gain_one, normed_one, inv_one)
    input_here, input_there = chunk_pair(grad_input)
    input_back = swap_y(input_there.astype(BF))

    acts = after((act_own, act_sib, act_next, act_diag), back_one)
    out_own, out_sib, out_next, out_diag = [
        jnp.dot(act, w_down, preferred_element_type=F32) for act in acts
    ]
    out_own = middle + out_own + swap_core(out_sib.astype(BF)).astype(F32)
    out_next = out_next + swap_core(out_diag.astype(BF)).astype(F32)

    own_here, own_there = chunk_pair(out_own)
    next_here, next_there = chunk_pair(out_next)
    out_back = swap_y(jnp.stack([own_there, next_there]).astype(BF))
    half = width // 2
    head_sum = jnp.stack(
        [
            *jnp.concatenate(
                [here + got.astype(F32) for here, got in zip(rows_here, rows_got)], 1
            ).reshape(2, span, width),
            mix_here + mix_grad_got.astype(F32),
        ]
    )
    sums_right, sums_left = RingSum(
        (right, left), indices, [down_grad[None], head_sum]
    ).finish()
    gate_part, up_part = unit_sum.finish()
    down_rows = units // copies

    def all_heads(part):
        owners = part[down_rows : down_rows + 2 * rows].reshape(2, rows, half)
        mine, other = at_core(owners[0], owners[1])
        both = by_core(mine, swap_core(other))
        return jnp.concatenate([part[:down_rows], *both, part[down_rows + 2 * rows :]])

    def own_rows(parts):
        both = jnp.stack([part.reshape(2, 2, rows, units) for part in parts], 1)
        mine, other = at_core(both[:, :, 0], both[:, :, 1])
        both_cores = jnp.stack(by_core(mine, swap_core(other)), 2)
        here, there = at_y(both_cores[0], both_cores[1])
        all_units = by_y(here, swap_y(there))
        return [
            jnp.concatenate([block[kind, at] for block in all_units for at in range(2)], 1)
            for kind in range(2)
        ]

    units_gather = RingGather(
        (right, left),
        indices,
        own_rows([gate_part, up_part]),
        [w_gate.shape, w_up.shape],
        [(side, side, (0, rows), (0, 4 * units), 0) for side in range(2)],
    )
    sums_right, sums_left = after((sums_right, sums_left), units_gather.advance(copies // 2 - 1))
    targets = []
    for side in range(2):
        targets.append((0, side, (0, down_rows), (0, half), side * half))
        for at in range(2):
            top = down_rows + at * rows
            place_rows = (top, top + rows)
            half_at = side * span + at * span // 2
            targets += [
                (1, side, place_rows, (0, span), side * 2 * span + at * span),
                (2, side, place_rows, (span, span + span // 2), half_at),
                (3, side, place_rows, (span + span // 2, 2 * span), half_at),
            ]
        top = down_rows + 2 * rows
        targets.append((4, side, (top, top + rows), (0, half), side * half))
    heads_gather = RingGather(
        (right, left),
        indices,
        [all_heads(sums_right), all_heads(sums_left)],
        [value.shape for value in (w_down, w_query, w_key, w_value, w_out)],
        targets,
    )
    w_gate_grad, w_up_grad = units_gather.advance(copies)
    w_down_grad, w_query_grad, w_key_grad, w_value_grad, w_out_grad = heads_gather.advance(copies)

    sums = jnp.concatenate([attn_gain_part, ffn_gain_part[0], head_gain_part.T.reshape(-1)])
    sums = after(sums.reshape(-1, 128), sums_right)
    sums = sums + swap_core(sums)
    sums = sums + swap_y(sums)
    step = 1
    while step < copies:
        sums = sums + lax.ppermute(sums, "replica", [(at, at ^ step) for at in range(copies)])
        step *= 2
    sums = sums.reshape(-1)
    attn_gain_grad = lax.dynamic_slice(sums, (member * span,), (span,))
    ffn_gain_grad = lax.dynamic_slice(sums, (width + member * span,), (span,))
    query_gain_grad = sums[2 * width : 2 * width + HD]
    key_gain_grad = sums[2 * width + HD : 2 * width + 2 * HD]

    out_back, input_back = after((out_back, input_back), sums_right)
    out_back, input_back = out_back.astype(F32), input_back.astype(F32)
    input_grad = jnp.stack(by_y(input_here, input_back))
    block_out = jnp.stack(by_y(own_here + out_back[1], next_here + out_back[0])).astype(BF)

    return (
        block_out,
        input_grad,
        attn_gain_grad,
        w_query_grad,
        w_key_grad,
        w_value_grad,
        query_gain_grad,
        key_gain_grad,
        w_out_grad,
        ffn_gain_grad,
        w_gate_grad,
        w_up_grad,
        w_down_grad,
    )


def solution(mesh):
    rows = P("group", None)
    tokens = P("replica", "group", None)
    placed = (
        tokens,
        P("replica", "group"),
        P("replica", "group"),
        tokens,
        P("group"),
        rows,
        rows,
        rows,
        P(),
        P(),
        rows,
        P("group"),
        rows,
        rows,
        rows,
    )
    return jax.shard_map(
        per_device,
        mesh=mesh,
        in_specs=placed,
        out_specs=(
            tokens,
            tokens,
            P("group"),
            rows,
            rows,
            rows,
            P(),
            P(),
            rows,
            P("group"),
            rows,
            rows,
            rows,
        ),
        check_vma=False,
    )
```

```python
import functools

import jax
import jax.numpy as jnp
from jax import lax
from jax.experimental import pallas as pl
from jax.experimental.pallas import tpu as pltpu
from jax.sharding import PartitionSpec as P

HEADS = 8
PAIRS = 4
HD = 64
HALF = 32
SPAN = 256
LANES = 128

EPS = 1e-05
THETA = 1000000.0
NEG = -1e30

BF = jnp.bfloat16
F32 = jnp.float32
NO_COST = pl.CostEstimate(flops=0, bytes_accessed=0, transcendentals=0)

Y_SWAP = [(0, 2), (2, 0), (1, 3), (3, 1)]
CORE_SWAP = [(0, 1), (1, 0), (2, 3), (3, 2)]
CROSS_SWAP = [(0, 3), (3, 0), (1, 2), (2, 1)]


def contract(left, right, left_dim, right_dim):
    return lax.dot_general(
        left, right, (((left_dim,), (right_dim,)), ((), ())), preferred_element_type=F32
    )


def visible_block(seg_col, seg_row, block):
    end = (block + 1) * SPAN
    key_at = lax.broadcasted_iota(jnp.int32, (end, SPAN), 0)
    query_at = lax.broadcasted_iota(jnp.int32, (end, SPAN), 1) + block * SPAN
    return (seg_col[0:end, :] == seg_row[:, block * SPAN : end]) & (key_at <= query_at)


def project_kernel(
    hidden_ref,
    weight_ref,
    cos_ref,
    sin_ref,
    gain_ref,
    rot_ref,
    key_ref,
    value_ref,
    value_t_ref,
    normed_ref,
    inv_ref,
):
    raw = jnp.dot(hidden_ref[...], weight_ref[...], preferred_element_type=F32)
    raw_t = raw.T
    for half in range(2):
        cols = slice(half * 2 * SPAN + 3 * LANES, (half + 1) * 2 * SPAN)
        place = slice(half * LANES, (half + 1) * LANES)
        value_ref[:, place] = raw[:, cols].astype(BF)
        value_t_ref[place, :] = raw_t[cols, :].astype(BF)
    cosine = cos_ref[...]
    sine = sin_ref[...]
    for head in range(HEADS + PAIRS):
        rows = slice(head * HD, (head + 1) * HD)
        if head < HEADS:
            at = head // 4 * 2 * SPAN + head % 4 * HD
        else:
            at = (head - HEADS) // 2 * 2 * SPAN + SPAN + head % 2 * HD
        part = raw_t[at : at + HD, :]
        inv = lax.rsqrt(jnp.mean(part * part, 0, keepdims=True) + EPS)
        normed = part * inv
        normed_ref[rows, :] = normed
        inv_ref[head : head + 1, :] = inv
        kind = 0 if head < HEADS else 1
        scaled = normed * gain_ref[:, kind : kind + 1]
        first = scaled[:HALF, :]
        second = scaled[HALF:, :]
        turned = jnp.concatenate(
            [first * cosine - second * sine, second * cosine + first * sine], 0
        ).astype(BF)
        if head < HEADS:
            rot_ref[rows, :] = turned * BF(HD**-0.5)
        else:
            rot_ref[rows, :] = turned
            key_ref[head - HEADS] = turned.astype(F32).T.astype(BF)


def forward_kernel(
    rot_ref,
    key_ref,
    value_t_ref,
    seg_row_ref,
    seg_col_ref,
    at_ref,
    w_own_ref,
    w_got_ref,
    mixed_ref,
    log_ref,
    w_mix_ref,
    mine_ref,
    other_ref,
    mixed_t,
):
    w_mix_ref[pl.ds(pl.multiple_of(at_ref[0] * SPAN, SPAN), SPAN), :] = w_own_ref[...]
    w_mix_ref[pl.ds(pl.multiple_of((1 - at_ref[0]) * SPAN, SPAN), SPAN), :] = w_got_ref[...]
    for block in range(mixed_ref.shape[0] // SPAN):
        end = (block + 1) * SPAN
        span = slice(block * SPAN, end)
        visible = visible_block(seg_col_ref[...], seg_row_ref[...], block)

        def one_head(head, carry, end=end, span=span, visible=visible):
            pair = head // 2
            rows = pl.ds(pl.multiple_of(head * HD, HD), HD)
            score = jnp.dot(
                key_ref[pair, 0:end, :], rot_ref[rows, span], preferred_element_type=F32
            )
            score = jnp.where(visible, score, NEG)
            top = jnp.max(score, 0, keepdims=True)
            weight = jnp.exp(score - top)
            total = jnp.sum(weight, 0, keepdims=True)
            log_ref[pl.ds(head, 1), span] = top + jnp.log(total)
            values_t = value_t_ref[pl.ds(pl.multiple_of(pair * HD, HD), HD), 0:end]
            mixed_t[rows, :] = jnp.dot(
                values_t, weight.astype(BF), preferred_element_type=F32
            ) * (1.0 / total)
            return carry

        lax.fori_loop(0, HEADS, one_head, 0)
        for pair in range(PAIRS):
            cols = slice(pair * 2 * HD, (pair + 1) * 2 * HD)
            mixed_ref[span, cols] = mixed_t[cols, :].T.astype(BF)
    core = at_ref[1]
    for part in range(2):
        span = slice(part * SPAN, (part + 1) * SPAN)
        for where, out in ((core, mine_ref), (1 - core, other_ref)):
            rows = pl.ds(pl.multiple_of((2 * part + where) * SPAN, SPAN), SPAN)
            out[span, :] = jnp.dot(
                mixed_ref[rows, :], w_mix_ref[...], preferred_element_type=F32
            ).astype(out.dtype)


def backward_kernel(
    half,
    grad_ref,
    query_ref,
    key_t_ref,
    key_ref,
    value_ref,
    query_normed_ref,
    key_normed_ref,
    inv_ref,
    log_ref,
    cos_ref,
    sin_ref,
    seg_row_ref,
    seg_col_ref,
    gain_ref,
    out_ref,
    gain_grad_ref,
    grad_t,
    head_grad,
    value_one,
    key_sum,
    value_sum,
    out_t,
):
    length = grad_ref.shape[0]
    heads = HEADS // 2
    pairs = PAIRS // 2
    for part in range(pairs):
        cols = slice(part * 2 * HD, (part + 1) * 2 * HD)
        grad_t[cols, :] = grad_ref[:, cols].astype(F32).T.astype(BF)
    values_t = value_ref[...].astype(F32).T
    for pair in range(pairs):
        value_one[pair] = values_t[pair * HD : (pair + 1) * HD, :].T.astype(BF)
    left_lane = lax.broadcasted_iota(jnp.int32, (SPAN, 2 * HD), 1) < HD
    zero = jnp.zeros((SPAN, 2 * HD), BF)

    def one_pair(pair, carry):
        key_sum[...] = jnp.zeros_like(key_sum)
        value_sum[...] = jnp.zeros_like(value_sum)
        keys_t = key_t_ref[pl.ds(pl.multiple_of(pair * HD, HD), HD), :]
        both = pl.ds(pl.multiple_of(pair * 2 * HD, 2 * HD), 2 * HD)
        for block in range(length // SPAN):
            end = (block + 1) * SPAN
            span = slice(block * SPAN, end)
            visible = visible_block(seg_col_ref[...], seg_row_ref[...], block)
            queries = query_ref[both, span].astype(F32).T.astype(BF)
            grads = grad_ref[span, both]
            values = []
            keys = []
            for side in range(2):
                head = pair * 2 + side
                rows = pl.ds(pl.multiple_of(head * HD, HD), HD)
                score = jnp.dot(
                    key_ref[pair, 0:end, :], query_ref[rows, span], preferred_element_type=F32
                )
                logs = log_ref[pl.ds(half * heads + head, 1), span]
                prob = jnp.where(visible, jnp.exp(score - logs), 0.0)
                grad_prob = jnp.dot(
                    value_one[pair, 0:end, :], grad_t[rows, span], preferred_element_type=F32
                )
                inner = jnp.sum(prob * grad_prob, 0, keepdims=True)
                grad_score = (prob * (grad_prob - inner)).astype(BF)
                mine = left_lane if side == 0 else jnp.logical_not(left_lane)
                values.append(
                    jnp.dot(
                        prob.astype(BF), jnp.where(mine, grads, zero), preferred_element_type=F32
                    )
                )
                keys.append(
                    jnp.dot(grad_score, jnp.where(mine, queries, zero), preferred_element_type=F32)
                )
                head_grad[rows, span] = jnp.dot(
                    keys_t[:, 0:end], grad_score, preferred_element_type=F32
                ) * (HD**-0.5)
            value_sum[0:end, :] += values[0] + values[1]
            key_sum[0:end, :] += keys[0] + keys[1]
        key_t = key_sum[...].T
        value_t = value_sum[...].T
        key_rows = pl.ds(pl.multiple_of((heads + pair) * HD, HD), HD)
        head_grad[key_rows, :] = key_t[:HD, :] + key_t[HD:, :]
        value_rows = pl.ds(pl.multiple_of((heads + pairs + pair) * HD, HD), HD)
        out_t[value_rows, :] = value_t[:HD, :] + value_t[HD:, :]
        return carry

    lax.fori_loop(0, pairs, one_pair, 0)

    cosine = cos_ref[...]
    sine = sin_ref[...]
    gain_sums = [jnp.zeros((HD, length), F32), jnp.zeros((HD, length), F32)]
    for head in range(heads + pairs):
        rows = slice(head * HD, (head + 1) * HD)
        kind = 0 if head < heads else 1
        part = head_grad[rows, :]
        first = part[:HALF, :]
        second = part[HALF:, :]
        turned = jnp.concatenate(
            [first * cosine + second * sine, second * cosine - first * sine], 0
        )
        if kind == 0:
            normed = query_normed_ref[rows, :]
            line = half * heads + head
        else:
            normed = key_normed_ref[(head - heads) * HD : (head - heads + 1) * HD, :]
            line = HEADS + half * pairs + head - heads
        gain_sums[kind] = gain_sums[kind] + turned * normed
        scaled = turned * gain_ref[:, kind : kind + 1]
        mean = jnp.mean(scaled * normed, 0, keepdims=True)
        out_t[rows, :] = inv_ref[line : line + 1, :] * (scaled - normed * mean)
    for kind in range(2):
        gain_grad_ref[:, kind : kind + 1] = jnp.sum(gain_sums[kind], 1, keepdims=True)
    for part in range(out_t.shape[0] // (2 * HD)):
        cols = slice(part * 2 * HD, (part + 1) * 2 * HD)
        out_ref[:, cols] = out_t[cols, :].T.astype(BF)


def in_hbm(shape, kind):
    return pltpu.HBM(shape, kind)


def from_hbm(*operands):
    return [
        pltpu.with_memory_space_constraint(value, pltpu.HBM) if value.size >= 2**16 else value
        for value in operands
    ]


def whole_refs(count):
    return [pl.BlockSpec(memory_space=pltpu.VMEM)] * count


def project(hidden, weight, cosine, sine, gains):
    length = hidden.shape[0]
    rows = (HEADS + PAIRS) * HD
    outs = [
        ((rows, length), BF),
        ((PAIRS, length, HD), BF),
        ((length, PAIRS * HD), BF),
        ((PAIRS * HD, length), BF),
        ((rows, length), F32),
        ((16, length), F32),
    ]
    return pl.pallas_call(
        project_kernel,
        out_shape=[in_hbm(shape, kind) for shape, kind in outs],
        grid=(length // SPAN,),
        in_specs=[
            pl.BlockSpec((SPAN, hidden.shape[1]), lambda at: (at, 0)),
            pl.BlockSpec(weight.shape, lambda at: (0, 0)),
            pl.BlockSpec((HALF, SPAN), lambda at: (0, at)),
            pl.BlockSpec((HALF, SPAN), lambda at: (0, at)),
            pl.BlockSpec(gains.shape, lambda at: (0, 0)),
        ],
        out_specs=[
            pl.BlockSpec((rows, SPAN), lambda at: (0, at)),
            pl.BlockSpec((PAIRS, SPAN, HD), lambda at: (0, at, 0)),
            pl.BlockSpec((SPAN, PAIRS * HD), lambda at: (at, 0)),
            pl.BlockSpec((PAIRS * HD, SPAN), lambda at: (0, at)),
            pl.BlockSpec((rows, SPAN), lambda at: (0, at)),
            pl.BlockSpec((16, SPAN), lambda at: (0, at)),
        ],
        compiler_params=pltpu.CompilerParams(vmem_limit_bytes=24 * 1024 * 1024),
        cost_estimate=NO_COST,
        name="project",
    )(*from_hbm(hidden, weight), cosine, sine, gains)


def attention_forward(rot, key, value_t, seg_row, seg_col, at, w_own, w_got):
    length = rot.shape[1]
    width = w_own.shape[1]
    outs = [
        ((length, HEADS * HD), BF),
        ((HEADS, length), F32),
        ((HEADS * HD, width), BF),
        ((length // 2, width), F32),
        ((length // 2, width), BF),
    ]
    return pl.pallas_call(
        forward_kernel,
        out_shape=[in_hbm(shape, kind) for shape, kind in outs],
        in_specs=whole_refs(5) + [pl.BlockSpec(memory_space=pltpu.SMEM)] + whole_refs(2),
        out_specs=whole_refs(len(outs)),
        scratch_shapes=[pltpu.VMEM((HEADS * HD, SPAN), F32)],
        compiler_params=pltpu.CompilerParams(vmem_limit_bytes=24 * 1024 * 1024),
        cost_estimate=NO_COST,
        name="attention_forward",
    )(*from_hbm(rot, key, value_t), seg_row, seg_col, at, *from_hbm(w_own, w_got))


def middle_kernel(inputs_ref, mine_ref, got_ref, gain_ref, middle_ref, hidden_ref):
    middle = inputs_ref[...].astype(F32) + mine_ref[...] + got_ref[...].astype(F32)
    middle_ref[...] = middle
    normed, _ = norm_rows(middle)
    hidden_ref[...] = (normed * gain_ref[...]).astype(BF)


def by_rows(kernel, name, rows_in, whole_in, rows_out, sums_out=0):
    rows, width = rows_in[0].shape
    tile = 2 * LANES
    block = pl.BlockSpec((tile, width), lambda at: (at, 0))
    line = pl.BlockSpec((1, width), lambda at: (0, 0))
    return pl.pallas_call(
        kernel,
        grid=(rows // tile,),
        out_shape=[in_hbm((rows, width), kind) for kind in rows_out]
        + [jax.ShapeDtypeStruct((1, width), F32)] * sums_out,
        in_specs=[block] * len(rows_in) + [line] * len(whole_in),
        out_specs=[block] * len(rows_out) + [line] * sums_out,
        compiler_params=pltpu.CompilerParams(vmem_limit_bytes=16 * 1024 * 1024),
        cost_estimate=NO_COST,
        name=name,
    )(*[from_hbm(value)[0] if value.dtype == F32 else value for value in rows_in], *whole_in)


def middle_grad_kernel(
    own_ref, sib_ref, got_ref, middle_ref, dy_ref, gain_ref, grad_ref, branch_ref, gain_grad_ref
):
    dh2 = own_ref[...] + sib_ref[...].astype(F32) + got_ref[...].astype(F32)
    normed, inv = norm_rows(middle_ref[...])

    @pl.when(pl.program_id(0) == 0)
    def _():
        gain_grad_ref[...] = jnp.zeros_like(gain_grad_ref)

    gain_grad_ref[...] += jnp.sum(dh2 * normed, 0, keepdims=True)
    grad = dy_ref[...].astype(F32) + norm_back(dh2 * gain_ref[...], normed, inv)
    grad_ref[...] = grad
    branch_ref[...] = grad.astype(BF)


def attention_backward(half, grad, rot, key, value, normed, inv, log, cosine, sine, seg_row, seg_col, gains):
    length = grad.shape[0]
    queries = HEADS * HD // 2
    keys = PAIRS * HD // 2
    width = queries + 2 * keys

    def rows_of(count, at):
        return pl.BlockSpec((count, length), lambda step: (at, 0))

    def columns_of(count):
        return pl.BlockSpec((length, count), lambda step: (0, half))

    key_at = 2 * queries // keys + half
    return pl.pallas_call(
        functools.partial(backward_kernel, half),
        grid=(1,),
        out_shape=[
            in_hbm((length, width), BF),
            jax.ShapeDtypeStruct((HD, 2), F32),
        ],
        in_specs=[
            columns_of(queries),
            rows_of(queries, half),
            rows_of(keys, key_at),
            pl.BlockSpec((PAIRS // 2, length, HD), lambda step: (half, 0, 0)),
            columns_of(keys),
            rows_of(queries, half),
            rows_of(keys, key_at),
        ]
        + whole_refs(7),
        out_specs=whole_refs(2),
        scratch_shapes=[
            pltpu.VMEM((queries, length), BF),
            pltpu.VMEM((queries + keys, length), F32),
            pltpu.VMEM((PAIRS // 2, length, HD), BF),
            pltpu.VMEM((length, 2 * HD), F32),
            pltpu.VMEM((length, 2 * HD), F32),
            pltpu.VMEM((width, length), F32),
        ],
        compiler_params=pltpu.CompilerParams(vmem_limit_bytes=28 * 1024 * 1024),
        cost_estimate=NO_COST,
        name="attention_backward",
    )(
        *from_hbm(grad, rot, rot, key, value, normed, normed),
        inv,
        log,
        cosine,
        sine,
        seg_row,
        seg_col,
        gains,
    )


def feed_forward_kernel(
    at_ref,
    h2_a,
    h2_b,
    dy_a,
    dy_a_got,
    dy_b,
    dy_b_got,
    w_gate,
    w_up,
    w_sib,
    piece_0,
    piece_1,
    piece_2,
    piece_3,
    w_down,
    act_a,
    act_b,
    grad_a,
    grad_b,
    back_a,
    back_b,
    dy_out_a,
    dy_out_b,
    h2_t_a,
    h2_t_b,
    act_t_a,
    act_t_b,
    h2_v,
    dy_v,
    in_v,
    down_v,
    act_v,
    grad_v,
    back_own,
    back_sib,
    h2_t,
    act_t,
    grad_act,
    load_sems,
    store_sems,
):
    units = down_v.shape[0]

    def rows_at(index):
        return pl.ds(pl.multiple_of(at_ref[index], SPAN), SPAN)

    def units_at(index):
        return pl.ds(pl.multiple_of(at_ref[index], LANES), units)

    loads = []

    def load(source, target):
        loads.append(pltpu.make_async_copy(source, target, load_sems.at[len(loads)]))
        loads[-1].start()

    def load_dy(part, own, got):
        load(own.at[at_ref[0]], dy_v.at[part, rows_at(1)])
        load(got.at[at_ref[0]], dy_v.at[part, rows_at(2)])

    load_dy(0, dy_a, dy_a_got)
    load(w_down, down_v)
    load(h2_a, h2_v.at[0])
    load(w_gate.at[:, units_at(3)], in_v.at[rows_at(4), 0:units])
    load(w_up.at[:, units_at(3)], in_v.at[rows_at(4), units : 2 * units])
    load(w_sib, in_v.at[rows_at(5)])
    for at, piece in enumerate((piece_0, piece_1, piece_2, piece_3)):
        load(piece, in_v.at[rows_at(6 + at), units_at(10 + at)])
    weights_end = len(loads)
    load_dy(1, dy_b, dy_b_got)
    load(h2_b, h2_v.at[1])
    stores = []
    for part in range(2):
        for at in range(3) if part == 0 else range(weights_end, weights_end + 2):
            loads[at].wait()
        for start in range(0, units, 256):
            end = min(start + 256, units)
            grad_act[:, start:end] = contract(dy_v[part], down_v[start:end, :], 1, 1)
        for at in range(3, weights_end) if part == 0 else [weights_end + 2]:
            loads[at].wait()
        for start in range(0, units, LANES):
            gate_cols = slice(start, start + LANES)
            up_cols = slice(units + start, units + start + LANES)
            weight = jnp.concatenate([in_v[:, gate_cols], in_v[:, up_cols]], 1)
            both = jnp.dot(h2_v[part], weight, preferred_element_type=F32)
            gate, up = both[:, :LANES], both[:, LANES:]
            sig = jax.nn.sigmoid(gate)
            silu = gate * sig
            grad = grad_act[:, gate_cols]
            act_v[part, :, gate_cols] = (silu * up).astype(BF)
            grad_gate = grad * up * sig * (1.0 + gate * (1.0 - sig))
            grad_v[part, :, gate_cols] = grad_gate.astype(BF)
            grad_v[part, :, up_cols] = (grad * silu).astype(BF)
        h2_t[part] = h2_v[part].T
        act_t[part] = act_v[part].T
        back = contract(grad_v[part], in_v[...], 1, 1)
        if part == 0:
            back_own[...] = back
        else:
            back_sib[...] = back.astype(BF)
        for at, (source, target) in enumerate(
            [
                (act_v.at[part], (act_a, act_b)[part]),
                (grad_v.at[part], (grad_a, grad_b)[part]),
                ((back_own, back_sib)[part], (back_a, back_b)[part]),
                (dy_v.at[part], (dy_out_a, dy_out_b)[part]),
                (h2_t.at[part], (h2_t_a, h2_t_b)[part]),
                (act_t.at[part], (act_t_a, act_t_b)[part]),
            ]
        ):
            stores.append(pltpu.make_async_copy(source, target, store_sems.at[part * 6 + at]))
            stores[-1].start()
    for store in stores:
        store.wait()


def feed_forward(at, h2, dy, weights, w_down):
    rows, width = h2[0].shape
    units = w_down.shape[0]
    outs = (
        [((rows, units), BF)] * 2
        + [((rows, 2 * units), BF)] * 2
        + [((rows, width), F32), ((rows, width), BF)]
        + [((rows, width), BF)] * 2
        + [((width, rows), BF)] * 2
        + [((units, rows), BF)] * 2
    )
    operands = from_hbm(*h2, *dy, *weights, w_down)
    return pl.pallas_call(
        feed_forward_kernel,
        out_shape=[in_hbm(shape, kind) for shape, kind in outs],
        in_specs=[pl.BlockSpec(memory_space=pltpu.SMEM)]
        + [pl.BlockSpec(memory_space=pl.ANY)] * len(operands),
        out_specs=[pl.BlockSpec(memory_space=pl.ANY)] * len(outs),
        scratch_shapes=[
            pltpu.VMEM((2, rows, width), BF),
            pltpu.VMEM((2, rows, width), BF),
            pltpu.VMEM((width, 2 * units), BF),
            pltpu.VMEM(w_down.shape, BF),
            pltpu.VMEM((2, rows, units), BF),
            pltpu.VMEM((2, rows, 2 * units), BF),
            pltpu.VMEM((rows, width), F32),
            pltpu.VMEM((rows, width), BF),
            pltpu.VMEM((2, width, rows), BF),
            pltpu.VMEM((2, units, rows), BF),
            pltpu.VMEM((rows, units), F32),
            pltpu.SemaphoreType.DMA((14,)),
            pltpu.SemaphoreType.DMA((12,)),
        ],
        compiler_params=pltpu.CompilerParams(vmem_limit_bytes=44 * 1024 * 1024),
        cost_estimate=NO_COST,
        name="feed_forward",
    )(at, *operands)


def weight_grad_kernel(count, *refs):
    left, right = refs[:count], refs[count : 2 * count]
    out = refs[-1]
    total = jnp.dot(left[0][...], right[0][...], preferred_element_type=F32)
    for at in range(1, count):
        total += jnp.dot(left[at][...], right[at][...], preferred_element_type=F32)
    out[...] = total.astype(BF)


def weight_grad(left, right):
    height, rows = left[0].shape
    width = right[0].shape[1]
    count = len(left)
    step = 3 * SPAN if width % (3 * SPAN) == 0 else 2 * SPAN
    return pl.pallas_call(
        functools.partial(weight_grad_kernel, count),
        grid=(width // step,),
        out_shape=in_hbm((height, width), BF),
        in_specs=[pl.BlockSpec((height, rows), lambda at: (0, 0))] * count
        + [pl.BlockSpec((rows, step), lambda at: (0, at))] * count,
        out_specs=pl.BlockSpec((height, step), lambda at: (0, at)),
        compiler_params=pltpu.CompilerParams(vmem_limit_bytes=24 * 1024 * 1024),
        cost_estimate=NO_COST,
        name="weight_grad",
    )(*from_hbm(*left, *right))


def norm_rows(inputs):
    inv = lax.rsqrt(jnp.mean(inputs * inputs, -1, keepdims=True) + EPS)
    return (inputs * inv, inv)


def norm_back(grad, normed, inv):
    return inv * (grad - normed * jnp.mean(grad * normed, -1, keepdims=True))


def swap_y(value):
    return lax.ppermute(value, "group", Y_SWAP)


def swap_cross(value):
    return lax.ppermute(value, "group", CROSS_SWAP)


def swap_core(value):
    return lax.ppermute(value, "group", CORE_SWAP)


def after(value, *earlier):
    return lax.optimization_barrier((value, earlier))[0]


def cycle_of(count):
    return list(range(0, count, 2)) + list(range(count - 1, 0, -2))


class Ring:
    def __init__(self, way):
        count = lax.axis_size("replica")
        cycle = cycle_of(count)[::way]
        self.count = count
        self.way = way
        self.hops = [(cycle[at], cycle[(at + 1) % count]) for at in range(count)]
        mine = lax.axis_index("replica")
        self.place = jnp.where(lax.rem(mine, 2) == 0, mine // 2, count - 1 - mine // 2)

    def chunk_at(self, back):
        at = lax.rem(self.place - self.way * back + self.count, self.count)
        return jnp.where(at < self.count // 2, 2 * at, 2 * (self.count - 1 - at) + 1)

    def send(self, value):
        return lax.ppermute(value, "replica", self.hops)


def pick_kernel(step, count, index_ref, *refs):
    sources = refs[:count]
    outs, shares, sems = refs[-count - 3 : -count - 1], refs[-count - 1 : -1], refs[-1]
    arrived = refs[count : -count - 3]
    copies = []
    for side in range(2):
        for at, (source, share) in enumerate(zip(sources, shares)):
            _, _, rows, half = share.shape
            row = pl.multiple_of(index_ref[step, side] * rows, 8)
            copies.append(
                pltpu.make_async_copy(
                    source.at[:, pl.ds(row, rows), side * half : (side + 1) * half],
                    share.at[side],
                    sems.at[side, at],
                )
            )
    for copy in copies:
        copy.start()
    for copy in copies:
        copy.wait()
    for side in range(2):
        start = 0
        for share in shares:
            _, kinds, rows, _ = share.shape
            for kind in range(kinds):
                span = slice(start, start + rows)
                part = share[side, kind].astype(F32)
                if arrived:
                    part = part + arrived[side][span, :].astype(F32)
                outs[side][span, :] = part.astype(BF)
                start += rows


def pick_chunks(step, indices, sources, arrived):
    copies = indices.shape[0]
    rows = [source.shape[1] // copies for source in sources]
    half = sources[0].shape[2] // 2
    if any(count % 16 for count in rows):
        moving = []
        for side in range(2):
            parts = [
                lax.dynamic_slice(
                    source,
                    (0, indices[step, side] * count, side * half),
                    (source.shape[0], count, half),
                ).reshape(-1, half)
                for source, count in zip(sources, rows)
            ]
            part = jnp.concatenate([part.astype(F32) for part in parts])
            if arrived:
                part = part + arrived[side].astype(F32)
            moving.append(part.astype(BF))
        return moving
    total = sum(source.shape[0] * count for source, count in zip(sources, rows))
    return pl.pallas_call(
        functools.partial(pick_kernel, step, len(sources)),
        out_shape=[jax.ShapeDtypeStruct((total, half), BF)] * 2,
        in_specs=[pl.BlockSpec(memory_space=pltpu.SMEM)]
        + [pl.BlockSpec(memory_space=pl.ANY)] * len(sources)
        + whole_refs(len(arrived)),
        out_specs=whole_refs(2),
        scratch_shapes=[
            pltpu.VMEM((2, source.shape[0], count, half), source.dtype)
            for source, count in zip(sources, rows)
        ]
        + [pltpu.SemaphoreType.DMA((2, len(sources)))],
        compiler_params=pltpu.CompilerParams(vmem_limit_bytes=8 * 1024 * 1024),
        cost_estimate=NO_COST,
        name="pick_chunks",
    )(indices, *from_hbm(*sources), *arrived)


class RingSum:
    def __init__(self, rings, indices, sources):
        self.rings, self.indices, self.sources = rings, indices, sources
        self.moving = pick_chunks(1, indices, sources, [])
        self.step = 1

    def advance(self, *earlier):
        count = self.rings[0].count
        if self.step == count:
            return
        self.step += 1
        arrived = [ring.send(chunk) for ring, chunk in zip(self.rings, self.moving)]
        arrived = after(arrived, *earlier)
        self.moving = pick_chunks(self.step % count, self.indices, self.sources, arrived)

    def finish(self):
        while self.step < self.rings[0].count:
            self.advance()
        return self.moving


def place_kernel(steps, targets, stores, index_ref, *refs):
    count = 2 * len(steps)
    chunks = refs[:count]
    outs = refs[-1 - count - stores : -1 - count]
    wide = refs[-1 - count : -1]
    sems = refs[-1]
    copies = []
    for turn, step in enumerate(steps):
        for side in range(2):
            wide[2 * turn + side][...] = chunks[2 * turn + side][...].astype(F32)
        for at, (store, side, (top, bottom), (start, end), column) in enumerate(targets):
            rows = bottom - top
            row = pl.multiple_of(index_ref[step, side] * rows, 8)
            copies.append(
                pltpu.make_async_copy(
                    wide[2 * turn + side].at[top:bottom, start:end],
                    outs[store].at[pl.ds(row, rows), column : column + end - start],
                    sems.at[turn, at],
                )
            )
            copies[-1].start()
    for copy in copies:
        copy.wait()


def place_chunks(steps, indices, chunks, stores, shapes, targets):
    if any((bottom - top) % 8 for _, _, (top, bottom), _, _ in targets):
        stores = stores or [jnp.zeros(shape, F32) for shape in shapes]
        for turn, step in enumerate(steps):
            for store, side, (top, bottom), (start, end), column in targets:
                stores[store] = lax.dynamic_update_slice(
                    stores[store],
                    chunks[2 * turn + side][top:bottom, start:end].astype(F32),
                    (indices[step, side] * (bottom - top), column),
                )
        return stores
    given = stores or []
    return list(
        pl.pallas_call(
            functools.partial(place_kernel, steps, targets, len(shapes)),
            out_shape=[in_hbm(shape, F32) for shape in shapes],
            in_specs=[pl.BlockSpec(memory_space=pltpu.SMEM)]
            + whole_refs(len(chunks))
            + [pl.BlockSpec(memory_space=pl.ANY)] * len(given),
            out_specs=[pl.BlockSpec(memory_space=pl.ANY)] * len(shapes),
            scratch_shapes=[pltpu.VMEM(chunk.shape, F32) for chunk in chunks]
            + [pltpu.SemaphoreType.DMA((len(steps), len(targets)))],
            input_output_aliases={1 + len(chunks) + at: at for at in range(len(given))},
            compiler_params=pltpu.CompilerParams(vmem_limit_bytes=12 * 1024 * 1024),
            cost_estimate=NO_COST,
            name="place_chunks",
        )(indices, *chunks, *from_hbm(*given))
    )


class RingGather:
    def __init__(self, rings, indices, chunks, shapes, targets):
        self.rings, self.indices, self.chunks = rings, indices, chunks
        self.shapes, self.targets = shapes, targets
        self.stores = []
        self.waiting = [(0, chunks)]
        self.placed = [[], []]
        self.step = 0

    def advance(self, steps):
        count = self.rings[0].count
        while steps and self.step + 1 < count:
            steps -= 1
            self.step += 1
            held = after(self.chunks, *self.placed.pop(0))
            self.chunks = [ring.send(chunk) for ring, chunk in zip(self.rings, held)]
            self.waiting.append((self.step, self.chunks))
            if len(self.waiting) == 2 or self.step + 1 == count:
                self.stores = place_chunks(
                    [step for step, _ in self.waiting],
                    self.indices,
                    [chunk for _, pair in self.waiting for chunk in pair],
                    self.stores,
                    self.shapes,
                    self.targets,
                )
                self.waiting = []
            self.placed.append(self.stores)
        return self.stores


def per_device(
    hidden_in,
    segments,
    positions,
    out_grad,
    attn_gain,
    w_query,
    w_key,
    w_value,
    query_gain,
    key_gain,
    w_out,
    ffn_gain,
    w_gate,
    w_up,
    w_down,
):
    copies = lax.axis_size("replica")
    member = lax.axis_index("group")
    y_at = member // 2
    core = lax.rem(member, 2)
    on_low_y = y_at == 0
    on_low_core = core == 0
    span, width = hidden_in.shape[1:]
    hidden_units = w_down.shape[0]

    def by_y(mine, other):
        return jnp.where(on_low_y, mine, other), jnp.where(on_low_y, other, mine)

    def by_core(mine, other):
        return jnp.where(on_low_core, mine, other), jnp.where(on_low_core, other, mine)

    def at_y(pair_low, pair_high):
        return jnp.where(on_low_y, pair_low, pair_high), jnp.where(on_low_y, pair_high, pair_low)

    def at_core(low, high):
        return jnp.where(on_low_core, low, high), jnp.where(on_low_core, high, low)

    def quarters(weight):
        size = weight.shape[1] // 4
        return [weight[:, at * size : (at + 1) * size] for at in range(4)]

    def core_columns(*weights):
        parts = [quarters(weight) for weight in weights]
        low = [part[0] for part in parts] + [part[2] for part in parts]
        high = [part[1] for part in parts] + [part[3] for part in parts]
        return at_core(jnp.concatenate(low, 1), jnp.concatenate(high, 1))

    def own_and_other(rows):
        parts = rows.reshape(2, 2, span, rows.shape[-1])
        mine, other = at_core(parts[:, 0], parts[:, 1])
        return mine.reshape(2 * span, -1), other.reshape(2 * span, -1)

    def in_order(mine, at_y, sibling, across):
        here = jnp.concatenate(by_core(mine, sibling), 0)
        there = jnp.concatenate(by_core(at_y, across), 0)
        return jnp.concatenate(by_y(here, there), 0)

    replica = lax.axis_index("replica")
    bit_low = lax.rem(replica, 2)
    bit_high = lax.rem(replica // 2, 2)

    def swap_replica(value, bit):
        return lax.ppermute(value, "replica", [(at, at ^ bit) for at in range(copies)])

    kv_rows = jnp.concatenate([w_key, w_value], 1)
    half_send = jnp.where(bit_low == 0, w_query, kv_rows)
    half_got = swap_y(half_send)
    small = after((attn_gain, ffn_gain, segments, positions), half_send)
    small = jnp.concatenate(
        [value.astype(F32)[None] for value in small[:2]]
        + [value.astype(F32) for value in small[2:]],
        0,
    )
    small_got = swap_y(small)

    hidden_first = after(hidden_in, half_send, small)
    seq_mine, seq_other = at_y(hidden_first[0], hidden_first[1])
    seq_got = swap_y(seq_other)
    w_query, w_key, w_value, w_gate, w_up = after(
        (w_query, w_key, w_value, w_gate, w_up), seq_other
    )
    mine_cols, other_cols = core_columns(w_query, w_key, w_value)
    rows_core = swap_core(other_cols)

    def unit_columns(weight, owner):
        return lax.dynamic_slice(weight, (0, owner * hidden_units), (span, hidden_units))

    target = member ^ (2 + bit_high)
    piece_send = jnp.where(bit_low == 0, unit_columns(w_gate, target), unit_columns(w_up, target))
    pieces = {
        0: lax.ppermute(
            piece_send,
            ("replica", "group"),
            [
                (4 * at + of, 4 * at + (of ^ (2 + (at // 2) % 2)))
                for at in range(copies)
                for of in range(4)
            ],
        )
    }

    small_low, small_high = by_y(small, small_got)
    small_two = jnp.stack([small_low, small_high])
    small_even, small_odd = by_core(small_two, swap_core(small_two))
    small_all = jnp.stack([small_even, small_odd], 1).reshape(4, 6, span)
    small_rows = small_all.transpose(1, 0, 2).reshape(6, 4 * span)
    gain_one = small_rows[0]
    gain_two = small_rows[1]
    seg = jnp.where(on_low_y, small_rows[2], small_rows[3])
    place = jnp.where(on_low_y, small_rows[4], small_rows[5])

    own_low, own_high = by_y(seq_mine, seq_got)
    own_in = jnp.stack([own_low, own_high])
    all_even, all_odd = by_core(own_in, swap_core(own_in))
    all_in = jnp.stack([all_even, all_odd], 1).reshape(4 * span, width)
    normed_all, inv_all = norm_rows(all_in.astype(F32))
    hidden_one = (normed_all * gain_one).astype(BF)
    freq = THETA ** (-(jnp.arange(HALF, dtype=F32) * 2.0 / HD))
    angle = freq[:, None] * place[None, :]
    cosine, sine = jnp.cos(angle), jnp.sin(angle)
    gains = jnp.stack([query_gain, key_gain], 1).astype(F32)
    seg_row = seg[None, :]
    seg_col = seg[:, None]
    unit_core = swap_core(
        jnp.concatenate([unit_columns(w_gate, member ^ 1), unit_columns(w_up, member ^ 1)], 1)
    )

    half_swapped = swap_replica(half_got, 1)
    query_y = jnp.where(bit_low == 0, half_got, half_swapped)
    rest_y = jnp.where(bit_low == 0, half_swapped, half_got)
    mine_y, other_y = core_columns(query_y, rest_y[:, : width // 2], rest_y[:, width // 2 :])
    rows_cross = swap_core(other_y)
    w_attn = in_order(mine_cols, mine_y, rows_core, rows_cross)
    w_out_send, dy_first = after((w_out, out_grad), other_y)
    out_got = swap_y(w_out_send)
    dy_sib = swap_core(dy_first)

    rot, key_rot, value_low, value_t, head_normed, head_inv = project(
        hidden_one, w_attn, cosine, sine, gains
    )
    pieces[0], rot, dy_send = after((pieces[0], rot, out_grad), rot, pieces[0])
    for bits in range(1, 4):
        pieces[bits] = swap_replica(pieces[0], bits)
    dy_got = swap_y(dy_send)
    rot, out_got, unit_core, dy_sib = after((rot, out_got, unit_core, dy_sib), pieces[0])
    mixed, log_total, w_mix, mix_mine, mix_other = attention_forward(
        rot, key_rot, value_t, seg_row, seg_col, jnp.stack([y_at, core]), w_out, out_got
    )
    mix_other, dy_got, pieces[1], pieces[2], pieces[3] = after(
        (mix_other, dy_got, pieces[1], pieces[2], pieces[3]), mixed
    )
    mix_got = swap_core(mix_other)
    dy_got, mix_got = after((dy_got, mix_got), mix_got)

    inputs = own_in.reshape(2 * span, width)
    middle, hidden_two = by_rows(
        middle_kernel, "middle", [inputs, mix_mine, mix_got], [gain_two[None]], [F32, BF]
    )
    h2_got = swap_y(hidden_two)
    h2_sib = swap_core(hidden_two)
    dy_sib_got = swap_core(dy_got)
    units = hidden_units
    fours = bit_low + 2 * bit_high
    kinds = [fours ^ at for at in range(4)]
    places = [member * span, (member ^ 1) * span]
    places += [(member ^ (2 + kind // 2)) * span for kind in kinds]
    places += [lax.rem(kind, 2) * units for kind in kinds]

    def ffn(seq, h2):
        head = [seq, y_at * span, (1 - y_at) * span, member * units]
        return feed_forward(
            jnp.stack(head + places),
            h2,
            (out_grad, dy_got, dy_sib, dy_sib_got),
            (w_gate, w_up, unit_core, *[pieces[at] for at in range(4)]),
            w_down,
        )

    (
        act_own,
        act_sib,
        grad_own,
        grad_sib,
        back_own,
        back_sib,
        dy_own,
        dy_sib_own,
        *h2_near_t,
        act_own_t,
        act_sib_t,
    ) = ffn(y_at, (hidden_two, h2_sib))
    sib_got = swap_core(back_sib)
    h2_next = after(h2_got, sib_got)
    h2_far = (h2_next, swap_core(h2_next))
    (
        act_next,
        act_diag,
        grad_next,
        grad_diag,
        back_next,
        back_diag,
        dy_next,
        dy_diag,
        *h2_far_t,
        act_next_t,
        act_diag_t,
    ) = ffn(1 - y_at, h2_far)
    dh2_send = (back_next + swap_core(back_diag).astype(F32)).astype(BF)
    dh2_got = swap_y(dh2_send)
    grads = after((grad_own, grad_sib, grad_next, grad_diag), dh2_send)
    ffn_grad = weight_grad((*h2_near_t, *h2_far_t), grads)
    down_grad = weight_grad(
        after((act_own_t, act_sib_t, act_next_t, act_diag_t), ffn_grad),
        (dy_own, dy_sib_own, dy_next, dy_diag),
    )
    right, left = Ring(1), Ring(-1)
    rows = span // copies
    indices = jnp.stack(
        [jnp.stack([ring.chunk_at(step) for ring in (right, left)]) for step in range(copies)]
    )
    unit_sum = RingSum((right, left), indices, [ffn_grad.reshape(4, span, 2 * units)])
    dh2_got = after(dh2_got, down_grad, *unit_sum.moving)

    def chunk_pair(rows):
        parts = rows.reshape(2, span, width)
        return at_y(parts[0], parts[1])

    grad_middle, grad_branch, ffn_gain_part = by_rows(
        middle_grad_kernel,
        "middle_grad",
        [back_own, sib_got, dh2_got, middle, dy_own],
        [gain_two[None]],
        [F32, BF],
        1,
    )
    unit_sum.advance(grad_branch)
    grad_branch = after(grad_branch, *unit_sum.moving)
    grad_branch = grad_branch.reshape(2, span, width)
    branch_even, branch_odd = by_core(grad_branch, swap_core(grad_branch))
    branch_all = jnp.stack([branch_even, branch_odd], 1).reshape(4 * span, width)
    grad_mixed = contract(branch_all, w_mix, 1, 1).astype(BF)
    mix_grad = contract(mixed, branch_all, 0, 0)
    mix_here, mix_there = at_y(mix_grad[:span], mix_grad[span:])
    mix_there = mix_there.astype(BF)
    mix_grad_got = swap_y(mix_there)
    unit_sum.advance(grad_mixed, mix_there)
    grad_mixed = after(grad_mixed, mix_there, *unit_sum.moving)
    head_grads = []
    head_gain_part = 0.0
    rows_here = []
    rows_got = []
    for part in range(2):
        grad_heads, gain_part = attention_backward(
            part,
            grad_mixed,
            rot,
            key_rot,
            value_low,
            head_normed,
            head_inv,
            log_total,
            cosine,
            sine,
            seg_row,
            seg_col,
            gains,
        )
        head_gain_part = head_gain_part + gain_part
        unit_sum.advance(grad_heads)
        grad_heads = after(grad_heads, *unit_sum.moving)
        head_grads.append(grad_heads)
        attn_grad = contract(hidden_one, grad_heads, 0, 0).reshape(2, 2 * span, -1)
        here, there = at_y(attn_grad[0], attn_grad[1])
        there = there.astype(BF)
        rows_here.append(here)
        rows_got.append(swap_y(there))
        grad_mixed = after(grad_mixed, there)
    head_grads = jnp.concatenate(after(head_grads, grad_mixed), 1)
    back_one = contract(head_grads, w_attn, 1, 1)
    one_mine, one_other = own_and_other(back_one)
    grad_hidden_one = one_mine + swap_core(one_other.astype(BF)).astype(F32)
    inputs = inputs.astype(F32)
    inv_one, _ = own_and_other(inv_all)
    normed_one = inputs * inv_one
    attn_gain_part = jnp.sum(grad_hidden_one * normed_one, 0)
    grad_input = grad_middle + norm_back(grad_hidden_one * gain_one, normed_one, inv_one)
    input_here, input_there = chunk_pair(grad_input)
    input_back = swap_y(input_there.astype(BF))

    acts = after((act_own, act_sib, act_next, act_diag), back_one)
    out_own, out_sib, out_next, out_diag = [
        jnp.dot(act, w_down, preferred_element_type=F32) for act in acts
    ]
    out_own = middle + out_own + swap_core(out_sib.astype(BF)).astype(F32)
    out_next = out_next + swap_core(out_diag.astype(BF)).astype(F32)

    own_here, own_there = chunk_pair(out_own)
    next_here, next_there = chunk_pair(out_next)
    out_back = swap_y(jnp.stack([own_there, next_there]).astype(BF))
    half = width // 2
    head_sum = jnp.stack(
        [
            *jnp.concatenate(
                [here + got.astype(F32) for here, got in zip(rows_here, rows_got)], 1
            ).reshape(2, span, width),
            mix_here + mix_grad_got.astype(F32),
        ]
    )
    sums_right, sums_left = RingSum(
        (right, left), indices, [down_grad[None], head_sum]
    ).finish()
    gate_part, up_part = unit_sum.finish()
    down_rows = units // copies

    def all_heads(part):
        owners = part[down_rows : down_rows + 2 * rows].reshape(2, rows, half)
        mine, other = at_core(owners[0], owners[1])
        both = by_core(mine, swap_core(other))
        return jnp.concatenate([part[:down_rows], *both, part[down_rows + 2 * rows :]])

    def own_rows(parts):
        both = jnp.stack([part.reshape(2, 2, rows, units) for part in parts], 1)
        mine, other = at_core(both[:, :, 0], both[:, :, 1])
        both_cores = jnp.stack(by_core(mine, swap_core(other)), 2)
        here, there = at_y(both_cores[0], both_cores[1])
        all_units = by_y(here, swap_y(there))
        return [
            jnp.concatenate([block[kind, at] for block in all_units for at in range(2)], 1)
            for kind in range(2)
        ]

    units_gather = RingGather(
        (right, left),
        indices,
        own_rows([gate_part, up_part]),
        [w_gate.shape, w_up.shape],
        [(side, side, (0, rows), (0, 4 * units), 0) for side in range(2)],
    )
    sums_right, sums_left = after((sums_right, sums_left), units_gather.advance(copies // 2 - 1))
    targets = []
    for side in range(2):
        targets.append((0, side, (0, down_rows), (0, half), side * half))
        for at in range(2):
            top = down_rows + at * rows
            place_rows = (top, top + rows)
            half_at = side * span + at * span // 2
            targets += [
                (1, side, place_rows, (0, span), side * 2 * span + at * span),
                (2, side, place_rows, (span, span + span // 2), half_at),
                (3, side, place_rows, (span + span // 2, 2 * span), half_at),
            ]
        top = down_rows + 2 * rows
        targets.append((4, side, (top, top + rows), (0, half), side * half))
    heads_gather = RingGather(
        (right, left),
        indices,
        [all_heads(sums_right), all_heads(sums_left)],
        [value.shape for value in (w_down, w_query, w_key, w_value, w_out)],
        targets,
    )
    w_gate_grad, w_up_grad = units_gather.advance(copies)
    w_down_grad, w_query_grad, w_key_grad, w_value_grad, w_out_grad = heads_gather.advance(copies)

    sums = jnp.concatenate([attn_gain_part, ffn_gain_part[0], head_gain_part.T.reshape(-1)])
    sums = after(sums.reshape(-1, 128), sums_right)
    sums = sums + swap_core(sums)
    sums = sums + swap_y(sums)
    step = 1
    while step < copies:
        sums = sums + lax.ppermute(sums, "replica", [(at, at ^ step) for at in range(copies)])
        step *= 2
    sums = sums.reshape(-1)
    attn_gain_grad = lax.dynamic_slice(sums, (member * span,), (span,))
    ffn_gain_grad = lax.dynamic_slice(sums, (width + member * span,), (span,))
    query_gain_grad = sums[2 * width : 2 * width + HD]
    key_gain_grad = sums[2 * width + HD : 2 * width + 2 * HD]

    out_back, input_back = after((out_back, input_back), sums_right)
    out_back, input_back = out_back.astype(F32), input_back.astype(F32)
    input_grad = jnp.stack(by_y(input_here, input_back))
    block_out = jnp.stack(by_y(own_here + out_back[1], next_here + out_back[0])).astype(BF)

    return (
        block_out,
        input_grad,
        attn_gain_grad,
        w_query_grad,
        w_key_grad,
        w_value_grad,
        query_gain_grad,
        key_gain_grad,
        w_out_grad,
        ffn_gain_grad,
        w_gate_grad,
        w_up_grad,
        w_down_grad,
    )


def solution(mesh):
    rows = P("group", None)
    tokens = P("replica", "group", None)
    placed = (
        tokens,
        P("replica", "group"),
        P("replica", "group"),
        tokens,
        P("group"),
        rows,
        rows,
        rows,
        P(),
        P(),
        rows,
        P("group"),
        rows,
        rows,
        rows,
    )
    return jax.shard_map(
        per_device,
        mesh=mesh,
        in_specs=placed,
        out_specs=(
            tokens,
            tokens,
            P("group"),
            rows,
            rows,
            rows,
            P(),
            P(),
            rows,
            P("group"),
            rows,
            rows,
            rows,
        ),
        check_vma=False,
    )
```
